32 devices in a mesh: dp: 8 (over y, x, core), swap: 4 (over z).
Axes of the slice: x: 2, y: 2, z: 4, core: 2. Of those that a mesh axis runs over, the one named last changes fastest.
Arguments:
- source_tiles_smallest: bfloat16 [100, 192, 384], P(None, 'dp', 'swap'), may hold values from -6 to 6
- source_tiles_moderate: bfloat16 [196, 192, 384], P(None, 'dp', 'swap'), may hold values from -6 to 6
- source_tiles_largest: bfloat16 [324, 64, 384], P(None, 'dp', 'swap'), may hold values from -6 to 6
- target_cotangent_smallest: bfloat16 [100, 192, 384], P(None, 'dp', 'swap'), may hold values from -6 to 6
- target_cotangent_moderate: bfloat16 [196, 192, 384], P(None, 'dp', 'swap'), may hold values from -6 to 6
- target_cotangent_largest: bfloat16 [324, 64, 384], P(None, 'dp', 'swap'), may hold values from -6 to 6
- surviving_tallies: int32 [8, 3], P('dp'), may hold values from 4 to 24, as said below
- token_affine_factor: float32 [2, 384], replicated, may hold values from 0.1 to 1.9
- token_affine_addend: float32 [2, 384], replicated, may hold values from -1.75 to 1.75
- crosstile_matrix_smallest: bfloat16 [2, 100, 100], replicated, may hold values from -0.625 to 0.625
- crosstile_matrix_moderate: bfloat16 [2, 196, 196], replicated, may hold values from -0.4375 to 0.4375
- crosstile_matrix_largest: bfloat16 [2, 324, 324], replicated, may hold values from -0.3125 to 0.3125
- crosstile_addend_smallest: float32 [2, 100], replicated, may hold values from -1.75 to 1.75
- crosstile_addend_moderate: float32 [2, 196], replicated, may hold values from -1.75 to 1.75
- crosstile_addend_largest: float32 [2, 324], replicated, may hold values from -1.75 to 1.75
- token_blend_factor: float32 [2, 384], replicated, may hold values from 0.3 to 1
- feedforward_affine_factor: float32 [2, 384], replicated, may hold values from 0.1 to 1.9
- feedforward_affine_addend: float32 [2, 384], replicated, may hold values from -1.75 to 1.75
- widening_matrix: bfloat16 [2, 384, 1536], replicated, may hold values from -0.3125 to 0.3125
- widening_addend: float32 [2, 1536], replicated, may hold values from -1.75 to 1.75
- narrowing_matrix: bfloat16 [2, 1536, 384], replicated, may hold values from -0.15625 to 0.15625
- narrowing_addend: float32 [2, 384], replicated, may hold values from -1.75 to 1.75
- feedforward_factor: float32 [2, 384], replicated, may hold values from 0.3 to 1
Outputs:
- out_small: float32 [100, 192, 384], P(None, 'dp', 'swap')
- out_medium: float32 [196, 192, 384], P(None, 'dp', 'swap')
- out_large: float32 [324, 64, 384], P(None, 'dp', 'swap')
- grad_small: float32 [100, 192, 384], P(None, 'dp', 'swap')
- grad_medium: float32 [196, 192, 384], P(None, 'dp', 'swap')
- grad_large: float32 [324, 64, 384], P(None, 'dp', 'swap')
- grad_prescale: float32 [2, 384], replicated
- grad_preshift: float32 [2, 384], replicated
- grad_mix_small: float32 [2, 100, 100], replicated
- grad_mix_medium: float32 [2, 196, 196], replicated
- grad_mix_large: float32 [2, 324, 324], replicated
- grad_bias_small: float32 [2, 100], replicated
- grad_bias_medium: float32 [2, 196], replicated
- grad_bias_large: float32 [2, 324], replicated
- grad_mixgain: float32 [2, 384], replicated
- grad_mlpscale: float32 [2, 384], replicated
- grad_mlpshift: float32 [2, 384], replicated
- grad_weight_in: float32 [2, 384, 1536], replicated
- grad_bias_in: float32 [2, 1536], replicated
- grad_weight_out: float32 [2, 1536, 384], replicated
- grad_bias_out: float32 [2, 384], replicated
- grad_mlpgain: float32 [2, 384], replicated
The draws below stay inside these ranges and needn't reach their ends.
Inputs may be any that keep to these rules, and one draw needn't show every extreme that they name: surviving_tallies[i, g] is the number of live images of group g on index i of dp, which occupy that index's first slots; at least half of its 24, 24 or 8 slots are live, and in every group some index is full.
All inputs are finite; a program needn't handle non-finite values.
Results may differ from the reference program's by a relative error of at most 0.01.
Values may be sent and summed in bfloat16 or wider, within the bound.
No kernel may reach another device: no remote copies, remote signals or barrier semaphores. Data moves between devices by JAX's collectives and lax.ppermute only.
A program may use at most 192 MiB of HBM per device.

```python
import math
import jax
import jax.numpy as jnp
from jax import lax

FEATURE_BREADTH = 384
FF = 1536
PATCH_M = 196
PATCH_S = 100
PATCH_L = 324
DEPTH_TOTAL = 2
CAP_S = 24
CAP_M = 24
CAP_L = 8
IMAGES_S = 192
IMAGES_M = 192
IMAGES_L = 64
N_DP = 8


def draw_surviving_tallies(key, part):
    key = jax.random.fold_in(key, 11)
    first_key, second_key = jax.random.split(key)
    capacity = jnp.array([CAP_S, CAP_M, CAP_L], jnp.int32)
    lowest = capacity // 2
    spread = jax.random.randint(first_key, (N_DP, 3), 0, 1 << 20)
    values = lowest[None, :] + spread % (capacity - lowest + 1)[None, :]
    chosen = jax.random.randint(second_key, (3,), 0, N_DP)
    rows_index = jnp.arange(N_DP, dtype=jnp.int32)[:, None]
    return jnp.where(rows_index == chosen[None, :], capacity[None, :], values).astype(jnp.int32)


def steps_of(stream_key, dims, shards, low, largest):
    gain = 1.0
    for position, parts in shards:
        steps = jax.random.uniform(jax.random.fold_in(jax.random.fold_in(stream_key, 6), position), (parts,), jnp.float32, low / len(shards), largest / len(shards))
        gain = gain * jnp.repeat(jnp.exp(steps), dims[position] // parts).reshape((-1,) + (1,) * (len(dims) - 1 - position))
    return gain


def noise(own_key, dims, scale, limit, shards=(), kind=jnp.bfloat16):
    values = jax.random.normal(own_key, dims, jnp.float32) * scale
    if len(shards) > 0:
        values = steps_of(own_key, dims, shards, -0.22, 0.18) * values
    return jnp.clip(values, min=-limit, max=limit).astype(kind)


def setup_inputs(seed: int = 0) -> dict:
    key_list = jax.random.split(jax.random.key(seed), 24)
    source_tiles_smallest = noise(key_list[0], (PATCH_S, IMAGES_S, FEATURE_BREADTH), 1.0, 6.0, ((1, 8), (2, 4)))
    source_tiles_moderate = noise(key_list[1], (PATCH_M, IMAGES_M, FEATURE_BREADTH), 1.0, 6.0, ((1, 8), (2, 4)))
    source_tiles_largest = noise(key_list[2], (PATCH_L, IMAGES_L, FEATURE_BREADTH), 1.0, 6.0, ((1, 8), (2, 4)))
    target_cotangent_smallest = noise(key_list[3], (PATCH_S, IMAGES_S, FEATURE_BREADTH), 1.0, 6.0, ((1, 8), (2, 4)))
    target_cotangent_moderate = noise(key_list[4], (PATCH_M, IMAGES_M, FEATURE_BREADTH), 1.0, 6.0, ((1, 8), (2, 4)))
    target_cotangent_largest = noise(key_list[5], (PATCH_L, IMAGES_L, FEATURE_BREADTH), 1.0, 6.0, ((1, 8), (2, 4)))
    surviving_tallies = draw_surviving_tallies(jax.random.fold_in(key_list[23], 71), 0)
    token_affine_factor = jnp.clip(1.0 + 0.18 * jax.random.normal(key_list[7], (DEPTH_TOTAL, FEATURE_BREADTH), jnp.float32), 0.1, 1.9)
    token_affine_addend = noise(key_list[8], (DEPTH_TOTAL, FEATURE_BREADTH), 0.3, 1.75, (), jnp.float32)
    crosstile_matrix_smallest = noise(key_list[9], (DEPTH_TOTAL, PATCH_S, PATCH_S), PATCH_S ** -0.5, 0.625)
    crosstile_matrix_moderate = noise(key_list[10], (DEPTH_TOTAL, PATCH_M, PATCH_M), PATCH_M ** -0.5, 0.4375)
    crosstile_matrix_largest = noise(key_list[11], (DEPTH_TOTAL, PATCH_L, PATCH_L), PATCH_L ** -0.5, 0.3125)
    crosstile_addend_smallest = noise(key_list[12], (DEPTH_TOTAL, PATCH_S), 0.3, 1.75, (), jnp.float32)
    crosstile_addend_moderate = noise(key_list[13], (DEPTH_TOTAL, PATCH_M), 0.3, 1.75, (), jnp.float32)
    crosstile_addend_largest = noise(key_list[14], (DEPTH_TOTAL, PATCH_L), 0.3, 1.75, (), jnp.float32)
    token_blend_factor = jnp.clip(jnp.exp(jax.random.uniform(key_list[15], (DEPTH_TOTAL, FEATURE_BREADTH), jnp.float32, math.log(0.3), math.log(1.0))), 0.3, 1.0)
    feedforward_affine_factor = jnp.clip(1.0 + 0.18 * jax.random.normal(key_list[16], (DEPTH_TOTAL, FEATURE_BREADTH), jnp.float32), 0.1, 1.9)
    feedforward_affine_addend = noise(key_list[17], (DEPTH_TOTAL, FEATURE_BREADTH), 0.3, 1.75, (), jnp.float32)
    widening_matrix = noise(key_list[18], (DEPTH_TOTAL, FEATURE_BREADTH, FF), FEATURE_BREADTH ** -0.5, 0.3125)
    widening_addend = noise(key_list[19], (DEPTH_TOTAL, FF), 0.3, 1.75, (), jnp.float32)
    narrowing_matrix = noise(key_list[20], (DEPTH_TOTAL, FF, FEATURE_BREADTH), FF ** -0.5, 0.15625)
    narrowing_addend = noise(key_list[21], (DEPTH_TOTAL, FEATURE_BREADTH), 0.3, 1.75, (), jnp.float32)
    feedforward_factor = jnp.clip(jnp.exp(jax.random.uniform(key_list[22], (DEPTH_TOTAL, FEATURE_BREADTH), jnp.float32, math.log(0.3), math.log(1.0))), 0.3, 1.0)
    return dict(source_tiles_smallest=source_tiles_smallest, source_tiles_moderate=source_tiles_moderate, source_tiles_largest=source_tiles_largest, target_cotangent_smallest=target_cotangent_smallest, target_cotangent_moderate=target_cotangent_moderate, target_cotangent_largest=target_cotangent_largest, surviving_tallies=surviving_tallies, token_affine_factor=token_affine_factor, token_affine_addend=token_affine_addend, crosstile_matrix_smallest=crosstile_matrix_smallest, crosstile_matrix_moderate=crosstile_matrix_moderate, crosstile_matrix_largest=crosstile_matrix_largest, crosstile_addend_smallest=crosstile_addend_smallest, crosstile_addend_moderate=crosstile_addend_moderate, crosstile_addend_largest=crosstile_addend_largest, token_blend_factor=token_blend_factor, feedforward_affine_factor=feedforward_affine_factor, feedforward_affine_addend=feedforward_affine_addend, widening_matrix=widening_matrix, widening_addend=widening_addend, narrowing_matrix=narrowing_matrix, narrowing_addend=narrowing_addend, feedforward_factor=feedforward_factor)


@jax.custom_vjp
def low(v):
    return lax.optimization_barrier(v.astype(jnp.bfloat16)).astype(jnp.float32)

@jax.custom_vjp
def low_back(v):
    return v

def low_keep(v):
    return (low(v), None)

def low_pass(kept, grad):
    return (grad,)

def back_keep(v):
    return (v, None)

def back_low(kept, grad):
    return (low(grad),)
low.defvjp(low_keep, low_pass)
low_back.defvjp(back_keep, back_low)

def one_layer(weights, depth_index, group_id, tensor):
    highest = lax.Precision.HIGHEST
    mixing = weights[2 + group_id][depth_index]
    patch_bias = weights[5 + group_id][depth_index]
    normed = low(tensor * weights[0][depth_index] + weights[1][depth_index])
    mixture = low_back(jnp.einsum('pq,qnd->pnd', mixing, normed, precision=highest) + patch_bias[:, None, None])
    middle = tensor + weights[8][depth_index] * mixture
    scaled = low(low_back(middle * weights[9][depth_index] + weights[10][depth_index]))
    hidden = low_back(jnp.einsum('pnd,de->pne', scaled, weights[11][depth_index], precision=highest) + weights[12][depth_index])
    activ = low(jax.nn.gelu(hidden))
    branch = low(low_back(jnp.einsum('pne,ed->pnd', activ, weights[13][depth_index], precision=highest) + weights[14][depth_index]))
    return middle + weights[15][depth_index] * branch

def reference(source_tiles_smallest, source_tiles_moderate, source_tiles_largest, target_cotangent_smallest, target_cotangent_moderate, target_cotangent_largest, surviving_tallies, token_affine_factor, token_affine_addend, crosstile_matrix_smallest, crosstile_matrix_moderate, crosstile_matrix_largest, crosstile_addend_smallest, crosstile_addend_moderate, crosstile_addend_largest, token_blend_factor, feedforward_affine_factor, feedforward_affine_addend, widening_matrix, widening_addend, narrowing_matrix, narrowing_addend, feedforward_factor):
    learned_registry = tuple((scalar_item.astype(jnp.float32) for scalar_item in (token_affine_factor, token_affine_addend, crosstile_matrix_smallest, crosstile_matrix_moderate, crosstile_matrix_largest, crosstile_addend_smallest, crosstile_addend_moderate, crosstile_addend_largest, token_blend_factor, feedforward_affine_factor, feedforward_affine_addend, widening_matrix, widening_addend, narrowing_matrix, narrowing_addend, feedforward_factor)))
    fields = tuple((scalar_item.astype(jnp.float32) for scalar_item in (source_tiles_smallest, source_tiles_moderate, source_tiles_largest)))
    cotans = tuple((scalar_item.astype(jnp.float32) for scalar_item in (target_cotangent_smallest, target_cotangent_moderate, target_cotangent_largest)))
    capacity = (CAP_S, CAP_M, CAP_L)
    masking = []
    for group_id in range(3):
        slot_index = jnp.arange(N_DP * capacity[group_id], dtype=jnp.int32)
        alive_slot = slot_index % capacity[group_id] < surviving_tallies[slot_index // capacity[group_id], group_id]
        masking.append(alive_slot.astype(jnp.float32))

    def network(weights, inputs):
        outputs = []
        for group_id in range(3):
            tensor = inputs[group_id]
            patches = tensor.shape[0]
            blocks = tensor.reshape(patches, N_DP, capacity[group_id], FEATURE_BREADTH).transpose(1, 0, 2, 3)

            def run_block(images_block, group_id=group_id):
                for depth_index in range(DEPTH_TOTAL):
                    images_block = one_layer(weights, depth_index, group_id, images_block)
                return images_block
            mapped = lax.map(jax.checkpoint(run_block), blocks)
            joined = mapped.transpose(1, 0, 2, 3).reshape(patches, N_DP * capacity[group_id], FEATURE_BREADTH)
            outputs.append(joined * masking[group_id][None, :, None])
        return tuple(outputs)
    results, pullback = jax.vjp(network, learned_registry, fields)
    grad_params, grad_fields = pullback(cotans)
    return (results[0], results[1], results[2], grad_fields[0], grad_fields[1], grad_fields[2], grad_params[0], grad_params[1], grad_params[2], grad_params[3], grad_params[4], grad_params[5], grad_params[6], grad_params[7], grad_params[8], grad_params[9], grad_params[10], grad_params[11], grad_params[12], grad_params[13], grad_params[14], grad_params[15])
```

```python
import functools

import jax
import jax.numpy as jnp
from jax import lax
from jax.experimental import pallas as pl
from jax.experimental.pallas import tpu as pltpu
from jax.sharding import PartitionSpec as P

BF = jnp.bfloat16
F32 = jnp.float32
CHUNK = 256
FFC = 512
ROWS = 64
VMEM_LIMIT = 62 << 20


def round_up(value, unit):
    return -(-value // unit) * unit


def nt(a, b):
    return lax.dot_general(a, b, (((1,), (1,)), ((), ())), preferred_element_type=F32)


def tn(a, b):
    return lax.dot_general(a, b, (((0,), (0,)), ((), ())), preferred_element_type=F32)


def nn(a, b):
    return jnp.dot(a, b, preferred_element_type=F32)


class Piece:
    def __init__(self, members, patches):
        self.members = []
        offset = 0
        for group, index in members:
            self.members.append((group, index, offset))
            offset += patches[group]
        self.total = offset
        self.width = round_up(offset, 128)
        self.work = round_up(offset, CHUNK)
        self.groups = sorted({group for group, _ in members})


def pack_kernel(piece, k, patches, me_ref, live_ref, *refs):
    ng = len(piece.groups)
    xs = dict(zip(piece.groups, refs[:ng]))
    cs = dict(zip(piece.groups, refs[ng : 2 * ng]))
    outs = refs[2 * ng :]
    me = me_ref[0]
    for s in range(k):
        owner = lax.rem(me + s, k)
        out = outs[s]
        for group, index, offset in piece.members:
            p = patches[group]
            image = owner + k * index
            alive = (image < live_ref[group]).astype(F32)
            out[0, :, offset : offset + p] = xs[group][image]
            out[1, :, offset : offset + p] = (cs[group][image].astype(F32) * alive).astype(BF)
        if piece.width > piece.total:
            c = out.shape[1]
            out[:, :, piece.total :] = jnp.zeros((2, c, piece.width - piece.total), BF)


def pack(piece, k, patches, me, live, tensors, cotans):
    c = tensors[0].shape[1]
    vmem = pl.BlockSpec(memory_space=pltpu.VMEM)
    smem = pl.BlockSpec(memory_space=pltpu.SMEM)
    return pl.pallas_call(
        functools.partial(pack_kernel, piece, k, patches),
        out_shape=[jax.ShapeDtypeStruct((2, c, piece.width), BF)] * k,
        in_specs=[smem, smem] + [vmem] * (2 * len(piece.groups)),
        out_specs=[vmem] * k,
        compiler_params=pltpu.CompilerParams(vmem_limit_bytes=48 << 20),
        name="pack",
    )(me, live, *[tensors[g] for g in piece.groups], *[cotans[g] for g in piece.groups])


def unpack_kernel(pieces, groups, k, patches, me_ref, live_ref, *refs):
    buffers = [refs[i * k : (i + 1) * k] for i in range(len(pieces))]
    outs = refs[len(pieces) * k :]
    me = me_ref[0]
    for piece, bufs in zip(pieces, buffers):
        for s in range(k):
            owner = lax.rem(me - s + k, k)
            for group, index, offset in piece.members:
                if group not in groups:
                    continue
                at = 2 * groups.index(group)
                p = patches[group]
                image = owner + k * index
                alive = (image < live_ref[group]).astype(F32)
                outs[at][image] = bufs[s][0, :, offset : offset + p].astype(F32) * alive
                outs[at + 1][image] = bufs[s][1, :, offset : offset + p].astype(F32)


def unpack(pieces, groups, k, patches, images, me, live, buffers):
    c = buffers[0][0].shape[1]
    vmem = pl.BlockSpec(memory_space=pltpu.VMEM)
    smem = pl.BlockSpec(memory_space=pltpu.SMEM)
    shapes = []
    for g in groups:
        shapes += [jax.ShapeDtypeStruct((images[g], c, patches[g]), F32)] * 2
    return pl.pallas_call(
        functools.partial(unpack_kernel, pieces, groups, k, patches),
        out_shape=shapes,
        in_specs=[smem, smem] + [vmem] * (k * len(pieces)),
        out_specs=[vmem] * len(shapes),
        compiler_params=pltpu.CompilerParams(vmem_limit_bytes=48 << 20),
        name="unpack",
    )(me, live, *[b for bufs in buffers for b in bufs])


class Rows:
    def __init__(self, ff, width, patches, unit):
        self.mix = [
            (ff + round_up(patches[2], 8), round_up(patches[1], 128)),
            (ff + round_up(patches[2], 8), 0),
            (ff, 0),
        ]
        base = ff + round_up(patches[2], 8) + round_up(patches[1], 8)
        self.bias_in = base
        self.patch = [base + ff // width + g for g in range(3)]
        self.vec = round_up(base + ff // width + 3, 8)
        self.total = round_up(self.vec + 8, unit)


def layers_kernel(piece, k, patches, rows, first, layers, *refs):
    refs = list(refs)

    def take(n):
        out, refs[:] = refs[:n], refs[n:]
        return out

    (me_ref,) = take(1)
    ins = take(k)
    w1t_h, w2t_h, w1_h, w2_h = take(4)
    mixt = dict(zip(piece.groups, take(len(piece.groups))))
    mix = dict(zip(piece.groups, take(len(piece.groups))))
    pb_ref, cols, b1c = take(3)
    if not first:
        acc1_h, acc2_h = take(2)
    outs = take(k)
    out1_h, out2_h = take(2)
    (x0, x1, gn, mixs, nrm, sc, brs, act, dact, gb, gs, dy, bufp, bufq, acc1, acc2, gb1, gcol, gpb, wsem, asem, osem) = refs

    D, W = x1.shape
    F = bufp.shape[1]
    c = D // k
    me = me_ref[0]
    loads = [
        (pltpu.make_async_copy(w1t_h.at[l], bufp.at[l], wsem.at[0, l]),
         pltpu.make_async_copy(w2t_h.at[l], bufq.at[l], wsem.at[1, l]))
        for l in range(layers)
    ]
    reloads = [
        (pltpu.make_async_copy(w2_h.at[l], bufp.at[l], wsem.at[2, l]),
         pltpu.make_async_copy(w1_h.at[l], bufq.at[l], wsem.at[3, l]))
        for l in range(layers)
    ]
    for pair in loads:
        for cp in pair:
            cp.start()
    if not first:
        accs = [pltpu.make_async_copy(acc1_h, acc1, asem.at[0]), pltpu.make_async_copy(acc2_h, acc2, asem.at[1])]
        for cp in accs:
            cp.start()

    def over_rows(body):
        def step(i, carry):
            body(pl.ds(pl.multiple_of(i * ROWS, ROWS), ROWS))
            return carry

        lax.fori_loop(0, D // ROWS, step, 0)

    def over_lanes(body):
        def step(i, carry):
            body(pl.ds(pl.multiple_of(i * CHUNK, CHUNK), CHUNK))
            return carry

        lax.fori_loop(0, W // CHUNK, step, 0)

    for s in range(k):
        at = pl.ds(pl.multiple_of(lax.rem(me - s + k, k) * c, 16), c)
        x0[at, : piece.width] = ins[s][0]
        dy[at, : piece.width] = ins[s][1].astype(F32)
    if W > piece.width:
        x0[:, piece.width :] = jnp.zeros((D, W - piece.width), BF)
        dy[:, piece.width :] = jnp.zeros((D, W - piece.width), F32)
    for l in range(layers):
        if W > piece.total:
            mixs[l, :, piece.total :] = jnp.zeros((D, W - piece.total), F32)
        sc[l, D:, :] = jnp.ones((sc.shape[1] - D, W), BF)

    def state(l, r):
        return x0[r, :].astype(F32) if l == 0 else x1[r, :]

    for l in range(layers):
        a, b, g, f, h, ff, b2 = [lambda r, j=j, l=l: cols[l, r, j : j + 1] for j in range(7)]
        nxt = x1 if l + 1 < layers else gn

        def normalise(r, l=l):
            nrm[l, r, :] = (state(l, r) * a(r) + b(r)).astype(BF)

        over_rows(normalise)
        for group, _, o in piece.members:
            p = patches[group]
            mixs[l, :, o : o + p] = nn(nrm[l, :, o : o + p], mixt[group][l])

        def blend(r, l=l, nxt=nxt):
            mixture = mixs[l, r, :] + pb_ref[l]
            mixs[l, r, :] = mixture
            middle = state(l, r) + g(r) * mixture
            nxt[r, :] = middle
            sc[l, r, :] = (middle * f(r) + h(r)).astype(BF)

        over_rows(blend)
        for cp in loads[l]:
            cp.wait()

        def mlp(ln, l=l, nxt=nxt):
            s = sc[l, :D, ln]
            for i in range(F // FFC):
                fr = pl.ds(i * FFC, FFC)
                v = nn(bufp[l, fr, :], s) + b1c[l, fr, :]
                v2 = v * v
                t = jnp.tanh(v * (0.7978845608 + (0.7978845608 * 0.044715) * v2))
                hp = 0.5 * t + 0.5
                ac = v * hp
                q = 2 * 0.7978845608 + (6 * 0.7978845608 * 0.044715) * v2
                act[l, fr, ln] = ac.astype(BF)
                dact[l, fr, ln] = (hp + (ac - ac * hp) * q).astype(BF)
            br = (nn(bufq[l], act[l, :, ln]) + cols[l, :, 6:7]).astype(BF)
            brs[l, :, ln] = br
            nxt[:, ln] = nxt[:, ln] + cols[l, :, 5:6] * br.astype(F32)

        over_lanes(mlp)
        for cp in reloads[l]:
            cp.start()

    for s in range(k):
        at = pl.ds(pl.multiple_of(lax.rem(me + s, k) * c, 16), c)
        outs[s][0] = gn[at, : piece.width].astype(BF)

    if first:
        acc1[...] = jnp.zeros(acc1.shape, F32)
        acc2[...] = jnp.zeros(acc2.shape, F32)
    else:
        for cp in accs:
            cp.wait()
    gcol[...] = jnp.zeros(gcol.shape, F32)
    if W > piece.total:
        gn[:, piece.total :] = jnp.zeros((D, W - piece.total), F32)

    stores = []
    for l in reversed(range(layers)):
        a, b, g, f, h, ff, b2 = [lambda r, j=j, l=l: cols[l, r, j : j + 1] for j in range(7)]

        def put(r, j, v):
            gcol[r, j : j + 1] = jnp.sum(v, 1, keepdims=True)

        def gain(r, l=l):
            d = dy[r, :]
            put(r, 5, d * brs[l, r, :].astype(F32))
            gbv = (d * ff(r)).astype(BF)
            gb[r, :] = gbv
            put(r, 6, gbv.astype(F32))

        over_rows(gain)
        for cp in reloads[l]:
            cp.wait()

        def mlp_back(ln, l=l):
            up = gb[:, ln]
            for i in range(F // FFC):
                fr = pl.ds(i * FFC, FFC)
                gh = nn(bufp[l, fr, :], up) * dact[l, fr, ln].astype(F32)
                dact[l, fr, ln] = gh.astype(BF)
            gs[:, ln] = nn(bufq[l], dact[l, :, ln]).astype(BF)

        over_lanes(mlp_back)

        def weight_in(n, carry, l=l):
            fr = pl.ds(pl.multiple_of(n * 256, 256), 256)
            r = nt(sc[l], dact[l, fr, :])
            acc1[l, :, fr] = acc1[l, :, fr] + r[:D]
            gb1[:, fr] = r[D : D + 8]
            return carry

        lax.fori_loop(0, F // 256, weight_in, 0)

        def weight_out(n, carry, l=l):
            fr = pl.ds(pl.multiple_of(n * FFC, FFC), FFC)
            acc2[l, fr, :] = acc2[l, fr, :] + nt(act[l, fr, :], gb[...])
            return carry

        lax.fori_loop(0, F // FFC, weight_out, 0)
        gpb[...] = jnp.zeros(gpb.shape, F32)

        def back(r, l=l):
            gsf = gs[r, :].astype(F32)
            mixture = mixs[l, r, :]
            middle = state(l, r) + g(r) * mixture
            gm = dy[r, :] + f(r) * gsf
            dy[r, :] = gm
            put(r, 3, gsf * middle)
            put(r, 4, gsf)
            put(r, 2, gm * mixture)
            gmb = (g(r) * gm).astype(BF)
            gb[r, :] = gmb
            gpb[...] = gpb[...] + gmb.astype(F32).reshape(ROWS // 8, 8, W).sum(0)

        over_rows(back)
        pbias = jnp.sum(gpb[...], 0, keepdims=True)
        for group, _, o in piece.members:
            p = patches[group]
            gi = gb[:, o : o + p]
            r0, l0 = rows.mix[group]
            acc2[l, r0 : r0 + p, l0 : l0 + p] = acc2[l, r0 : r0 + p, l0 : l0 + p] + tn(gi, nrm[l, :, o : o + p])
            gn[:, o : o + p] = nn(gi, mix[group][l])
            r0 = rows.patch[group]
            acc2[l, r0 : r0 + 1, :p] = acc2[l, r0 : r0 + 1, :p] + pbias[:, o : o + p]

        def last(r, l=l):
            n = gn[r, :]
            put(r, 0, n * state(l, r))
            put(r, 1, n)
            dy[r, :] = dy[r, :] + a(r) * n

        over_rows(last)
        acc2[l, rows.vec : rows.vec + 8, :] = acc2[l, rows.vec : rows.vec + 8, :] + jnp.transpose(gcol[...])[:8]
        for t in range(F // D):
            r0 = rows.bias_in + t
            acc2[l, r0 : r0 + 1, :] = acc2[l, r0 : r0 + 1, :] + gb1[0:1, t * D : (t + 1) * D]
        pair = [
            pltpu.make_async_copy(acc1.at[l], out1_h.at[l], osem.at[0, l]),
            pltpu.make_async_copy(acc2.at[l], out2_h.at[l], osem.at[1, l]),
        ]
        for cp in pair:
            cp.start()
        stores += pair

    for s in range(k):
        at = pl.ds(pl.multiple_of(lax.rem(me + s, k) * c, 16), c)
        outs[s][1] = dy[at, : piece.width].astype(BF)
    for cp in stores:
        cp.wait()


def run_layers(piece, k, patches, rows, me, bufs, weights, mixes, patch_rows, cols, b1c, accs):
    w1t, w2t, w1, w2 = weights
    L, D, F = w1.shape
    W = piece.work
    first = accs is None
    vmem = pl.BlockSpec(memory_space=pltpu.VMEM)
    smem = pl.BlockSpec(memory_space=pltpu.SMEM)
    hbm = pl.BlockSpec(memory_space=pl.ANY)
    args = [me, *bufs, w1t, w2t, w1, w2]
    specs = [smem] + [vmem] * k + [hbm] * 4
    args += [jnp.swapaxes(mixes[g], 1, 2) for g in piece.groups] + [mixes[g] for g in piece.groups]
    args += [patch_rows, cols, b1c]
    specs += [vmem] * (2 * len(piece.groups) + 3)
    if not first:
        args += list(accs)
        specs += [hbm] * 2
    c = bufs[0].shape[1]
    out_shape = [jax.ShapeDtypeStruct((2, c, piece.width), BF)] * k
    out_shape += [jax.ShapeDtypeStruct((L, D, F), F32), jax.ShapeDtypeStruct((L, rows.total, D), F32)]
    scratch = [
        pltpu.VMEM((D, W), BF),
        pltpu.VMEM((D, W), F32),
        pltpu.VMEM((D, W), F32),
        pltpu.VMEM((L, D, W), F32),
        pltpu.VMEM((L, D, W), BF),
        pltpu.VMEM((L, D + 16, W), BF),
        pltpu.VMEM((L, D, W), BF),
        pltpu.VMEM((L, F, W), BF),
        pltpu.VMEM((L, F, W), BF),
        pltpu.VMEM((D, W), BF),
        pltpu.VMEM((D, W), BF),
        pltpu.VMEM((D, W), F32),
        pltpu.VMEM((L, F, D), BF),
        pltpu.VMEM((L, D, F), BF),
        pltpu.VMEM((L, D, F), F32),
        pltpu.VMEM((L, rows.total, D), F32),
        pltpu.VMEM((8, F), F32),
        pltpu.VMEM((D, 128), F32),
        pltpu.VMEM((8, W), F32),
        pltpu.SemaphoreType.DMA((4, L)),
        pltpu.SemaphoreType.DMA((2,)),
        pltpu.SemaphoreType.DMA((2, L)),
    ]
    flops = L * 6 * 2 * D * F * W
    return pl.pallas_call(
        functools.partial(layers_kernel, piece, k, patches, rows, first, L),
        out_shape=out_shape,
        in_specs=specs,
        out_specs=[vmem] * k + [hbm] * 2,
        scratch_shapes=scratch,
        cost_estimate=pl.CostEstimate(flops=flops, bytes_accessed=40 << 20, transcendentals=L * F * W),
        compiler_params=pltpu.CompilerParams(vmem_limit_bytes=VMEM_LIMIT),
        name="layers",
    )(*args)


def flip(v, bit, n):
    return lax.ppermute(v, "dp", [(i, i ^ bit) for i in range(n)])


def halve(v, bit, n, idx):
    half = v.shape[0] // 2
    mine = (idx // bit) % 2
    send = lax.dynamic_slice_in_dim(v, (1 - mine) * half, half, 0).astype(BF)
    keep = lax.dynamic_slice_in_dim(v, mine * half, half, 0)
    return keep + flip(send, bit, n).astype(F32)


def double(v, bit, n, idx):
    other = flip(v, bit, n)
    mine = (idx // bit) % 2
    return jnp.where(mine == 0, jnp.concatenate([v, other], 0), jnp.concatenate([other, v], 0))


def cycle(v, s, k):
    return lax.ppermute(v, "swap", [(i, (i + s) % k) for i in range(k)])


def total_sum(acc1, acc2, n, k, idx, me):
    core = idx % 2
    bits = [1 << i for i in range(1, n.bit_length() - 1)]
    chains = []
    for acc, order in ((acc1, bits), (acc2, bits[::-1])):
        rows = acc.shape[1]
        v = halve(acc.reshape(2 * rows, -1), 1, n, idx)
        chains.append([v, order])
    for step in range(len(bits)):
        for chain in chains:
            chain[0] = halve(chain[0], chain[1][step], n, idx)
    for chain in chains:
        v = chain[0]
        part = v.shape[0] // k
        total = lax.dynamic_slice_in_dim(v, me * part, part, 0)
        for s in range(1, k):
            send = lax.dynamic_slice_in_dim(v, ((me + s) % k) * part, part, 0).astype(BF)
            total = total + cycle(send, s, k).astype(F32)
        done = total.astype(BF)
        out = jnp.zeros(v.shape, BF)
        out = lax.dynamic_update_slice_in_dim(out, done, me * part, 0)
        for s in range(1, k):
            out = lax.dynamic_update_slice_in_dim(out, cycle(done, s, k), ((me - s) % k) * part, 0)
        chain[0] = out
    for step in reversed(range(len(bits))):
        for chain in chains:
            chain[0] = double(chain[0], chain[1][step], n, idx)
    results = []
    for chain, acc in zip(chains, (acc1, acc2)):
        results.append(double(chain[0], 1, n, idx).reshape(acc.shape).astype(F32))
    return results


def on_device(
    n_dp,
    k,
    source_tiles_smallest,
    source_tiles_moderate,
    source_tiles_largest,
    target_cotangent_smallest,
    target_cotangent_moderate,
    target_cotangent_largest,
    surviving_tallies,
    token_affine_factor,
    token_affine_addend,
    crosstile_matrix_smallest,
    crosstile_matrix_moderate,
    crosstile_matrix_largest,
    crosstile_addend_smallest,
    crosstile_addend_moderate,
    crosstile_addend_largest,
    token_blend_factor,
    feedforward_affine_factor,
    feedforward_affine_addend,
    widening_matrix,
    widening_addend,
    narrowing_matrix,
    narrowing_addend,
    feedforward_factor,
):
    L, D, F = widening_matrix.shape
    tensors = [source_tiles_smallest, source_tiles_moderate, source_tiles_largest]
    cotans = [target_cotangent_smallest, target_cotangent_moderate, target_cotangent_largest]
    mixes = [crosstile_matrix_smallest, crosstile_matrix_moderate, crosstile_matrix_largest]
    biases = [crosstile_addend_smallest, crosstile_addend_moderate, crosstile_addend_largest]
    patches = [t.shape[0] for t in tensors]
    images = [t.shape[1] for t in tensors]
    own = [count // k for count in images]
    idx = lax.axis_index("dp")
    pos = lax.axis_index("swap")
    me = pos.astype(jnp.int32).reshape(1)
    live = surviving_tallies[0]

    pieces = [
        Piece([(1, i) for i in range(own[1])] + [(0, 0)], patches),
        Piece([(2, i) for i in range(own[2])] + [(0, i) for i in range(1, own[0])], patches),
    ]
    rows = Rows(F, D, patches, max(128, n_dp // 2 * k))

    tensors = [jnp.transpose(t, (1, 2, 0)) for t in tensors]
    cotans = [jnp.transpose(t, (1, 2, 0)) for t in cotans]
    cols = jnp.stack(
        [
            token_affine_factor,
            token_affine_addend,
            token_blend_factor,
            feedforward_affine_factor,
            feedforward_affine_addend,
            feedforward_factor,
            narrowing_addend,
            jnp.zeros_like(narrowing_addend),
        ],
        -1,
    )
    b1c = widening_addend[:, :, None]
    weights = (
        jnp.swapaxes(widening_matrix, 1, 2),
        jnp.swapaxes(narrowing_matrix, 1, 2),
        widening_matrix,
        narrowing_matrix,
    )

    packed = [pack(piece, k, patches, me, live, tensors, cotans) for piece in pieces]
    arrived = [[bufs[0]] + [cycle(bufs[s], s, k) for s in range(1, k)] for bufs in packed]
    accs = None
    sent = []
    for piece, bufs in zip(pieces, arrived):
        line = [biases[g] for g, _, _ in piece.members] + [jnp.zeros((L, piece.work - piece.total), F32)]
        patch_rows = jnp.concatenate(line, 1)[:, None, :]
        out = run_layers(piece, k, patches, rows, me, bufs, weights, mixes, patch_rows, cols, b1c, accs)
        accs = out[k:]
        sent.append([out[0]] + [cycle(out[s], s, k) for s in range(1, k)])
    outs = [None] * 6
    for used, groups in (((0,), (1,)), ((0, 1), (0, 2))):
        got = unpack([pieces[i] for i in used], groups, k, patches, images, me, live, [sent[i] for i in used])
        for i, g in enumerate(groups):
            outs[g] = jnp.transpose(got[2 * i], (2, 0, 1))
            outs[3 + g] = jnp.transpose(got[2 * i + 1], (2, 0, 1))
    acc1, acc2 = total_sum(accs[0], accs[1], n_dp, k, idx, pos)

    def vec(j):
        return acc2[:, rows.vec + j]

    def mix_of(g):
        r0, l0 = rows.mix[g]
        return acc2[:, r0 : r0 + patches[g], l0 : l0 + patches[g]]

    return (
        *outs,
        vec(0),
        vec(1),
        mix_of(0),
        mix_of(1),
        mix_of(2),
        acc2[:, rows.patch[0], : patches[0]],
        acc2[:, rows.patch[1], : patches[1]],
        acc2[:, rows.patch[2], : patches[2]],
        vec(2),
        vec(3),
        vec(4),
        acc1,
        acc2[:, rows.bias_in : rows.bias_in + F // D].reshape(L, F),
        acc2[:, :F],
        vec(6),
        vec(5),
    )


def solution(mesh):
    tokens = P(None, "dp", "swap")
    in_specs = (tokens,) * 6 + (P("dp", None),) + (P(),) * 16
    out_specs = (tokens,) * 6 + (P(),) * 16
    return jax.shard_map(
        functools.partial(on_device, mesh.shape["dp"], mesh.shape["swap"]),
        mesh=mesh,
        in_specs=in_specs,
        out_specs=out_specs,
        check_vma=False,
    )
```

```python
import functools

import jax
import jax.numpy as jnp
from jax import lax
from jax.experimental import pallas as pl
from jax.experimental.pallas import tpu as pltpu
from jax.sharding import PartitionSpec as P

BF = jnp.bfloat16
F32 = jnp.float32
FFC = 256
ROWS = 128
VMEM_LIMIT = 62 << 20


def round_up(value, unit):
    return -(-value // unit) * unit


def nt(a, b):
    return lax.dot_general(a, b, (((1,), (1,)), ((), ())), preferred_element_type=F32)


def tn(a, b):
    return lax.dot_general(a, b, (((0,), (0,)), ((), ())), preferred_element_type=F32)


def nn(a, b):
    return jnp.dot(a, b, preferred_element_type=F32)


class Piece:
    def __init__(self, members, patches):
        self.members = []
        offset = 0
        for group, index in members:
            self.members.append((group, index, offset))
            offset += patches[group]
        self.total = offset
        self.width = round_up(offset, 128)
        self.work = round_up(offset, 256)
        self.groups = sorted({group for group, _ in members})


def pack_kernel(piece, k, patches, me_ref, live_ref, *refs):
    ng = len(piece.groups)
    xs = dict(zip(piece.groups, refs[:ng]))
    cs = dict(zip(piece.groups, refs[ng : 2 * ng]))
    outs = refs[2 * ng :]
    me = me_ref[0]
    for s in range(k):
        owner = lax.rem(me + s, k)
        out = outs[s]
        for group, index, offset in piece.members:
            p = patches[group]
            image = owner + k * index
            alive = (image < live_ref[group]).astype(F32)
            out[0, :, offset : offset + p] = xs[group][image]
            out[1, :, offset : offset + p] = (cs[group][image].astype(F32) * alive).astype(BF)
        if piece.width > piece.total:
            c = out.shape[1]
            out[:, :, piece.total :] = jnp.zeros((2, c, piece.width - piece.total), BF)


def pack(piece, k, patches, me, live, tensors, cotans):
    c = tensors[0].shape[1]
    vmem = pl.BlockSpec(memory_space=pltpu.VMEM)
    smem = pl.BlockSpec(memory_space=pltpu.SMEM)
    return pl.pallas_call(
        functools.partial(pack_kernel, piece, k, patches),
        out_shape=[jax.ShapeDtypeStruct((2, c, piece.width), BF)] * k,
        in_specs=[smem, smem] + [vmem] * (2 * len(piece.groups)),
        out_specs=[vmem] * k,
        compiler_params=pltpu.CompilerParams(vmem_limit_bytes=48 << 20),
        name="pack",
    )(me, live, *[tensors[g] for g in piece.groups], *[cotans[g] for g in piece.groups])


def unpack_kernel(pieces, groups, k, patches, me_ref, live_ref, *refs):
    buffers = [refs[i * k : (i + 1) * k] for i in range(len(pieces))]
    outs = refs[len(pieces) * k :]
    me = me_ref[0]
    for piece, bufs in zip(pieces, buffers):
        for s in range(k):
            owner = lax.rem(me - s + k, k)
            for group, index, offset in piece.members:
                if group not in groups:
                    continue
                at = 2 * groups.index(group)
                p = patches[group]
                image = owner + k * index
                alive = (image < live_ref[group]).astype(F32)
                outs[at][image] = bufs[s][0, :, offset : offset + p].astype(F32) * alive
                outs[at + 1][image] = bufs[s][1, :, offset : offset + p].astype(F32)


def unpack(pieces, groups, k, patches, images, me, live, buffers):
    c = buffers[0][0].shape[1]
    vmem = pl.BlockSpec(memory_space=pltpu.VMEM)
    smem = pl.BlockSpec(memory_space=pltpu.SMEM)
    shapes = []
    for g in groups:
        shapes += [jax.ShapeDtypeStruct((images[g], c, patches[g]), F32)] * 2
    return pl.pallas_call(
        functools.partial(unpack_kernel, pieces, groups, k, patches),
        out_shape=shapes,
        in_specs=[smem, smem] + [vmem] * (k * len(pieces)),
        out_specs=[vmem] * len(shapes),
        compiler_params=pltpu.CompilerParams(vmem_limit_bytes=48 << 20),
        name="unpack",
    )(me, live, *[b for bufs in buffers for b in bufs])


class Rows:
    def __init__(self, ff, width, patches, blocks):
        self.out = ff
        base = 2 * ff
        self.mix = [
            (base + round_up(patches[2], 8), round_up(patches[1], 128)),
            (base + round_up(patches[2], 8), 0),
            (base, 0),
        ]
        self.misc = base
        base += round_up(patches[2], 8) + round_up(patches[1], 8)
        self.bias_in = base
        self.patch = [base + ff // width + g for g in range(3)]
        self.vec = round_up(base + ff // width + 3, 8)
        self.used = self.vec + 8
        self.blocks = blocks
        self.block = round_up(-(-self.used // blocks), 8)
        self.total = blocks * self.block


def layers_kernel(piece, k, patches, rows, first, last, layers, *refs):
    refs = list(refs)

    def take(n):
        out, refs[:] = refs[:n], refs[n:]
        return out

    (me_ref,) = take(1)
    ins = take(k)
    w1t_h, w2t_h, w1_h, w2_h = take(4)
    mixt = dict(zip(piece.groups, take(len(piece.groups))))
    mix = dict(zip(piece.groups, take(len(piece.groups))))
    pb_ref, cols, b1c = take(3)
    if not first:
        (acc_h,) = take(1)
    outs = take(k)
    if last:
        send_h, keep_h = take(2)
    else:
        (out_h,) = take(1)
    (x0, x1, gn, mixs, nrm, sc, brs, act, dact, gb, gs, dy, bufp, bufq, acc, stage, gb1, gcol, gpb, wsem, asem, osem) = refs

    D, W = x1.shape
    F = bufp.shape[1]
    c = D // k
    me = me_ref[0]
    core = lax.rem(me_ref[1], 2)
    loads = [
        (pltpu.make_async_copy(w1t_h.at[l], bufp.at[l], wsem.at[0, l]),
         pltpu.make_async_copy(w2t_h.at[l], bufq.at[l], wsem.at[1, l]))
        for l in range(layers)
    ]
    reloads = [
        (pltpu.make_async_copy(w2_h.at[l], bufp.at[l], wsem.at[2, l]),
         pltpu.make_async_copy(w1_h.at[l], bufq.at[l], wsem.at[3, l]))
        for l in range(layers)
    ]
    for pair in loads:
        for cp in pair:
            cp.start()
    if not first:
        load_acc = pltpu.make_async_copy(acc_h, acc, asem)
        load_acc.start()

    def over_rows(body):
        def step(i, carry):
            body(pl.ds(pl.multiple_of(i * ROWS, ROWS), ROWS))
            return carry

        lax.fori_loop(0, D // ROWS, step, 0)

    def over_lanes(body):
        body(pl.ds(0, W))

    for s in range(k):
        at = pl.ds(pl.multiple_of(lax.rem(me - s + k, k) * c, 16), c)
        x0[at, : piece.width] = ins[s][0]
        dy[at, : piece.width] = ins[s][1].astype(F32)
    if W > piece.width:
        x0[:, piece.width :] = jnp.zeros((D, W - piece.width), BF)
        dy[:, piece.width :] = jnp.zeros((D, W - piece.width), F32)
    for l in range(layers):
        if W > piece.total:
            mixs[l, :, piece.total :] = jnp.zeros((D, W - piece.total), F32)
        sc[l, D:, :] = jnp.ones((sc.shape[1] - D, W), BF)

    def state(l, r):
        return x0[r, :].astype(F32) if l == 0 else x1[r, :]

    for l in range(layers):
        a, b, g, f, h, ff, b2 = [lambda r, j=j, l=l: cols[l, r, j : j + 1] for j in range(7)]
        nxt = x1 if l + 1 < layers else gn

        def normalise(r, l=l):
            nrm[l, r, :] = (state(l, r) * a(r) + b(r)).astype(BF)

        over_rows(normalise)
        for group, _, o in piece.members:
            p = patches[group]
            mixs[l, :, o : o + p] = nn(nrm[l, :, o : o + p], mixt[group][l])

        def blend(r, l=l, nxt=nxt):
            mixture = mixs[l, r, :] + pb_ref[l]
            mixs[l, r, :] = mixture
            middle = state(l, r) + g(r) * mixture
            nxt[r, :] = middle
            sc[l, r, :] = (middle * f(r) + h(r)).astype(BF)

        over_rows(blend)
        for cp in loads[l]:
            cp.wait()

        def mlp(ln, l=l, nxt=nxt):
            s = sc[l, :D, ln]
            for i in range(F // FFC):
                fr = pl.ds(i * FFC, FFC)
                v = nn(bufp[l, fr, :], s) + b1c[l, fr, :]
                v2 = v * v
                t = jnp.tanh(v * (0.7978845608 + (0.7978845608 * 0.044715) * v2))
                hp = 0.5 * t + 0.5
                ac = v * hp
                q = 2 * 0.7978845608 + (6 * 0.7978845608 * 0.044715) * v2
                act[l, fr, ln] = ac.astype(BF)
                dact[l, fr, ln] = (hp + (ac - ac * hp) * q).astype(BF)
            br = (nn(bufq[l], act[l, :, ln]) + cols[l, :, 6:7]).astype(BF)
            brs[l, :, ln] = br
            nxt[:, ln] = nxt[:, ln] + cols[l, :, 5:6] * br.astype(F32)

        over_lanes(mlp)
        for cp in reloads[l]:
            cp.start()

    for s in range(k):
        at = pl.ds(pl.multiple_of(lax.rem(me + s, k) * c, 16), c)
        outs[s][0] = gn[at, : piece.width].astype(BF)

    if first:
        acc[:, rows.misc :, :] = jnp.zeros((layers, rows.total - rows.misc, D), F32)
    else:
        load_acc.wait()
    gcol[...] = jnp.zeros(gcol.shape, F32)
    if W > piece.total:
        gn[:, piece.total :] = jnp.zeros((D, W - piece.total), F32)

    stores = []
    for l in reversed(range(layers)):
        a, b, g, f, h, ff, b2 = [lambda r, j=j, l=l: cols[l, r, j : j + 1] for j in range(7)]

        def put(r, j, v):
            gcol[r, j : j + 1] = jnp.sum(v, 1, keepdims=True)

        def gain(r, l=l):
            d = dy[r, :]
            put(r, 5, d * brs[l, r, :].astype(F32))
            gbv = (d * ff(r)).astype(BF)
            gb[r, :] = gbv
            put(r, 6, gbv.astype(F32))

        over_rows(gain)
        for cp in reloads[l]:
            cp.wait()

        def mlp_back(ln, l=l):
            up = gb[:, ln]
            for i in range(F // FFC):
                fr = pl.ds(i * FFC, FFC)
                gh = nn(bufp[l, fr, :], up) * dact[l, fr, ln].astype(F32)
                dact[l, fr, ln] = gh.astype(BF)
            gs[:, ln] = nn(bufq[l], dact[l, :, ln]).astype(BF)

        over_lanes(mlp_back)

        def weight_in(n, carry, l=l):
            r = nt(sc[l], dact[l, pl.ds(pl.multiple_of(n * 2 * D, 2 * D), 2 * D), :])
            for i in range(2):
                at = pl.ds(pl.multiple_of((2 * n + i) * D, D), D)
                part = r[:D, i * D : (i + 1) * D]
                acc[l, at, :] = part if first else acc[l, at, :] + part
            gb1[:, pl.ds(pl.multiple_of(n * 2 * D, 2 * D), 2 * D)] = r[D : D + 8]
            return carry

        lax.fori_loop(0, F // (2 * D), weight_in, 0)

        def weight_out(n, carry, l=l):
            r = nt(act[l, pl.ds(pl.multiple_of(n * 512, 512), 512), :], gb[...])
            at = pl.ds(pl.multiple_of(rows.out + n * 512, 512), 512)
            acc[l, at, :] = r if first else acc[l, at, :] + r
            return carry

        lax.fori_loop(0, F // 512, weight_out, 0)
        gpb[...] = jnp.zeros(gpb.shape, F32)

        def back(r, l=l):
            gsf = gs[r, :].astype(F32)
            mixture = mixs[l, r, :]
            middle = state(l, r) + g(r) * mixture
            gm = dy[r, :] + f(r) * gsf
            dy[r, :] = gm
            put(r, 3, gsf * middle)
            put(r, 4, gsf)
            put(r, 2, gm * mixture)
            gmb = (g(r) * gm).astype(BF)
            gb[r, :] = gmb
            gpb[...] = gpb[...] + gmb.astype(F32).reshape(ROWS // 8, 8, W).sum(0)

        over_rows(back)
        pbias = jnp.sum(gpb[...], 0, keepdims=True)
        for group, _, o in piece.members:
            p = patches[group]
            gi = gb[:, o : o + p]
            r0, l0 = rows.mix[group]
            acc[l, r0 : r0 + p, l0 : l0 + p] = acc[l, r0 : r0 + p, l0 : l0 + p] + tn(gi, nrm[l, :, o : o + p])
            gn[:, o : o + p] = nn(gi, mix[group][l])
            r0 = rows.patch[group]
            acc[l, r0 : r0 + 1, :p] = acc[l, r0 : r0 + 1, :p] + pbias[:, o : o + p]

        def finish(r, l=l):
            n = gn[r, :]
            put(r, 0, n * state(l, r))
            put(r, 1, n)
            dy[r, :] = dy[r, :] + a(r) * n

        over_rows(finish)
        acc[l, rows.vec : rows.vec + 8, :] = acc[l, rows.vec : rows.vec + 8, :] + jnp.transpose(gcol[...])[:8]
        for t in range(F // D):
            r0 = rows.bias_in + t
            acc[l, r0 : r0 + 1, :] = acc[l, r0 : r0 + 1, :] + gb1[0:1, t * D : (t + 1) * D]
        if last:
            half = rows.total // 2
            stage[l] = acc[l, pl.ds(pl.multiple_of((1 - core) * half, 16), half), :].astype(BF)
            kept = acc.at[l, pl.ds(pl.multiple_of(core * half, 16), half)]
            pair = [
                pltpu.make_async_copy(stage.at[l], send_h.at[l], osem.at[0, l]),
                pltpu.make_async_copy(kept, keep_h.at[l], osem.at[1, l]),
            ]
        else:
            pair = [pltpu.make_async_copy(acc.at[l], out_h.at[l], osem.at[0, l])]
        for cp in pair:
            cp.start()
        stores += pair

    for s in range(k):
        at = pl.ds(pl.multiple_of(lax.rem(me + s, k) * c, 16), c)
        outs[s][1] = dy[at, : piece.width].astype(BF)
    for cp in stores:
        cp.wait()


def run_layers(piece, k, patches, rows, me, bufs, weights, mixes, patch_rows, cols, b1c, acc, last):
    w1t, w2t, w1, w2 = weights
    L, D, F = w1.shape
    W = piece.work
    first = acc is None
    vmem = pl.BlockSpec(memory_space=pltpu.VMEM)
    smem = pl.BlockSpec(memory_space=pltpu.SMEM)
    hbm = pl.BlockSpec(memory_space=pl.ANY)
    args = [me, *bufs, w1t, w2t, w1, w2]
    specs = [smem] + [vmem] * k + [hbm] * 4
    args += [jnp.swapaxes(mixes[g], 1, 2) for g in piece.groups] + [mixes[g] for g in piece.groups]
    args += [patch_rows, cols, b1c]
    specs += [vmem] * (2 * len(piece.groups) + 3)
    if not first:
        args += [acc]
        specs += [hbm]
    c = bufs[0].shape[1]
    out_shape = [jax.ShapeDtypeStruct((2, c, piece.width), BF)] * k
    half = rows.total // 2
    if last:
        out_shape += [jax.ShapeDtypeStruct((L, half, D), BF), jax.ShapeDtypeStruct((L, half, D), F32)]
    else:
        out_shape += [jax.ShapeDtypeStruct((L, rows.total, D), F32)]
    scratch = [
        pltpu.VMEM((D, W), BF),
        pltpu.VMEM((D, W), F32),
        pltpu.VMEM((D, W), F32),
        pltpu.VMEM((L, D, W), F32),
        pltpu.VMEM((L, D, W), BF),
        pltpu.VMEM((L, D + 16, W), BF),
        pltpu.VMEM((L, D, W), BF),
        pltpu.VMEM((L, F, W), BF),
        pltpu.VMEM((L, F, W), BF),
        pltpu.VMEM((D, W), BF),
        pltpu.VMEM((D, W), BF),
        pltpu.VMEM((D, W), F32),
        pltpu.VMEM((L, F, D), BF),
        pltpu.VMEM((L, D, F), BF),
        pltpu.VMEM((L, rows.total, D), F32),
        pltpu.VMEM((L, half, D) if last else (8, 128), BF),
        pltpu.VMEM((8, F), F32),
        pltpu.VMEM((D, 128), F32),
        pltpu.VMEM((8, W), F32),
        pltpu.SemaphoreType.DMA((4, L)),
        pltpu.SemaphoreType.DMA,
        pltpu.SemaphoreType.DMA((2, L)),
    ]
    flops = L * 6 * 2 * D * F * W
    return pl.pallas_call(
        functools.partial(layers_kernel, piece, k, patches, rows, first, last, L),
        out_shape=out_shape,
        in_specs=specs,
        out_specs=[vmem] * k + [hbm] * (len(out_shape) - k),
        scratch_shapes=scratch,
        cost_estimate=pl.CostEstimate(flops=flops, bytes_accessed=40 << 20, transcendentals=L * F * W),
        compiler_params=pltpu.CompilerParams(vmem_limit_bytes=VMEM_LIMIT),
        name="layers",
    )(*args)


def flip(v, bit, n):
    return lax.ppermute(v, "dp", [(i, i ^ bit) for i in range(n)])


def cycle(v, s, k):
    return lax.ppermute(v, "swap", [(i, (i + s) % k) for i in range(k)])


def local(body, pos, ins, shapes, name):
    vmem = pl.BlockSpec(memory_space=pltpu.VMEM)
    return pl.pallas_call(
        body,
        out_shape=[jax.ShapeDtypeStruct(*shape) for shape in shapes],
        in_specs=[pl.BlockSpec(memory_space=pltpu.SMEM)] + [vmem] * len(ins),
        out_specs=[vmem] * len(shapes),
        compiler_params=pltpu.CompilerParams(vmem_limit_bytes=40 << 20),
        name=name,
    )(pos, *ins)


def side(pos_ref, bit):
    return lax.rem(lax.div(pos_ref[1], bit), 2)


def split_first(pos, keep, came, bits):
    n, r, d = keep.shape
    q = n // 4

    def body(pos_ref, keep_ref, came_ref, *outs):
        for h in range(2):
            mine = side(pos_ref, bits[h])
            at = pl.ds(2 * q * h + mine * q, q)
            outs[2 * h][...] = keep_ref[at] + came_ref[at].astype(F32)
            at = pl.ds(2 * q * h + (1 - mine) * q, q)
            outs[2 * h + 1][...] = (keep_ref[at] + came_ref[at].astype(F32)).astype(BF)

    out = local(body, pos, [keep, came], [((q, r, d), F32), ((q, r, d), BF)] * 2, "split")
    return [(out[0], out[1]), (out[2], out[3])]


def split_next(pos, keeps, cames, bits):
    n, r, d = keeps[0].shape
    q = n // 2

    def body(pos_ref, k0, k1, c0, c1, *outs):
        for h, (keep_ref, came_ref) in enumerate(((k0, c0), (k1, c1))):
            mine = side(pos_ref, bits[h])
            at = pl.ds(mine * q, q)
            outs[2 * h][...] = keep_ref[at] + came_ref[at].astype(F32)
            at = pl.ds((1 - mine) * q, q)
            outs[2 * h + 1][...] = (keep_ref[at] + came_ref[at].astype(F32)).astype(BF)

    out = local(body, pos, [*keeps, *cames], [((q, r, d), F32), ((q, r, d), BF)] * 2, "split")
    return [(out[0], out[1]), (out[2], out[3])]


def split_swap(pos, keeps, cames, k):
    n, r, d = keeps[0].shape

    def body(pos_ref, k0, k1, c0, c1, *refs):
        outs, both = refs[:k], refs[k]
        both[:n] = k0[...] + c0[...].astype(F32)
        both[n:] = k1[...] + c1[...].astype(F32)
        me = pos_ref[0]
        outs[0][...] = both[me]
        for s in range(1, k):
            outs[s][...] = both[lax.rem(me + s, k)].astype(BF)

    vmem = pl.BlockSpec(memory_space=pltpu.VMEM)
    return pl.pallas_call(
        body,
        out_shape=[jax.ShapeDtypeStruct((r, d), F32)] + [jax.ShapeDtypeStruct((r, d), BF)] * (k - 1),
        in_specs=[pl.BlockSpec(memory_space=pltpu.SMEM)] + [vmem] * 4,
        out_specs=[vmem] * k,
        scratch_shapes=[pltpu.VMEM((2 * n, r, d), F32)],
        name="split_swap",
    )(pos, *keeps, *cames)


def add_swap(pos, keep, cames):
    def body(pos_ref, keep_ref, *refs):
        total = keep_ref[...]
        for came in refs[:-1]:
            total = total + came[...].astype(F32)
        refs[-1][...] = total.astype(BF)

    return local(body, pos, [keep, *cames], [(keep.shape, BF)], "add_swap")[0]


def join_swap(pos, parts, k):
    r, d = parts[0].shape
    n = k // 2

    def body(pos_ref, *refs):
        ins, (o0, o1), both = refs[:k], refs[k : k + 2], refs[k + 2]
        for s in range(k):
            both[lax.rem(pos_ref[0] - s + k, k)] = ins[s][...]
        o0[...] = both[:n]
        o1[...] = both[n:]

    vmem = pl.BlockSpec(memory_space=pltpu.VMEM)
    return pl.pallas_call(
        body,
        out_shape=[jax.ShapeDtypeStruct((n, r, d), BF)] * 2,
        in_specs=[pl.BlockSpec(memory_space=pltpu.SMEM)] + [vmem] * k,
        out_specs=[vmem] * 2,
        scratch_shapes=[pltpu.VMEM((k, r, d), BF)],
        name="join_swap",
    )(pos, *parts)


def join(pos, owns, cames, bits, whole):
    q, r, d = owns[0].shape

    def body(pos_ref, v0, v1, c0, c1, *outs):
        for h, (own, came) in enumerate(((v0, c0), (v1, c1))):
            mine = side(pos_ref, bits[h])
            out, base = (outs[0], 2 * q * h) if whole else (outs[h], 0)
            out[pl.ds(base + mine * q, q)] = own[...]
            out[pl.ds(base + (1 - mine) * q, q)] = came[...]

    shapes = [((4 * q, r, d), BF)] if whole else [((2 * q, r, d), BF)] * 2
    return local(body, pos, [*owns, *cames], shapes, "join")


def finish(pos, rows, ff, layer, layers, mine, other, before):
    r, d = rows.total, mine.shape[-1]
    half = r // 2
    shapes = [(layers, d, ff), (layers, ff, d), (layers, rows.used - rows.misc, d)]

    def body(pos_ref, a_ref, b_ref, *refs):
        outs, (full, win, sem) = refs[-6:-3], refs[-3:]
        core = lax.rem(pos_ref[1], 2)
        full[pl.ds(pl.multiple_of(core * half, 16), half), :] = a_ref[...].astype(F32)
        full[pl.ds(pl.multiple_of((1 - core) * half, 16), half), :] = b_ref[...].astype(F32)
        copies = [
            pltpu.make_async_copy(full.at[pl.ds(rows.out, ff)], outs[1].at[layer], sem.at[1]),
            pltpu.make_async_copy(full.at[pl.ds(rows.misc, rows.used - rows.misc)], outs[2].at[layer], sem.at[2]),
        ]
        for t in range(ff // d):
            win[:, t * d : (t + 1) * d] = full[t * d : (t + 1) * d, :]
        copies.append(pltpu.make_async_copy(win, outs[0].at[layer], sem.at[0]))
        for cp in copies:
            cp.start()
        for cp in copies:
            cp.wait()

    vmem = pl.BlockSpec(memory_space=pltpu.VMEM)
    hbm = pl.BlockSpec(memory_space=pl.ANY)
    return pl.pallas_call(
        body,
        out_shape=[jax.ShapeDtypeStruct(shape, F32) for shape in shapes],
        in_specs=[pl.BlockSpec(memory_space=pltpu.SMEM), vmem, vmem] + [hbm] * len(before),
        out_specs=[hbm] * 3,
        scratch_shapes=[pltpu.VMEM((r, d), F32), pltpu.VMEM((d, ff), F32), pltpu.SemaphoreType.DMA((3,))],
        input_output_aliases={3 + i: i for i in range(len(before))},
        compiler_params=pltpu.CompilerParams(vmem_limit_bytes=40 << 20),
        name="finish",
    )(pos, mine, other, *before)


def orders(n):
    bits = [1 << i for i in range(1, n.bit_length() - 1)]
    return list(zip(bits, bits[::-1]))


def scatter_dp(pos, send, keep, rows, n):
    view = (rows.blocks // 2, rows.block, send.shape[-1])
    steps = orders(n)
    halves = split_first(pos, keep.reshape(view), flip(send, 1, n).reshape(view), steps[0])
    for t, bits in enumerate(steps):
        keeps = [h[0] for h in halves]
        cames = [flip(h[1], bit, n) for h, bit in zip(halves, bits)]
        if t + 1 < len(steps):
            halves = split_next(pos, keeps, cames, steps[t + 1])
    return keeps, cames


def over_swap(pos, keeps, cames, k):
    parts = split_swap(pos, keeps, cames, k)
    done = add_swap(pos, parts[0], [cycle(parts[s], s, k) for s in range(1, k)])
    return [done] + [cycle(done, s, k) for s in range(1, k)]


def gather_dp(pos, parts, n, k):
    owns = join_swap(pos, parts, k)
    steps = orders(n)
    for t in reversed(range(len(steps))):
        cames = [flip(v, bit, n) for v, bit in zip(owns, steps[t])]
        owns = join(pos, owns, cames, steps[t], t == 0)
    mine = owns[0].reshape(-1, owns[0].shape[-1])
    return mine, flip(mine, 1, n)


def on_device(
    n_dp,
    k,
    source_tiles_smallest,
    source_tiles_moderate,
    source_tiles_largest,
    target_cotangent_smallest,
    target_cotangent_moderate,
    target_cotangent_largest,
    surviving_tallies,
    token_affine_factor,
    token_affine_addend,
    crosstile_matrix_smallest,
    crosstile_matrix_moderate,
    crosstile_matrix_largest,
    crosstile_addend_smallest,
    crosstile_addend_moderate,
    crosstile_addend_largest,
    token_blend_factor,
    feedforward_affine_factor,
    feedforward_affine_addend,
    widening_matrix,
    widening_addend,
    narrowing_matrix,
    narrowing_addend,
    feedforward_factor,
):
    L, D, F = widening_matrix.shape
    tensors = [source_tiles_smallest, source_tiles_moderate, source_tiles_largest]
    cotans = [target_cotangent_smallest, target_cotangent_moderate, target_cotangent_largest]
    mixes = [crosstile_matrix_smallest, crosstile_matrix_moderate, crosstile_matrix_largest]
    biases = [crosstile_addend_smallest, crosstile_addend_moderate, crosstile_addend_largest]
    patches = [t.shape[0] for t in tensors]
    images = [t.shape[1] for t in tensors]
    own = [count // k for count in images]
    idx = lax.axis_index("dp")
    pos = lax.axis_index("swap")
    me = jnp.stack([pos, idx]).astype(jnp.int32)
    live = surviving_tallies[0]

    pieces = [
        Piece([(1, i) for i in range(own[1])] + [(0, 0)], patches),
        Piece([(2, i) for i in range(own[2])] + [(0, i) for i in range(1, own[0])], patches),
    ]
    rows = Rows(F, D, patches, n_dp * k)

    tensors = [jnp.transpose(t, (1, 2, 0)) for t in tensors]
    cotans = [jnp.transpose(t, (1, 2, 0)) for t in cotans]
    cols = jnp.stack(
        [
            token_affine_factor,
            token_affine_addend,
            token_blend_factor,
            feedforward_affine_factor,
            feedforward_affine_addend,
            feedforward_factor,
            narrowing_addend,
            jnp.zeros_like(narrowing_addend),
        ],
        -1,
    )
    b1c = widening_addend[:, :, None]
    weights = (
        jnp.swapaxes(widening_matrix, 1, 2),
        jnp.swapaxes(narrowing_matrix, 1, 2),
        widening_matrix,
        narrowing_matrix,
    )

    packed = [pack(piece, k, patches, me, live, tensors, cotans) for piece in pieces]
    arrived = []
    for bufs in packed:
        if arrived:
            bufs, arrived[-1] = lax.optimization_barrier((bufs, arrived[-1]))
        arrived.append([bufs[0]] + [cycle(bufs[s], s, k) for s in range(1, k)])
    acc = None
    sent = []
    for piece, bufs in zip(pieces, arrived):
        line = [biases[g] for g, _, _ in piece.members] + [jnp.zeros((L, piece.work - piece.total), F32)]
        patch_rows = jnp.concatenate(line, 1)[:, None, :]
        final = piece is pieces[-1]
        out = list(run_layers(piece, k, patches, rows, me, bufs, weights, mixes, patch_rows, cols, b1c, acc, final))
        if final:
            out[k:], sent[-1] = lax.optimization_barrier((out[k:], sent[-1]))
        acc = out[k]
        sent.append([out[0]] + [cycle(out[s], s, k) for s in range(1, k)])
    send, keep = out[k:]
    order = list(reversed(range(L)))
    scattered = {l: scatter_dp(me, send[l], keep[l], rows, n_dp) for l in order}
    scattered, sent[-1] = lax.optimization_barrier((scattered, sent[-1]))
    parts = {l: over_swap(me, *scattered[l], k) for l in order}
    outs = [None] * 6
    for used, groups in (((0,), (1,)), ((0, 1), (0, 2))):
        got = unpack([pieces[i] for i in used], groups, k, patches, images, me, live, [sent[i] for i in used])
        for i, g in enumerate(groups):
            outs[g] = got[2 * i]
            outs[3 + g] = got[2 * i + 1]
    parts, outs = lax.optimization_barrier((parts, outs))
    outs = [jnp.transpose(v, (2, 0, 1)) for v in outs]
    sums = []
    for l in order:
        sums = finish(me, rows, F, l, L, *gather_dp(me, parts[l], n_dp, k), sums)
    grad_in, grad_out, misc = sums

    def vec(j):
        return misc[:, rows.vec - rows.misc + j]

    def patch_bias(g):
        return misc[:, rows.patch[g] - rows.misc, : patches[g]]

    def mix_of(g):
        r0, l0 = rows.mix[g]
        return misc[:, r0 - rows.misc : r0 - rows.misc + patches[g], l0 : l0 + patches[g]]

    bias_in = rows.bias_in - rows.misc
    return (
        *outs,
        vec(0),
        vec(1),
        mix_of(0),
        mix_of(1),
        mix_of(2),
        patch_bias(0),
        patch_bias(1),
        patch_bias(2),
        vec(2),
        vec(3),
        vec(4),
        grad_in,
        misc[:, bias_in : bias_in + F // D].reshape(L, F),
        grad_out,
        vec(6),
        vec(5),
    )


def solution(mesh):
    tokens = P(None, "dp", "swap")
    in_specs = (tokens,) * 6 + (P("dp", None),) + (P(),) * 16
    out_specs = (tokens,) * 6 + (P(),) * 16
    return jax.shard_map(
        functools.partial(on_device, mesh.shape["dp"], mesh.shape["swap"]),
        mesh=mesh,
        in_specs=in_specs,
        out_specs=out_specs,
        check_vma=False,
    )
```

```python
import functools

import jax
import jax.numpy as jnp
from jax import lax
from jax.experimental import pallas as pl
from jax.experimental.layout import Layout, with_layout_constraint
from jax.experimental.pallas import tpu as pltpu
from jax.sharding import PartitionSpec as P

BF = jnp.bfloat16
F32 = jnp.float32
FFC = 256
ROWS = 128
VMEM_LIMIT = 64 << 20


def round_up(value, unit):
    return -(-value // unit) * unit


def nt(a, b):
    return lax.dot_general(a, b, (((1,), (1,)), ((), ())), preferred_element_type=F32)


def tn(a, b):
    return lax.dot_general(a, b, (((0,), (0,)), ((), ())), preferred_element_type=F32)


def nn(a, b):
    return jnp.dot(a, b, preferred_element_type=F32)


class Piece:
    def __init__(self, members, patches):
        self.members = []
        offset = 0
        for group, index in members:
            self.members.append((group, index, offset))
            offset += patches[group]
        self.total = offset
        self.width = round_up(offset, 128)
        self.work = round_up(offset, 256)
        self.groups = sorted({group for group, _ in members})


def pack_kernel(piece, k, patches, masked, me_ref, live_ref, *refs):
    ng = len(piece.groups)
    xs = dict(zip(piece.groups, refs[:ng]))
    outs = refs[ng:]
    me = me_ref[0]
    for s in range(k):
        owner = lax.rem(me + s, k)
        out = outs[s]
        for group, index, offset in piece.members:
            p = patches[group]
            image = owner + k * index
            v = xs[group][image]
            if masked:
                v = (v.astype(F32) * (image < live_ref[group]).astype(F32)).astype(BF)
            out[:, offset : offset + p] = v
        if piece.width > piece.total:
            out[:, piece.total :] = jnp.zeros((out.shape[0], piece.width - piece.total), BF)


def pack(piece, k, patches, me, live, tensors, masked):
    c = tensors[0].shape[1]
    vmem = pl.BlockSpec(memory_space=pltpu.VMEM)
    smem = pl.BlockSpec(memory_space=pltpu.SMEM)
    return pl.pallas_call(
        functools.partial(pack_kernel, piece, k, patches, masked),
        out_shape=[jax.ShapeDtypeStruct((c, piece.width), BF)] * k,
        in_specs=[smem, smem] + [vmem] * len(piece.groups),
        out_specs=[vmem] * k,
        compiler_params=pltpu.CompilerParams(vmem_limit_bytes=32 << 20),
        name="pack",
    )(me, live, *[tensors[g] for g in piece.groups])


def unpack_kernel(pieces, groups, k, patches, masked, me_ref, live_ref, *refs):
    buffers = [refs[i * k : (i + 1) * k] for i in range(len(pieces))]
    outs = refs[len(pieces) * k :]
    me = me_ref[0]
    for piece, bufs in zip(pieces, buffers):
        for s in range(k):
            owner = lax.rem(me - s + k, k)
            for group, index, offset in piece.members:
                if group not in groups:
                    continue
                p = patches[group]
                image = owner + k * index
                v = bufs[s][:, offset : offset + p].astype(F32)
                if masked:
                    v = v * (image < live_ref[group]).astype(F32)
                outs[groups.index(group)][image] = v


def unpack(pieces, groups, k, patches, images, me, live, buffers, masked):
    c = buffers[0][0].shape[0]
    vmem = pl.BlockSpec(memory_space=pltpu.VMEM)
    smem = pl.BlockSpec(memory_space=pltpu.SMEM)
    return pl.pallas_call(
        functools.partial(unpack_kernel, pieces, groups, k, patches, masked),
        out_shape=[jax.ShapeDtypeStruct((images[g], c, patches[g]), F32) for g in groups],
        in_specs=[smem, smem] + [vmem] * (k * len(pieces)),
        out_specs=[vmem] * len(groups),
        compiler_params=pltpu.CompilerParams(vmem_limit_bytes=32 << 20),
        name="unpack",
    )(me, live, *[b for bufs in buffers for b in bufs])


class Rows:
    def __init__(self, ff, width, patches, blocks):
        self.out = ff
        base = 2 * ff
        self.mix = [
            (base + round_up(patches[2], 8), round_up(patches[1], 128)),
            (base + round_up(patches[2], 8), 0),
            (base, 0),
        ]
        self.misc = base
        base += round_up(patches[2], 8) + round_up(patches[1], 8)
        self.bias_in = base
        self.patch = [base + ff // width + g for g in range(3)]
        self.vec = round_up(base + ff // width + 3, 8)
        self.used = self.vec + 8
        self.blocks = blocks
        self.block = round_up(-(-self.used // blocks), 8)
        self.total = blocks * self.block


def over_rows(count, body):
    def step(i, carry):
        body(pl.ds(pl.multiple_of(i * ROWS, ROWS), ROWS))
        return carry

    lax.fori_loop(0, count // ROWS, step, 0)


def channel(cols, layer, j):
    return lambda r: cols[layer, r, j : j + 1]


class Copies:
    def __init__(self, sem):
        self.sem, self.count = sem, 0
        self.started = {}

    def start(self, key, src, dst):
        cp = pltpu.make_async_copy(src, dst, self.sem.at[self.count])
        self.count += 1
        cp.start()
        self.started[key] = cp

    def wait(self, *keys):
        for key in keys:
            self.started.pop(key).wait()

    def wait_all(self):
        self.wait(*list(self.started))


KEPT = ("state", "mixs", "nrm", "sc", "brs", "act", "dact")


def kept_shapes(layer, D, F, W):
    return {
        "state": ((D, W), BF if layer == 0 else F32),
        "mixs": ((D, W), F32),
        "nrm": ((D, W), BF),
        "sc": ((D, W), BF),
        "brs": ((D, W), BF),
        "act": ((F, W), BF),
        "dact": ((F, W), BF),
    }


def load_columns(refs, line, cols, layers):
    line[...] = jnp.zeros(line.shape, F32)
    for l in range(layers):
        for j, ref in enumerate(refs):
            line[j : j + 1, :] = ref[l : l + 1, :]
        cols[l] = jnp.transpose(line[...])


def forward_kernel(piece, k, patches, layers, *refs):
    refs = list(refs)

    def take(n):
        out, refs[:] = refs[:n], refs[n:]
        return out

    (me_ref,) = take(1)
    ins = take(k)
    w1_h, w2_h = take(2)
    mix = dict(zip(piece.groups, take(len(piece.groups))))
    bias = dict(zip(piece.groups, take(len(piece.groups))))
    vectors = take(7)
    (b1_ref,) = take(1)
    outs = take(k)
    kept_h = [dict(zip(KEPT, take(len(KEPT)))) for _ in range(layers)]
    kept = [dict(zip(KEPT, take(len(KEPT)))) for _ in range(layers)]
    last, w1, w2, line, cols, sem = refs
    D, W = last.shape
    F = w2.shape[1]
    c = D // k
    me = me_ref[0]
    copies = Copies(sem)
    for l in range(layers):
        copies.start((l, "w1"), w1_h.at[l], w1.at[l, pl.ds(0, D)])
        copies.start((l, "w2"), w2_h.at[l], w2.at[l])

    def keep(l, name):
        copies.start((l, name), kept[l][name].at[pl.ds(0, D)], kept_h[l][name])

    x0 = kept[0]["state"]
    for s in range(k):
        at = pl.ds(pl.multiple_of(lax.rem(me - s + k, k) * c, 16), c)
        x0[at, : piece.width] = ins[s][...]
    if W > piece.width:
        x0[:, piece.width :] = jnp.zeros((D, W - piece.width), BF)
    keep(0, "state")
    load_columns(vectors, line, cols, layers)

    for l in range(layers):
        a, b, g, f, h, ff, b2 = [channel(cols, l, j) for j in range(7)]
        state, mixs, nrm, sc, brs, act, dact = [kept[l][name] for name in KEPT]
        nxt = kept[l + 1]["state"] if l + 1 < layers else last
        if W > piece.total:
            mixs[:, piece.total :] = jnp.zeros((D, W - piece.total), F32)

        def normalise(r):
            nrm[r, :] = (state[r, :].astype(F32) * a(r) + b(r)).astype(BF)

        over_rows(D, normalise)
        keep(l, "nrm")
        for group, _, o in piece.members:
            p = patches[group]
            mixs[:, o : o + p] = nt(nrm[:, o : o + p], mix[group][l]) + bias[group][l : l + 1, :]

        def blend(r):
            middle = state[r, :].astype(F32) + g(r) * mixs[r, :]
            nxt[r, :] = middle
            sc[r, :] = (middle * f(r) + h(r)).astype(BF)

        over_rows(D, blend)
        keep(l, "mixs")
        keep(l, "sc")
        sc[D:, :] = jnp.ones((sc.shape[0] - D, W), BF)
        rest = b1_ref[l : l + 1, :]
        parts = []
        for _ in range(3):
            parts.append(rest.astype(BF).astype(F32))
            rest = rest - parts[-1]
        parts.append(jnp.zeros((w1.shape[1] - D - 3, F), F32))
        w1[l, D:, :] = jnp.concatenate(parts, 0).astype(BF)
        copies.wait((l, "w1"), (l, "w2"))
        s = sc[...]
        for i in range(F // FFC):
            fr = pl.ds(i * FFC, FFC)
            v = tn(w1[l, :, fr], s)
            v2 = v * v
            t = jnp.tanh(v * (0.7978845608 + (0.7978845608 * 0.044715) * v2))
            hp = 0.5 * t + 0.5
            ac = v * hp
            q = 2 * 0.7978845608 + (6 * 0.7978845608 * 0.044715) * v2
            act[fr, :] = ac.astype(BF)
            dact[fr, :] = (hp + (ac - ac * hp) * q).astype(BF)
            for name in ("act", "dact"):
                copies.start((l, name, i), kept[l][name].at[fr], kept_h[l][name].at[fr])
        br = (tn(w2[l], act[...]) + cols[l, :, 6:7]).astype(BF)
        brs[...] = br
        nxt[...] = nxt[...] + cols[l, :, 5:6] * br.astype(F32)
        keep(l, "brs")
        if l + 1 < layers:
            keep(l + 1, "state")

    for s in range(k):
        at = pl.ds(pl.multiple_of(lax.rem(me + s, k) * c, 16), c)
        outs[s][...] = last[at, : piece.width].astype(BF)
    copies.wait_all()


def with_ones(shapes, D, W):
    return {**shapes, "sc": ((D + 16, W), BF)}


def forward(piece, k, patches, me, bufs, w1, w2, mixes, biases, vectors, b1):
    L, D, F = w1.shape
    W = piece.work
    vmem = pl.BlockSpec(memory_space=pltpu.VMEM)
    smem = pl.BlockSpec(memory_space=pltpu.SMEM)
    hbm = pl.BlockSpec(memory_space=pl.ANY)
    args = [me, *bufs, w1, w2, *[mixes[g] for g in piece.groups], *[biases[g] for g in piece.groups], *vectors, b1]
    specs = [smem] + [vmem] * k + [hbm] * 2 + [vmem] * (2 * len(piece.groups) + len(vectors) + 1)
    c = bufs[0].shape[0]
    kept = [shape for l in range(L) for shape in kept_shapes(l, D, F, W).values()]
    scratch = [pltpu.VMEM(*v) for l in range(L) for v in with_ones(kept_shapes(l, D, F, W), D, W).values()]
    scratch += [
        pltpu.VMEM((D, W), F32),
        pltpu.VMEM((L, D + 16, F), BF),
        pltpu.VMEM((L, F, D), BF),
        pltpu.VMEM((128, D), F32),
        pltpu.VMEM((L, D, 128), F32),
        pltpu.SemaphoreType.DMA((L * (7 + 2 * (F // FFC)),)),
    ]
    out = pl.pallas_call(
        functools.partial(forward_kernel, piece, k, patches, L),
        out_shape=[jax.ShapeDtypeStruct((c, piece.width), BF)] * k + [jax.ShapeDtypeStruct(*v) for v in kept],
        in_specs=specs,
        out_specs=[vmem] * k + [hbm] * len(kept),
        scratch_shapes=scratch,
        compiler_params=pltpu.CompilerParams(vmem_limit_bytes=VMEM_LIMIT),
        name="forward",
    )(*args)
    n = len(KEPT)
    return out[:k], out[k:]


def backward_kernel(piece, k, patches, rows, layers, first, final, *refs):
    refs = list(refs)

    def take(n):
        out, refs[:] = refs[:n], refs[n:]
        return out

    (me_ref,) = take(1)
    ins = take(k)
    kept_h = [dict(zip(KEPT, take(len(KEPT)))) for _ in range(layers)]
    w1_h, w2_h = take(2)
    mix = dict(zip(piece.groups, take(len(piece.groups))))
    vectors = take(7)
    accs_h = [] if first else take(layers)
    outs = take(k)
    sums_h = [take(2 if final else 1) for _ in range(layers)]
    kept = [dict(zip(KEPT, take(len(KEPT)))) for _ in range(layers)]
    gn, gb, gs, dy, w1s, w2s, accs, stages, gb1, gcol, gpb, line, cols, sem = refs
    D, W = gn.shape
    F = w2s.shape[1]
    c = D // k
    me = me_ref[0]
    core = lax.rem(me_ref[1], 2)
    copies = Copies(sem)
    half_f = F // 2
    for l in reversed(range(layers)):
        copies.start((l, "brs"), kept_h[l]["brs"], kept[l]["brs"])
        copies.start((l, "w2"), w2_h.at[l], w2s.at[l])
        for i in range(2):
            at = pl.ds(i * half_f, half_f)
            copies.start((l, "dact", i), kept_h[l]["dact"].at[at], kept[l]["dact"].at[at])
        copies.start((l, "w1"), w1_h.at[l], w1s.at[l])
        copies.start((l, "sc"), kept_h[l]["sc"], kept[l]["sc"].at[pl.ds(0, D)])
        if not first:
            copies.start((l, "acc"), accs_h[l], accs.at[l])
        for name in ("act", "mixs", "state", "nrm"):
            copies.start((l, name), kept_h[l][name], kept[l][name])

    load_columns(vectors, line, cols, layers)
    for s in range(k):
        at = pl.ds(pl.multiple_of(lax.rem(me - s + k, k) * c, 16), c)
        dy[at, : piece.width] = ins[s][...].astype(F32)
    if W > piece.width:
        dy[:, piece.width :] = jnp.zeros((D, W - piece.width), F32)
    if W > piece.total:
        gn[:, piece.total :] = jnp.zeros((D, W - piece.total), F32)
    gcol[...] = jnp.zeros(gcol.shape, F32)

    def put(r, j, v):
        gcol[r, j : j + 1] = jnp.sum(v, 1, keepdims=True)

    for l in reversed(range(layers)):
        a, b, g, f, h, ff, b2 = [channel(cols, l, j) for j in range(7)]
        state, mixs, nrm, sc, brs, act, dact = [kept[l][name] for name in KEPT]
        acc = accs.at[l]
        w1, w2 = w1s.at[l], w2s.at[l]
        sc[D:, :] = jnp.ones((sc.shape[0] - D, W), BF)
        if first:
            acc[rows.misc :, :] = jnp.zeros((rows.total - rows.misc, D), F32)
        gpb[...] = jnp.zeros(gpb.shape, F32)
        copies.wait((l, "brs"))

        def gain(r):
            d = dy[r, :]
            put(r, 5, d * brs[r, :].astype(F32))
            gbv = (d * ff(r)).astype(BF)
            gb[r, :] = gbv
            put(r, 6, gbv.astype(F32))

        over_rows(D, gain)
        copies.wait((l, "w2"))
        up = gb[...]
        for i in range(F // FFC):
            if i * FFC % half_f == 0:
                copies.wait((l, "dact", i * FFC // half_f))
            fr = pl.ds(i * FFC, FFC)
            dact[fr, :] = (nn(w2[fr, :], up) * dact[fr, :].astype(F32)).astype(BF)
        copies.wait((l, "w1"))
        gs[...] = nn(w1[...], dact[...]).astype(BF)
        copies.wait((l, "sc"))
        if not first:
            copies.wait((l, "acc"))

        def weight_in(n, carry):
            r = nt(sc[...], dact[pl.ds(pl.multiple_of(n * 2 * D, 2 * D), 2 * D), :])
            for i in range(2):
                at = pl.ds(pl.multiple_of((2 * n + i) * D, D), D)
                part = r[:D, i * D : (i + 1) * D]
                acc[at, :] = part if first else acc[at, :] + part
            gb1[:, pl.ds(pl.multiple_of(n * 2 * D, 2 * D), 2 * D)] = r[D : D + 8]
            return carry

        lax.fori_loop(0, F // (2 * D), weight_in, 0)
        copies.wait((l, "act"))

        def weight_out(n, carry):
            r = nt(act[pl.ds(pl.multiple_of(n * 512, 512), 512), :], gb[...])
            at = pl.ds(pl.multiple_of(rows.out + n * 512, 512), 512)
            acc[at, :] = r if first else acc[at, :] + r
            return carry

        lax.fori_loop(0, F // 512, weight_out, 0)
        copies.wait((l, "mixs"), (l, "state"))

        def back(r):
            gsf = gs[r, :].astype(F32)
            mixture = mixs[r, :]
            middle = state[r, :].astype(F32) + g(r) * mixture
            gm = dy[r, :] + f(r) * gsf
            dy[r, :] = gm
            put(r, 3, gsf * middle)
            put(r, 4, gsf)
            put(r, 2, gm * mixture)
            gmb = (g(r) * gm).astype(BF)
            gb[r, :] = gmb
            gpb[...] = gpb[...] + gmb.astype(F32).reshape(ROWS // 8, 8, W).sum(0)

        over_rows(D, back)
        pbias = jnp.sum(gpb[...], 0, keepdims=True)
        copies.wait((l, "nrm"))
        for group, _, o in piece.members:
            p = patches[group]
            gi = gb[:, o : o + p]
            r0, l0 = rows.mix[group]
            acc[r0 : r0 + p, l0 : l0 + p] = acc[r0 : r0 + p, l0 : l0 + p] + tn(gi, nrm[:, o : o + p])
            gn[:, o : o + p] = nn(gi, mix[group][l])
            r0 = rows.patch[group]
            acc[r0 : r0 + 1, :p] = acc[r0 : r0 + 1, :p] + pbias[:, o : o + p]

        def pass_down(r):
            n = gn[r, :]
            put(r, 0, n * state[r, :].astype(F32))
            put(r, 1, n)
            dy[r, :] = dy[r, :] + a(r) * n

        over_rows(D, pass_down)
        acc[rows.vec : rows.vec + 8, :] = acc[rows.vec : rows.vec + 8, :] + jnp.transpose(gcol[...])[:8]
        for t in range(F // D):
            r0 = rows.bias_in + t
            acc[r0 : r0 + 1, :] = acc[r0 : r0 + 1, :] + gb1[0:1, t * D : (t + 1) * D]
        if final:
            half = rows.total // 2
            stages[l] = acc[pl.ds(pl.multiple_of((1 - core) * half, 16), half), :].astype(BF)
            copies.start((l, "send"), stages.at[l], sums_h[l][0])
            copies.start((l, "keep"), acc.at[pl.ds(pl.multiple_of(core * half, 16), half)], sums_h[l][1])
        else:
            copies.start((l, "sums"), acc, sums_h[l][0])

    for s in range(k):
        at = pl.ds(pl.multiple_of(lax.rem(me + s, k) * c, 16), c)
        outs[s][...] = dy[at, : piece.width].astype(BF)
    copies.wait_all()


def backward(piece, k, patches, rows, me, incoming, kept, w1, w2, mixes, vectors, accs, final):
    L, D, F = w1.shape
    W = piece.work
    first = accs is None
    vmem = pl.BlockSpec(memory_space=pltpu.VMEM)
    smem = pl.BlockSpec(memory_space=pltpu.SMEM)
    hbm = pl.BlockSpec(memory_space=pl.ANY)
    args = [me, *incoming, *kept, w1, w2, *[mixes[g] for g in piece.groups], *vectors]
    specs = [smem] + [vmem] * k + [hbm] * (len(kept) + 2) + [vmem] * (len(piece.groups) + len(vectors))
    if not first:
        args += accs
        specs += [hbm] * L
    out_shape = [jax.ShapeDtypeStruct((D // k, piece.width), BF)] * k
    half = rows.total // 2
    if final:
        out_shape += [jax.ShapeDtypeStruct((half, D), BF), jax.ShapeDtypeStruct((half, D), F32)] * L
    else:
        out_shape += [jax.ShapeDtypeStruct((rows.total, D), F32)] * L
    scratch = [pltpu.VMEM(*v) for l in range(L) for v in with_ones(kept_shapes(l, D, F, W), D, W).values()]
    scratch += [
        pltpu.VMEM((D, W), F32),
        pltpu.VMEM((D, W), BF),
        pltpu.VMEM((D, W), BF),
        pltpu.VMEM((D, W), F32),
        pltpu.VMEM((L, D, F), BF),
        pltpu.VMEM((L, F, D), BF),
        pltpu.VMEM((L, rows.total, D), F32),
        pltpu.VMEM((L, half, D) if final else (8, 128), BF),
        pltpu.VMEM((8, F), F32),
        pltpu.VMEM((D, 128), F32),
        pltpu.VMEM((8, W), F32),
        pltpu.VMEM((128, D), F32),
        pltpu.VMEM((L, D, 128), F32),
        pltpu.SemaphoreType.DMA((13 * L,)),
    ]
    out = pl.pallas_call(
        functools.partial(backward_kernel, piece, k, patches, rows, L, first, final),
        out_shape=out_shape,
        in_specs=specs,
        out_specs=[vmem] * k + [hbm] * (len(out_shape) - k),
        scratch_shapes=scratch,
        compiler_params=pltpu.CompilerParams(vmem_limit_bytes=VMEM_LIMIT),
        name="backward",
    )(*args)
    sums = out[k:]
    n = 2 if final else 1
    return out[:k], [sums[l * n : (l + 1) * n] for l in range(L)]


def after(value, *events):
    return lax.optimization_barrier((value, events))[0]


def flip(v, bit, n):
    return lax.ppermute(v, "dp", [(i, i ^ bit) for i in range(n)])


def cycle(v, s, k):
    return lax.ppermute(v, "swap", [(i, (i + s) % k) for i in range(k)])


def spread(bufs, distances=None):
    return [cycle(bufs[s], s, len(bufs)) if s else bufs[0] for s in distances or range(len(bufs))]


def local(body, pos, ins, shapes, name):
    vmem = pl.BlockSpec(memory_space=pltpu.VMEM)
    return pl.pallas_call(
        body,
        out_shape=[jax.ShapeDtypeStruct(*shape) for shape in shapes],
        in_specs=[pl.BlockSpec(memory_space=pltpu.SMEM)] + [vmem] * len(ins),
        out_specs=[vmem] * len(shapes),
        compiler_params=pltpu.CompilerParams(vmem_limit_bytes=40 << 20),
        name=name,
    )(pos, *ins)


def side(pos_ref, bit):
    return lax.rem(lax.div(pos_ref[1], bit), 2)


def split_first(pos, keep, came, bits):
    n, r, d = keep.shape
    q = n // 4

    def body(pos_ref, keep_ref, came_ref, *outs):
        for h in range(2):
            mine = side(pos_ref, bits[h])
            at = pl.ds(2 * q * h + mine * q, q)
            outs[2 * h][...] = keep_ref[at] + came_ref[at].astype(F32)
            at = pl.ds(2 * q * h + (1 - mine) * q, q)
            outs[2 * h + 1][...] = (keep_ref[at] + came_ref[at].astype(F32)).astype(BF)

    out = local(body, pos, [keep, came], [((q, r, d), F32), ((q, r, d), BF)] * 2, "split")
    return [(out[0], out[1]), (out[2], out[3])]


def split_next(pos, keeps, cames, bits):
    n, r, d = keeps[0].shape
    q = n // 2

    def body(pos_ref, k0, k1, c0, c1, *outs):
        for h, (keep_ref, came_ref) in enumerate(((k0, c0), (k1, c1))):
            mine = side(pos_ref, bits[h])
            at = pl.ds(mine * q, q)
            outs[2 * h][...] = keep_ref[at] + came_ref[at].astype(F32)
            at = pl.ds((1 - mine) * q, q)
            outs[2 * h + 1][...] = (keep_ref[at] + came_ref[at].astype(F32)).astype(BF)

    out = local(body, pos, [*keeps, *cames], [((q, r, d), F32), ((q, r, d), BF)] * 2, "split")
    return [(out[0], out[1]), (out[2], out[3])]


def split_swap(pos, keeps, cames, k):
    n, r, d = keeps[0].shape

    def body(pos_ref, k0, k1, c0, c1, *refs):
        outs, both = refs[:k], refs[k]
        both[:n] = k0[...] + c0[...].astype(F32)
        both[n:] = k1[...] + c1[...].astype(F32)
        me = pos_ref[0]
        outs[0][...] = both[me]
        for s in range(1, k):
            outs[s][...] = both[lax.rem(me + s, k)].astype(BF)

    vmem = pl.BlockSpec(memory_space=pltpu.VMEM)
    return pl.pallas_call(
        body,
        out_shape=[jax.ShapeDtypeStruct((r, d), F32)] + [jax.ShapeDtypeStruct((r, d), BF)] * (k - 1),
        in_specs=[pl.BlockSpec(memory_space=pltpu.SMEM)] + [vmem] * 4,
        out_specs=[vmem] * k,
        scratch_shapes=[pltpu.VMEM((2 * n, r, d), F32)],
        name="split_swap",
    )(pos, *keeps, *cames)


def add_swap(pos, keep, cames):
    def body(pos_ref, keep_ref, *refs):
        total = keep_ref[...]
        for came in refs[:-1]:
            total = total + came[...].astype(F32)
        refs[-1][...] = total.astype(BF)

    return local(body, pos, [keep, *cames], [(keep.shape, BF)], "add_swap")[0]


def join_swap(pos, parts, k):
    r, d = parts[0].shape
    n = k // 2

    def body(pos_ref, *refs):
        ins, (o0, o1), both = refs[:k], refs[k : k + 2], refs[k + 2]
        for s in range(k):
            both[lax.rem(pos_ref[0] - s + k, k)] = ins[s][...]
        o0[...] = both[:n]
        o1[...] = both[n:]

    vmem = pl.BlockSpec(memory_space=pltpu.VMEM)
    return pl.pallas_call(
        body,
        out_shape=[jax.ShapeDtypeStruct((n, r, d), BF)] * 2,
        in_specs=[pl.BlockSpec(memory_space=pltpu.SMEM)] + [vmem] * k,
        out_specs=[vmem] * 2,
        scratch_shapes=[pltpu.VMEM((k, r, d), BF)],
        name="join_swap",
    )(pos, *parts)


def join(pos, owns, cames, bits, whole):
    q, r, d = owns[0].shape

    def body(pos_ref, v0, v1, c0, c1, *outs):
        for h, (own, came) in enumerate(((v0, c0), (v1, c1))):
            mine = side(pos_ref, bits[h])
            out, base = (outs[0], 2 * q * h) if whole else (outs[h], 0)
            out[pl.ds(base + mine * q, q)] = own[...]
            out[pl.ds(base + (1 - mine) * q, q)] = came[...]

    shapes = [((4 * q, r, d), BF)] if whole else [((2 * q, r, d), BF)] * 2
    return local(body, pos, [*owns, *cames], shapes, "join")


def finish(pos, rows, ff, layer, layers, patches, mine, other, before):
    r, d = rows.total, mine.shape[-1]
    half = r // 2
    nm = rows.used - rows.misc
    last = layer == 0
    big = [(layers, d, ff), (layers, ff, d)]
    small = [(layers, d)] * 7 + [(layers, ff)] + [(layers, p) for p in patches] + [(p, layers, p) for p in patches]
    kept = before[:2]
    miscs = before[2:]

    def body(pos_ref, a_ref, b_ref, *refs):
        refs = refs[len(kept) :]
        misc_refs, refs = refs[: len(miscs)], refs[len(miscs) :]
        outs, rest, (full, win, sem) = refs[:2], refs[2:-3], refs[-3:]
        core = lax.rem(pos_ref[1], 2)
        full[pl.ds(pl.multiple_of(core * half, 16), half), :] = a_ref[...].astype(F32)
        full[pl.ds(pl.multiple_of((1 - core) * half, 16), half), :] = b_ref[...].astype(F32)
        copies = [pltpu.make_async_copy(full.at[pl.ds(rows.out, ff)], outs[1].at[layer], sem.at[1])]
        copies[0].start()
        for t in range(ff // d):
            win[:, t * d : (t + 1) * d] = full[t * d : (t + 1) * d, :]
        copies.append(pltpu.make_async_copy(win, outs[0].at[layer], sem.at[0]))
        copies[1].start()
        if last:
            sources = [(layers - 1 - i, ref, 0) for i, ref in enumerate(misc_refs)] + [(0, full, rows.misc)]
            for l, ref, base in sources:
                for j in range(7):
                    at = rows.vec - rows.misc + base + j
                    rest[j][l : l + 1, :] = ref[at : at + 1, :]
                for t in range(ff // d):
                    at = rows.bias_in - rows.misc + base + t
                    rest[7][l : l + 1, t * d : (t + 1) * d] = ref[at : at + 1, :]
                for g, p in enumerate(patches):
                    at = rows.patch[g] - rows.misc + base
                    rest[8 + g][l : l + 1, :] = ref[at : at + 1, :p]
                    at, l0 = rows.mix[g][0] - rows.misc + base, rows.mix[g][1]
                    rest[11 + g][:, l, :] = ref[at : at + p, l0 : l0 + p]
        else:
            rest[0][...] = full[rows.misc : rows.used, :]
        for cp in copies:
            cp.wait()

    vmem = pl.BlockSpec(memory_space=pltpu.VMEM)
    hbm = pl.BlockSpec(memory_space=pl.ANY)
    shapes = big + (small if last else [(nm, d)])
    out = pl.pallas_call(
        body,
        out_shape=[jax.ShapeDtypeStruct(shape, F32) for shape in shapes],
        in_specs=[pl.BlockSpec(memory_space=pltpu.SMEM), vmem, vmem] + [hbm] * len(kept) + [vmem] * len(miscs),
        out_specs=[hbm] * 2 + [vmem] * (len(shapes) - 2),
        scratch_shapes=[pltpu.VMEM((r, d), F32), pltpu.VMEM((d, ff), F32), pltpu.SemaphoreType.DMA((2,))],
        input_output_aliases={3 + i: i for i in range(len(kept))},
        compiler_params=pltpu.CompilerParams(vmem_limit_bytes=40 << 20),
        name="finish",
    )(pos, mine, other, *kept, *miscs)
    return out if last else [*out[:2], *miscs, out[2]]


def orders(n):
    bits = [1 << i for i in range(1, n.bit_length() - 1)]
    return list(zip(bits, bits[::-1]))


class Chain:
    def __init__(self, pos, rows, n, k):
        self.pos, self.rows, self.n, self.k = pos, rows, n, k
        self.steps = orders(n)

    def begin(self, send, keep):
        view = (self.rows.blocks // 2, self.rows.block, send.shape[-1])
        self.keep, self.came = keep.reshape(view), flip(send, 1, self.n).reshape(view)

    def ready(self, *events):
        self.came = after(self.came, events)

    def split(self, t):
        if t == 0:
            halves = split_first(self.pos, self.keep, self.came, self.steps[0])
        else:
            halves = split_next(self.pos, self.keep, self.came, self.steps[t])
        self.keep = [h[0] for h in halves]
        self.came = [flip(h[1], bit, self.n) for h, bit in zip(halves, self.steps[t])]
        return halves

    def split_swap(self):
        parts = split_swap(self.pos, self.keep, self.came, self.k)
        self.keep, self.came = parts[0], [cycle(parts[s], s, self.k) for s in range(1, self.k)]
        return parts

    def add_swap(self):
        self.keep = add_swap(self.pos, self.keep, self.came)
        self.came = [cycle(self.keep, s, self.k) for s in range(1, self.k)]
        return self.keep

    def join_swap(self):
        self.keep = join_swap(self.pos, [self.keep, *self.came], self.k)
        self.came = [flip(v, bit, self.n) for v, bit in zip(self.keep, self.steps[-1])]
        return self.keep

    def join(self, t):
        self.keep = join(self.pos, self.keep, self.came, self.steps[t], t == 0)
        if t > 0:
            self.came = [flip(v, bit, self.n) for v, bit in zip(self.keep, self.steps[t - 1])]
        else:
            self.keep = self.keep[0].reshape(-1, self.keep[0].shape[-1])
            self.came = flip(self.keep, 1, self.n)
        return self.keep


def on_device(
    n_dp,
    k,
    source_tiles_smallest,
    source_tiles_moderate,
    source_tiles_largest,
    target_cotangent_smallest,
    target_cotangent_moderate,
    target_cotangent_largest,
    surviving_tallies,
    token_affine_factor,
    token_affine_addend,
    crosstile_matrix_smallest,
    crosstile_matrix_moderate,
    crosstile_matrix_largest,
    crosstile_addend_smallest,
    crosstile_addend_moderate,
    crosstile_addend_largest,
    token_blend_factor,
    feedforward_affine_factor,
    feedforward_affine_addend,
    widening_matrix,
    widening_addend,
    narrowing_matrix,
    narrowing_addend,
    feedforward_factor,
):
    L, D, F = widening_matrix.shape
    tensors = [source_tiles_smallest, source_tiles_moderate, source_tiles_largest]
    cotans = [target_cotangent_smallest, target_cotangent_moderate, target_cotangent_largest]
    mixes = [crosstile_matrix_smallest, crosstile_matrix_moderate, crosstile_matrix_largest]
    biases = [crosstile_addend_smallest, crosstile_addend_moderate, crosstile_addend_largest]
    patches = [t.shape[0] for t in tensors]
    images = [t.shape[1] for t in tensors]
    own = [count // k for count in images]
    idx = lax.axis_index("dp")
    pos = lax.axis_index("swap")
    me = jnp.stack([pos, idx]).astype(jnp.int32)
    live = surviving_tallies[0]

    pieces = [
        Piece([(1, i) for i in range(own[1])] + [(0, 0)], patches),
        Piece([(2, i) for i in range(own[2])] + [(0, i) for i in range(1, own[0])], patches),
    ]
    rows = Rows(F, D, patches, n_dp * k)

    tensors = [jnp.transpose(t, (1, 2, 0)) for t in tensors]
    cotans = [jnp.transpose(t, (1, 2, 0)) for t in cotans]
    vectors = [
        token_affine_factor,
        token_affine_addend,
        token_blend_factor,
        feedforward_affine_factor,
        feedforward_affine_addend,
        feedforward_factor,
        narrowing_addend,
    ]
    w1, w2 = widening_matrix, narrowing_matrix

    first, second = pieces
    mixes = [with_layout_constraint(m, Layout((0, 1, 2))) for m in mixes]
    x_bufs = [pack(piece, k, patches, me, live, tensors, False) for piece in pieces]
    c_bufs = [pack(piece, k, patches, me, live, cotans, True) for piece in pieces]
    far = [k // 2]
    near = [s for s in range(1, k) if s != k // 2]

    x_first = after(spread(x_bufs[0]), (mixes, x_bufs[1], c_bufs))
    x_second = spread(after(x_bufs[1], x_first))
    out_first, kept_first = forward(first, k, patches, me, x_first, w1, w2, mixes, biases, vectors, widening_addend)
    x_second = after(x_second, out_first)
    c_first = spread(after(c_bufs[0], x_second))
    out_second, kept_second = forward(second, k, patches, me, x_second, w1, w2, mixes, biases, vectors, widening_addend)
    c_first = after(c_first, out_second)
    c_second = spread(after(c_bufs[1], c_first))
    came = {0: out_first[0]}
    came.update(zip(near, spread(after(out_first, c_first), near)))
    grad_first, sums = backward(first, k, patches, rows, me, c_first, kept_first, w1, w2, mixes, vectors, None, False)
    accs = [v[0] for v in sums]
    c_second, came = after((c_second, came), grad_first)
    came.update(zip(far, spread(after(out_first, c_second), far)))
    out_first = [came[s] for s in range(k)]
    out_second = spread(after(out_second, c_second))
    grad_second, halves = backward(second, k, patches, rows, me, c_second, kept_second, w1, w2, mixes, vectors, accs, True)
    out_first, out_second = after((out_first, out_second), grad_second)

    halves, grad_first = after((halves, grad_first), (out_first, out_second))
    came = {0: grad_first[0]}
    came.update(zip(near + far, spread(grad_first, near + far)))
    grad_first = [came[s] for s in range(k)]
    order = list(reversed(range(L)))
    chains = [Chain(me, rows, n_dp, k) for _ in order]
    for chain, l in zip(chains, order):
        chain.begin(*halves[l])
    token = ()

    def turn(step, *events):
        nonlocal token
        for i, chain in enumerate(chains):
            chain.ready(token, events[i] if i < len(events) else ())
            token = step(chain)

    outs = [None] * 6

    def arrange(base, used, groups, bufs, masked):
        chosen = [pieces[i] for i in used]
        got = unpack(chosen, groups, k, patches, images, me, live, [bufs[i] for i in used], masked)
        for i, g in enumerate(groups):
            outs[base + g] = got[i]
        return got

    count = len(orders(n_dp))
    for t in range(count):
        turn(lambda chain: chain.split(t), [came[s] for s in near] if t == 1 else ())
    turn(lambda chain: chain.split_swap(), grad_first)
    turn(lambda chain: chain.add_swap(), (), arrange(0, (0,), (1,), (after(out_first, token),), True))
    came = {0: grad_second[0]}
    came.update(zip(near, spread(after(grad_second, token), near)))
    turn(lambda chain: chain.join_swap(), arrange(0, (0, 1), (0, 2), (after(out_first, token), out_second), True))
    came.update(zip(far, spread(after(grad_second, token), far)))
    grad_second = [came[s] for s in range(k)]
    for t in reversed(range(count)):
        first_events = [came[s] for s in near] if t == count - 1 else ()
        last_events = [came[s] for s in far] if t == 0 else ()
        if t == 0:
            first_events = arrange(3, (0,), (1,), (after(grad_first, token),), False)
        turn(lambda chain: chain.join(t), first_events, last_events)
    sums = []
    for chain, l in zip(chains, order):
        if l == 0:
            chain.ready(arrange(3, (0, 1), (0, 2), (grad_first, after(grad_second, token)), False), sums)
        sums = finish(me, rows, F, l, L, patches, chain.keep, chain.came, sums)
    outs = [jnp.transpose(v, (2, 0, 1)) for v in outs]
    grad_in, grad_out, *small = sums
    vec, bias_in, patch_bias, mix_of = small[:7], small[7], small[8:11], small[11:]
    mix_of = [jnp.transpose(v, (1, 0, 2)) for v in mix_of]

    return (
        *outs,
        vec[0],
        vec[1],
        *mix_of,
        *patch_bias,
        vec[2],
        vec[3],
        vec[4],
        grad_in,
        bias_in,
        grad_out,
        vec[6],
        vec[5],
    )


def solution(mesh):
    tokens = P(None, "dp", "swap")
    in_specs = (tokens,) * 6 + (P("dp", None),) + (P(),) * 16
    out_specs = (tokens,) * 6 + (P(),) * 16
    return jax.shard_map(
        functools.partial(on_device, mesh.shape["dp"], mesh.shape["swap"]),
        mesh=mesh,
        in_specs=in_specs,
        out_specs=out_specs,
        check_vma=False,
    )
```

```python
import functools

import jax
import jax.numpy as jnp
from jax import lax
from jax.experimental import pallas as pl
from jax.experimental.layout import Layout, with_layout_constraint
from jax.experimental.pallas import tpu as pltpu
from jax.sharding import PartitionSpec as P

BF = jnp.bfloat16
F32 = jnp.float32
FFC = 256
ROWS = 384
VMEM_LIMIT = 64 << 20


def round_up(value, unit):
    return -(-value // unit) * unit


def nt(a, b):
    return lax.dot_general(a, b, (((1,), (1,)), ((), ())), preferred_element_type=F32)


def tn(a, b):
    return lax.dot_general(a, b, (((0,), (0,)), ((), ())), preferred_element_type=F32)


def nn(a, b):
    return jnp.dot(a, b, preferred_element_type=F32)


class Piece:
    def __init__(self, members, patches):
        self.members = []
        offset = 0
        for group, index in members:
            self.members.append((group, index, offset))
            offset += patches[group]
        self.total = offset
        self.width = round_up(offset, 128)
        self.work = round_up(offset, 128)
        self.groups = sorted({group for group, _ in members})


def pack_kernel(piece, k, patches, masked, me_ref, live_ref, *refs):
    ng = len(piece.groups)
    xs = dict(zip(piece.groups, refs[:ng]))
    outs = refs[ng:]
    me = me_ref[0]
    for s in range(k):
        owner = lax.rem(me + s, k)
        out = outs[s]
        for group, index, offset in piece.members:
            p = patches[group]
            image = owner + k * index
            v = xs[group][image]
            if masked:
                v = (v.astype(F32) * (image < live_ref[group]).astype(F32)).astype(BF)
            out[:, offset : offset + p] = v
        if piece.width > piece.total:
            out[:, piece.total :] = jnp.zeros((out.shape[0], piece.width - piece.total), BF)


def pack(piece, k, patches, me, live, tensors, masked):
    c = tensors[0].shape[1]
    vmem = pl.BlockSpec(memory_space=pltpu.VMEM)
    smem = pl.BlockSpec(memory_space=pltpu.SMEM)
    return pl.pallas_call(
        functools.partial(pack_kernel, piece, k, patches, masked),
        out_shape=[jax.ShapeDtypeStruct((c, piece.width), BF)] * k,
        in_specs=[smem, smem] + [vmem] * len(piece.groups),
        out_specs=[vmem] * k,
        compiler_params=pltpu.CompilerParams(vmem_limit_bytes=32 << 20),
        name="pack",
    )(me, live, *[tensors[g] for g in piece.groups])


def unpack_kernel(pieces, groups, k, patches, masked, me_ref, live_ref, *refs):
    buffers = [refs[i * k : (i + 1) * k] for i in range(len(pieces))]
    outs = refs[len(pieces) * k :]
    me = me_ref[0]
    for piece, bufs in zip(pieces, buffers):
        for s in range(k):
            owner = lax.rem(me - s + k, k)
            for group, index, offset in piece.members:
                if group not in groups:
                    continue
                p = patches[group]
                image = owner + k * index
                v = bufs[s][:, offset : offset + p].astype(F32)
                if masked:
                    v = v * (image < live_ref[group]).astype(F32)
                outs[groups.index(group)][image] = v


def unpack(pieces, groups, k, patches, images, me, live, buffers, masked):
    c = buffers[0][0].shape[0]
    vmem = pl.BlockSpec(memory_space=pltpu.VMEM)
    smem = pl.BlockSpec(memory_space=pltpu.SMEM)
    return pl.pallas_call(
        functools.partial(unpack_kernel, pieces, groups, k, patches, masked),
        out_shape=[jax.ShapeDtypeStruct((images[g], c, patches[g]), F32) for g in groups],
        in_specs=[smem, smem] + [vmem] * (k * len(pieces)),
        out_specs=[vmem] * len(groups),
        compiler_params=pltpu.CompilerParams(vmem_limit_bytes=32 << 20),
        name="unpack",
    )(me, live, *[b for bufs in buffers for b in bufs])


class Rows:
    def __init__(self, ff, width, patches, blocks):
        self.out = ff
        base = 2 * ff
        self.mix = [
            (base + round_up(patches[2], 8), round_up(patches[1], 128)),
            (base + round_up(patches[2], 8), 0),
            (base, 0),
        ]
        self.misc = base
        base += round_up(patches[2], 8) + round_up(patches[1], 8)
        self.bias_in = base
        self.patch = [base + ff // width + g for g in range(3)]
        self.vec = round_up(base + ff // width + 3, 8)
        self.used = self.vec + 8
        self.blocks = blocks
        self.block = round_up(-(-self.used // blocks), 8)
        self.total = blocks * self.block


def over_rows(count, body):
    def step(i, carry):
        body(pl.ds(pl.multiple_of(i * ROWS, ROWS), ROWS))
        return carry

    lax.fori_loop(0, count // ROWS, step, 0)


def channel(cols, layer, j):
    return lambda r: cols[layer, r, j : j + 1]


class Copies:
    def __init__(self, sem):
        self.sem, self.count = sem, 0
        self.started = {}

    def start(self, key, src, dst):
        cp = pltpu.make_async_copy(src, dst, self.sem.at[self.count])
        self.count += 1
        cp.start()
        self.started[key] = cp

    def wait(self, *keys):
        for key in keys:
            self.started.pop(key).wait()

    def wait_all(self):
        self.wait(*list(self.started))


KEPT = ("state", "mixs", "nrm", "sc", "brs", "act", "dact")


def kept_shapes(layer, D, F, W):
    return {
        "state": ((D, W), BF if layer == 0 else F32),
        "mixs": ((D, W), F32),
        "nrm": ((D, W), BF),
        "sc": ((D, W), BF),
        "brs": ((D, W), BF),
        "act": ((F, W), BF),
        "dact": ((F, W), BF),
    }


def load_columns(refs, line, cols, layers):
    line[...] = jnp.zeros(line.shape, F32)
    for l in range(layers):
        for j, ref in enumerate(refs):
            line[j : j + 1, :] = ref[l : l + 1, :]
        cols[l] = jnp.transpose(line[...])


def forward_kernel(piece, k, patches, layers, *refs):
    refs = list(refs)

    def take(n):
        out, refs[:] = refs[:n], refs[n:]
        return out

    (me_ref,) = take(1)
    ins = take(k)
    w1_h, w2_h = take(2)
    mix = dict(zip(piece.groups, take(len(piece.groups))))
    bias = dict(zip(piece.groups, take(len(piece.groups))))
    vectors = take(7)
    (b1_ref,) = take(1)
    outs = take(k)
    kept_h = [dict(zip(KEPT, take(len(KEPT)))) for _ in range(layers)]
    kept = [dict(zip(KEPT, take(len(KEPT)))) for _ in range(layers)]
    last, w1, w2, line, cols, sem = refs
    D, W = last.shape
    F = w2.shape[1]
    c = D // k
    me = me_ref[0]
    copies = Copies(sem)
    for l in range(layers):
        copies.start((l, "w1"), w1_h.at[l], w1.at[l, pl.ds(0, D)])
        copies.start((l, "w2"), w2_h.at[l], w2.at[l])

    def keep(l, name):
        copies.start((l, name), kept[l][name].at[pl.ds(0, D)], kept_h[l][name])

    x0 = kept[0]["state"]
    for s in range(k):
        at = pl.ds(pl.multiple_of(lax.rem(me - s + k, k) * c, 16), c)
        x0[at, : piece.width] = ins[s][...]
    if W > piece.width:
        x0[:, piece.width :] = jnp.zeros((D, W - piece.width), BF)
    keep(0, "state")
    load_columns(vectors, line, cols, layers)

    for l in range(layers):
        a, b, g, f, h, ff, b2 = [channel(cols, l, j) for j in range(7)]
        state, mixs, nrm, sc, brs, act, dact = [kept[l][name] for name in KEPT]
        nxt = kept[l + 1]["state"] if l + 1 < layers else last
        if W > piece.total:
            mixs[:, piece.total :] = jnp.zeros((D, W - piece.total), F32)

        def normalise(r):
            nrm[r, :] = (state[r, :].astype(F32) * a(r) + b(r)).astype(BF)

        over_rows(D, normalise)
        keep(l, "nrm")
        for group, _, o in piece.members:
            p = patches[group]
            mixs[:, o : o + p] = nt(nrm[:, o : o + p], mix[group][l]) + bias[group][l : l + 1, :]

        def blend(r):
            middle = state[r, :].astype(F32) + g(r) * mixs[r, :]
            nxt[r, :] = middle
            sc[r, :] = (middle * f(r) + h(r)).astype(BF)

        over_rows(D, blend)
        keep(l, "mixs")
        keep(l, "sc")
        sc[D:, :] = jnp.ones((sc.shape[0] - D, W), BF)
        rest = b1_ref[l : l + 1, :]
        parts = []
        for _ in range(3):
            parts.append(rest.astype(BF).astype(F32))
            rest = rest - parts[-1]
        parts.append(jnp.zeros((w1.shape[1] - D - 3, F), F32))
        w1[l, D:, :] = jnp.concatenate(parts, 0).astype(BF)
        copies.wait((l, "w1"), (l, "w2"))
        s = sc[...]
        for i in range(F // FFC):
            fr = pl.ds(i * FFC, FFC)
            v = tn(w1[l, :, fr], s)
            v2 = v * v
            t = jnp.tanh(v * (0.7978845608 + (0.7978845608 * 0.044715) * v2))
            hp = 0.5 * t + 0.5
            ac = v * hp
            q = 2 * 0.7978845608 + (6 * 0.7978845608 * 0.044715) * v2
            act[fr, :] = ac.astype(BF)
            dact[fr, :] = (hp + (ac - ac * hp) * q).astype(BF)
            for name in ("act", "dact"):
                copies.start((l, name, i), kept[l][name].at[fr], kept_h[l][name].at[fr])
        br = (tn(w2[l], act[...]) + cols[l, :, 6:7]).astype(BF)
        brs[...] = br
        nxt[...] = nxt[...] + cols[l, :, 5:6] * br.astype(F32)
        keep(l, "brs")
        if l + 1 < layers:
            keep(l + 1, "state")

    for s in range(k):
        at = pl.ds(pl.multiple_of(lax.rem(me + s, k) * c, 16), c)
        outs[s][...] = last[at, : piece.width].astype(BF)
    copies.wait_all()


def with_ones(shapes, D, W):
    return {**shapes, "sc": ((D + 16, W), BF)}


def forward(piece, k, patches, me, bufs, w1, w2, mixes, biases, vectors, b1):
    L, D, F = w1.shape
    W = piece.work
    vmem = pl.BlockSpec(memory_space=pltpu.VMEM)
    smem = pl.BlockSpec(memory_space=pltpu.SMEM)
    hbm = pl.BlockSpec(memory_space=pl.ANY)
    args = [me, *bufs, w1, w2, *[mixes[g] for g in piece.groups], *[biases[g] for g in piece.groups], *vectors, b1]
    specs = [smem] + [vmem] * k + [hbm] * 2 + [vmem] * (2 * len(piece.groups) + len(vectors) + 1)
    c = bufs[0].shape[0]
    kept = [shape for l in range(L) for shape in kept_shapes(l, D, F, W).values()]
    scratch = [pltpu.VMEM(*v) for l in range(L) for v in with_ones(kept_shapes(l, D, F, W), D, W).values()]
    scratch += [
        pltpu.VMEM((D, W), F32),
        pltpu.VMEM((L, D + 16, F), BF),
        pltpu.VMEM((L, F, D), BF),
        pltpu.VMEM((128, D), F32),
        pltpu.VMEM((L, D, 128), F32),
        pltpu.SemaphoreType.DMA((L * (7 + 2 * (F // FFC)),)),
    ]
    out = pl.pallas_call(
        functools.partial(forward_kernel, piece, k, patches, L),
        out_shape=[jax.ShapeDtypeStruct((c, piece.width), BF)] * k + [jax.ShapeDtypeStruct(*v) for v in kept],
        in_specs=specs,
        out_specs=[vmem] * k + [hbm] * len(kept),
        scratch_shapes=scratch,
        compiler_params=pltpu.CompilerParams(vmem_limit_bytes=VMEM_LIMIT),
        name="forward",
    )(*args)
    n = len(KEPT)
    return out[:k], out[k:]


def backward_kernel(piece, k, patches, rows, layers, first, final, *refs):
    refs = list(refs)

    def take(n):
        out, refs[:] = refs[:n], refs[n:]
        return out

    (me_ref,) = take(1)
    ins = take(k)
    kept_h = [dict(zip(KEPT, take(len(KEPT)))) for _ in range(layers)]
    w1_h, w2_h = take(2)
    mix = dict(zip(piece.groups, take(len(piece.groups))))
    vectors = take(7)
    accs_h = [] if first else take(layers)
    outs = take(k)
    sums_h = [take(2 if final else 1) for _ in range(layers)]
    kept = [dict(zip(KEPT, take(len(KEPT)))) for _ in range(layers)]
    gn, gb, gs, dy, w1s, w2s, accs, stages, gb1, gcol, gpb, line, cols, sem = refs
    D, W = gn.shape
    F = w2s.shape[1]
    c = D // k
    me = me_ref[0]
    core = lax.rem(me_ref[1], 2)
    copies = Copies(sem)
    half_f = F // 2
    for l in reversed(range(layers)):
        copies.start((l, "brs"), kept_h[l]["brs"], kept[l]["brs"])
        copies.start((l, "w2"), w2_h.at[l], w2s.at[l])
        for i in range(2):
            at = pl.ds(i * half_f, half_f)
            copies.start((l, "dact", i), kept_h[l]["dact"].at[at], kept[l]["dact"].at[at])
        copies.start((l, "w1"), w1_h.at[l], w1s.at[l])
        copies.start((l, "sc"), kept_h[l]["sc"], kept[l]["sc"].at[pl.ds(0, D)])
        if not first:
            copies.start((l, "acc"), accs_h[l], accs.at[l])
        for name in ("act", "mixs", "state", "nrm"):
            copies.start((l, name), kept_h[l][name], kept[l][name])

    load_columns(vectors, line, cols, layers)
    for s in range(k):
        at = pl.ds(pl.multiple_of(lax.rem(me - s + k, k) * c, 16), c)
        dy[at, : piece.width] = ins[s][...].astype(F32)
    if W > piece.width:
        dy[:, piece.width :] = jnp.zeros((D, W - piece.width), F32)
    if W > piece.total:
        gn[:, piece.total :] = jnp.zeros((D, W - piece.total), F32)
    gcol[...] = jnp.zeros(gcol.shape, F32)

    def put(r, j, v):
        gcol[r, j : j + 1] = jnp.sum(v, 1, keepdims=True)

    for l in reversed(range(layers)):
        a, b, g, f, h, ff, b2 = [channel(cols, l, j) for j in range(7)]
        state, mixs, nrm, sc, brs, act, dact = [kept[l][name] for name in KEPT]
        acc = accs.at[l]
        w1, w2 = w1s.at[l], w2s.at[l]
        sc[D:, :] = jnp.ones((sc.shape[0] - D, W), BF)
        if first:
            acc[rows.misc :, :] = jnp.zeros((rows.total - rows.misc, D), F32)
        gpb[...] = jnp.zeros(gpb.shape, F32)
        copies.wait((l, "brs"))

        def gain(r):
            d = dy[r, :]
            put(r, 5, d * brs[r, :].astype(F32))
            gbv = (d * ff(r)).astype(BF)
            gb[r, :] = gbv
            put(r, 6, gbv.astype(F32))

        over_rows(D, gain)
        copies.wait((l, "w2"))
        up = gb[...]
        for i in range(F // FFC):
            if i * FFC % half_f == 0:
                copies.wait((l, "dact", i * FFC // half_f))
            fr = pl.ds(i * FFC, FFC)
            dact[fr, :] = (nn(w2[fr, :], up) * dact[fr, :].astype(F32)).astype(BF)
        copies.wait((l, "w1"))
        gs[...] = nn(w1[...], dact[...]).astype(BF)
        copies.wait((l, "sc"))
        if not first:
            copies.wait((l, "acc"))

        def weight_in(n, carry):
            r = nt(sc[...], dact[pl.ds(pl.multiple_of(n * 2 * D, 2 * D), 2 * D), :])
            for i in range(2):
                at = pl.ds(pl.multiple_of((2 * n + i) * D, D), D)
                part = r[:D, i * D : (i + 1) * D]
                acc[at, :] = part if first else acc[at, :] + part
            gb1[:, pl.ds(pl.multiple_of(n * 2 * D, 2 * D), 2 * D)] = r[D : D + 8]
            return carry

        lax.fori_loop(0, F // (2 * D), weight_in, 0)
        copies.wait((l, "act"))

        def weight_out(n, carry):
            r = nt(act[pl.ds(pl.multiple_of(n * 512, 512), 512), :], gb[...])
            at = pl.ds(pl.multiple_of(rows.out + n * 512, 512), 512)
            acc[at, :] = r if first else acc[at, :] + r
            return carry

        lax.fori_loop(0, F // 512, weight_out, 0)
        copies.wait((l, "mixs"), (l, "state"))

        def back(r):
            gsf = gs[r, :].astype(F32)
            mixture = mixs[r, :]
            middle = state[r, :].astype(F32) + g(r) * mixture
            gm = dy[r, :] + f(r) * gsf
            dy[r, :] = gm
            put(r, 3, gsf * middle)
            put(r, 4, gsf)
            put(r, 2, gm * mixture)
            gmb = (g(r) * gm).astype(BF)
            gb[r, :] = gmb
            gpb[...] = gpb[...] + gmb.astype(F32).reshape(ROWS // 8, 8, W).sum(0)

        over_rows(D, back)
        pbias = jnp.sum(gpb[...], 0, keepdims=True)
        copies.wait((l, "nrm"))
        for group, _, o in piece.members:
            p = patches[group]
            gi = gb[:, o : o + p]
            r0, l0 = rows.mix[group]
            acc[r0 : r0 + p, l0 : l0 + p] = acc[r0 : r0 + p, l0 : l0 + p] + tn(gi, nrm[:, o : o + p])
            gn[:, o : o + p] = nn(gi, mix[group][l])
            r0 = rows.patch[group]
            acc[r0 : r0 + 1, :p] = acc[r0 : r0 + 1, :p] + pbias[:, o : o + p]

        def pass_down(r):
            n = gn[r, :]
            put(r, 0, n * state[r, :].astype(F32))
            put(r, 1, n)
            dy[r, :] = dy[r, :] + a(r) * n

        over_rows(D, pass_down)
        acc[rows.vec : rows.vec + 8, :] = acc[rows.vec : rows.vec + 8, :] + jnp.transpose(gcol[...])[:8]
        for t in range(F // D):
            r0 = rows.bias_in + t
            acc[r0 : r0 + 1, :] = acc[r0 : r0 + 1, :] + gb1[0:1, t * D : (t + 1) * D]
        if final:
            half = rows.total // 2
            stages[l] = acc[pl.ds(pl.multiple_of((1 - core) * half, 16), half), :].astype(BF)
            copies.start((l, "send"), stages.at[l], sums_h[l][0])
            copies.start((l, "keep"), acc.at[pl.ds(pl.multiple_of(core * half, 16), half)], sums_h[l][1])
        else:
            copies.start((l, "sums"), acc, sums_h[l][0])

    for s in range(k):
        at = pl.ds(pl.multiple_of(lax.rem(me + s, k) * c, 16), c)
        outs[s][...] = dy[at, : piece.width].astype(BF)
    copies.wait_all()


def backward(piece, k, patches, rows, me, incoming, kept, w1, w2, mixes, vectors, accs, final):
    L, D, F = w1.shape
    W = piece.work
    first = accs is None
    vmem = pl.BlockSpec(memory_space=pltpu.VMEM)
    smem = pl.BlockSpec(memory_space=pltpu.SMEM)
    hbm = pl.BlockSpec(memory_space=pl.ANY)
    args = [me, *incoming, *kept, w1, w2, *[mixes[g] for g in piece.groups], *vectors]
    specs = [smem] + [vmem] * k + [hbm] * (len(kept) + 2) + [vmem] * (len(piece.groups) + len(vectors))
    if not first:
        args += accs
        specs += [hbm] * L
    out_shape = [jax.ShapeDtypeStruct((D // k, piece.width), BF)] * k
    half = rows.total // 2
    if final:
        out_shape += [jax.ShapeDtypeStruct((half, D), BF), jax.ShapeDtypeStruct((half, D), F32)] * L
    else:
        out_shape += [jax.ShapeDtypeStruct((rows.total, D), F32)] * L
    scratch = [pltpu.VMEM(*v) for l in range(L) for v in with_ones(kept_shapes(l, D, F, W), D, W).values()]
    scratch += [
        pltpu.VMEM((D, W), F32),
        pltpu.VMEM((D, W), BF),
        pltpu.VMEM((D, W), BF),
        pltpu.VMEM((D, W), F32),
        pltpu.VMEM((L, D, F), BF),
        pltpu.VMEM((L, F, D), BF),
        pltpu.VMEM((L, rows.total, D), F32),
        pltpu.VMEM((L, half, D) if final else (8, 128), BF),
        pltpu.VMEM((8, F), F32),
        pltpu.VMEM((D, 128), F32),
        pltpu.VMEM((8, W), F32),
        pltpu.VMEM((128, D), F32),
        pltpu.VMEM((L, D, 128), F32),
        pltpu.SemaphoreType.DMA((13 * L,)),
    ]
    out = pl.pallas_call(
        functools.partial(backward_kernel, piece, k, patches, rows, L, first, final),
        out_shape=out_shape,
        in_specs=specs,
        out_specs=[vmem] * k + [hbm] * (len(out_shape) - k),
        scratch_shapes=scratch,
        compiler_params=pltpu.CompilerParams(vmem_limit_bytes=VMEM_LIMIT),
        name="backward",
    )(*args)
    sums = out[k:]
    n = 2 if final else 1
    return out[:k], [sums[l * n : (l + 1) * n] for l in range(L)]


def after(value, *events):
    return lax.optimization_barrier((value, events))[0]


def flip(v, bit, n):
    return lax.ppermute(v, "dp", [(i, i ^ bit) for i in range(n)])


def cycle(v, s, k):
    return lax.ppermute(v, "swap", [(i, (i + s) % k) for i in range(k)])


def spread(bufs, distances=None):
    return [cycle(bufs[s], s, len(bufs)) if s else bufs[0] for s in distances or range(len(bufs))]


def local(body, pos, ins, shapes, name):
    vmem = pl.BlockSpec(memory_space=pltpu.VMEM)
    return pl.pallas_call(
        body,
        out_shape=[jax.ShapeDtypeStruct(*shape) for shape in shapes],
        in_specs=[pl.BlockSpec(memory_space=pltpu.SMEM)] + [vmem] * len(ins),
        out_specs=[vmem] * len(shapes),
        compiler_params=pltpu.CompilerParams(vmem_limit_bytes=40 << 20),
        name=name,
    )(pos, *ins)


def side(pos_ref, bit):
    return lax.rem(lax.div(pos_ref[1], bit), 2)


def split_first(pos, keep, came, bits):
    n, r, d = keep.shape
    q = n // 4

    def body(pos_ref, keep_ref, came_ref, *outs):
        for h in range(2):
            mine = side(pos_ref, bits[h])
            at = pl.ds(2 * q * h + mine * q, q)
            outs[2 * h][...] = keep_ref[at] + came_ref[at].astype(F32)
            at = pl.ds(2 * q * h + (1 - mine) * q, q)
            outs[2 * h + 1][...] = (keep_ref[at] + came_ref[at].astype(F32)).astype(BF)

    out = local(body, pos, [keep, came], [((q, r, d), F32), ((q, r, d), BF)] * 2, "split")
    return [(out[0], out[1]), (out[2], out[3])]


def split_next(pos, keeps, cames, bits):
    n, r, d = keeps[0].shape
    q = n // 2

    def body(pos_ref, k0, k1, c0, c1, *outs):
        for h, (keep_ref, came_ref) in enumerate(((k0, c0), (k1, c1))):
            mine = side(pos_ref, bits[h])
            at = pl.ds(mine * q, q)
            outs[2 * h][...] = keep_ref[at] + came_ref[at].astype(F32)
            at = pl.ds((1 - mine) * q, q)
            outs[2 * h + 1][...] = (keep_ref[at] + came_ref[at].astype(F32)).astype(BF)

    out = local(body, pos, [*keeps, *cames], [((q, r, d), F32), ((q, r, d), BF)] * 2, "split")
    return [(out[0], out[1]), (out[2], out[3])]


def split_swap(pos, keeps, cames, k):
    n, r, d = keeps[0].shape

    def body(pos_ref, k0, k1, c0, c1, *refs):
        outs, both = refs[:k], refs[k]
        both[:n] = k0[...] + c0[...].astype(F32)
        both[n:] = k1[...] + c1[...].astype(F32)
        me = pos_ref[0]
        outs[0][...] = both[me]
        for s in range(1, k):
            outs[s][...] = both[lax.rem(me + s, k)].astype(BF)

    vmem = pl.BlockSpec(memory_space=pltpu.VMEM)
    return pl.pallas_call(
        body,
        out_shape=[jax.ShapeDtypeStruct((r, d), F32)] + [jax.ShapeDtypeStruct((r, d), BF)] * (k - 1),
        in_specs=[pl.BlockSpec(memory_space=pltpu.SMEM)] + [vmem] * 4,
        out_specs=[vmem] * k,
        scratch_shapes=[pltpu.VMEM((2 * n, r, d), F32)],
        name="split_swap",
    )(pos, *keeps, *cames)


def add_swap(pos, keep, cames):
    def body(pos_ref, keep_ref, *refs):
        total = keep_ref[...]
        for came in refs[:-1]:
            total = total + came[...].astype(F32)
        refs[-1][...] = total.astype(BF)

    return local(body, pos, [keep, *cames], [(keep.shape, BF)], "add_swap")[0]


def join_swap(pos, parts, k):
    r, d = parts[0].shape
    n = k // 2

    def body(pos_ref, *refs):
        ins, (o0, o1), both = refs[:k], refs[k : k + 2], refs[k + 2]
        for s in range(k):
            both[lax.rem(pos_ref[0] - s + k, k)] = ins[s][...]
        o0[...] = both[:n]
        o1[...] = both[n:]

    vmem = pl.BlockSpec(memory_space=pltpu.VMEM)
    return pl.pallas_call(
        body,
        out_shape=[jax.ShapeDtypeStruct((n, r, d), BF)] * 2,
        in_specs=[pl.BlockSpec(memory_space=pltpu.SMEM)] + [vmem] * k,
        out_specs=[vmem] * 2,
        scratch_shapes=[pltpu.VMEM((k, r, d), BF)],
        name="join_swap",
    )(pos, *parts)


def join(pos, owns, cames, bits, whole):
    q, r, d = owns[0].shape

    def body(pos_ref, v0, v1, c0, c1, *outs):
        for h, (own, came) in enumerate(((v0, c0), (v1, c1))):
            mine = side(pos_ref, bits[h])
            out, base = (outs[0], 2 * q * h) if whole else (outs[h], 0)
            out[pl.ds(base + mine * q, q)] = own[...]
            out[pl.ds(base + (1 - mine) * q, q)] = came[...]

    shapes = [((4 * q, r, d), BF)] if whole else [((2 * q, r, d), BF)] * 2
    return local(body, pos, [*owns, *cames], shapes, "join")


def finish(pos, rows, ff, layer, layers, patches, mine, other, before):
    r, d = rows.total, mine.shape[-1]
    half = r // 2
    nm = rows.used - rows.misc
    last = layer == 0
    big = [(layers, d, ff), (layers, ff, d)]
    small = [(layers, d)] * 7 + [(layers, ff)] + [(layers, p) for p in patches] + [(p, layers, p) for p in patches]
    kept = before[:2]
    miscs = before[2:]

    def body(pos_ref, a_ref, b_ref, *refs):
        refs = refs[len(kept) :]
        misc_refs, refs = refs[: len(miscs)], refs[len(miscs) :]
        outs, rest, (full, win, sem) = refs[:2], refs[2:-3], refs[-3:]
        core = lax.rem(pos_ref[1], 2)
        full[pl.ds(pl.multiple_of(core * half, 16), half), :] = a_ref[...].astype(F32)
        full[pl.ds(pl.multiple_of((1 - core) * half, 16), half), :] = b_ref[...].astype(F32)
        copies = [pltpu.make_async_copy(full.at[pl.ds(rows.out, ff)], outs[1].at[layer], sem.at[1])]
        copies[0].start()
        for t in range(ff // d):
            win[:, t * d : (t + 1) * d] = full[t * d : (t + 1) * d, :]
        copies.append(pltpu.make_async_copy(win, outs[0].at[layer], sem.at[0]))
        copies[1].start()
        if last:
            sources = [(layers - 1 - i, ref, 0) for i, ref in enumerate(misc_refs)] + [(0, full, rows.misc)]
            for l, ref, base in sources:
                for j in range(7):
                    at = rows.vec - rows.misc + base + j
                    rest[j][l : l + 1, :] = ref[at : at + 1, :]
                for t in range(ff // d):
                    at = rows.bias_in - rows.misc + base + t
                    rest[7][l : l + 1, t * d : (t + 1) * d] = ref[at : at + 1, :]
                for g, p in enumerate(patches):
                    at = rows.patch[g] - rows.misc + base
                    rest[8 + g][l : l + 1, :] = ref[at : at + 1, :p]
                    at, l0 = rows.mix[g][0] - rows.misc + base, rows.mix[g][1]
                    rest[11 + g][:, l, :] = ref[at : at + p, l0 : l0 + p]
        else:
            rest[0][...] = full[rows.misc : rows.used, :]
        for cp in copies:
            cp.wait()

    vmem = pl.BlockSpec(memory_space=pltpu.VMEM)
    hbm = pl.BlockSpec(memory_space=pl.ANY)
    shapes = big + (small if last else [(nm, d)])
    out = pl.pallas_call(
        body,
        out_shape=[jax.ShapeDtypeStruct(shape, F32) for shape in shapes],
        in_specs=[pl.BlockSpec(memory_space=pltpu.SMEM), vmem, vmem] + [hbm] * len(kept) + [vmem] * len(miscs),
        out_specs=[hbm] * 2 + [vmem] * (len(shapes) - 2),
        scratch_shapes=[pltpu.VMEM((r, d), F32), pltpu.VMEM((d, ff), F32), pltpu.SemaphoreType.DMA((2,))],
        input_output_aliases={3 + i: i for i in range(len(kept))},
        compiler_params=pltpu.CompilerParams(vmem_limit_bytes=40 << 20),
        name="finish",
    )(pos, mine, other, *kept, *miscs)
    return out if last else [*out[:2], *miscs, out[2]]


def orders(n):
    bits = [1 << i for i in range(1, n.bit_length() - 1)]
    return list(zip(bits, bits[::-1]))


class Chain:
    def __init__(self, pos, rows, n, k):
        self.pos, self.rows, self.n, self.k = pos, rows, n, k
        self.steps = orders(n)

    def begin(self, send, keep):
        view = (self.rows.blocks // 2, self.rows.block, send.shape[-1])
        self.keep, self.came = keep.reshape(view), flip(send, 1, self.n).reshape(view)

    def ready(self, *events):
        self.came = after(self.came, events)

    def split(self, t):
        if t == 0:
            halves = split_first(self.pos, self.keep, self.came, self.steps[0])
        else:
            halves = split_next(self.pos, self.keep, self.came, self.steps[t])
        self.keep = [h[0] for h in halves]
        self.came = [flip(h[1], bit, self.n) for h, bit in zip(halves, self.steps[t])]
        return halves

    def split_swap(self):
        parts = split_swap(self.pos, self.keep, self.came, self.k)
        self.keep, self.came = parts[0], [cycle(parts[s], s, self.k) for s in range(1, self.k)]
        return parts

    def add_swap(self):
        self.keep = add_swap(self.pos, self.keep, self.came)
        self.came = [cycle(self.keep, s, self.k) for s in range(1, self.k)]
        return self.keep

    def join_swap(self):
        self.keep = join_swap(self.pos, [self.keep, *self.came], self.k)
        self.came = [flip(v, bit, self.n) for v, bit in zip(self.keep, self.steps[-1])]
        return self.keep

    def join(self, t):
        self.keep = join(self.pos, self.keep, self.came, self.steps[t], t == 0)
        if t > 0:
            self.came = [flip(v, bit, self.n) for v, bit in zip(self.keep, self.steps[t - 1])]
        else:
            self.keep = self.keep[0].reshape(-1, self.keep[0].shape[-1])
            self.came = flip(self.keep, 1, self.n)
        return self.keep


def on_device(
    n_dp,
    k,
    source_tiles_smallest,
    source_tiles_moderate,
    source_tiles_largest,
    target_cotangent_smallest,
    target_cotangent_moderate,
    target_cotangent_largest,
    surviving_tallies,
    token_affine_factor,
    token_affine_addend,
    crosstile_matrix_smallest,
    crosstile_matrix_moderate,
    crosstile_matrix_largest,
    crosstile_addend_smallest,
    crosstile_addend_moderate,
    crosstile_addend_largest,
    token_blend_factor,
    feedforward_affine_factor,
    feedforward_affine_addend,
    widening_matrix,
    widening_addend,
    narrowing_matrix,
    narrowing_addend,
    feedforward_factor,
):
    L, D, F = widening_matrix.shape
    tensors = [source_tiles_smallest, source_tiles_moderate, source_tiles_largest]
    cotans = [target_cotangent_smallest, target_cotangent_moderate, target_cotangent_largest]
    mixes = [crosstile_matrix_smallest, crosstile_matrix_moderate, crosstile_matrix_largest]
    biases = [crosstile_addend_smallest, crosstile_addend_moderate, crosstile_addend_largest]
    patches = [t.shape[0] for t in tensors]
    images = [t.shape[1] for t in tensors]
    own = [count // k for count in images]
    idx = lax.axis_index("dp")
    pos = lax.axis_index("swap")
    me = jnp.stack([pos, idx]).astype(jnp.int32)
    live = surviving_tallies[0]

    pieces = [
        Piece([(2, i) for i in range(own[2])] + [(0, i) for i in range(1, own[0])], patches),
        Piece([(1, i) for i in range(own[1])] + [(0, 0)], patches),
    ]
    rows = Rows(F, D, patches, n_dp * k)

    tensors = [jnp.transpose(t, (1, 2, 0)) for t in tensors]
    cotans = [jnp.transpose(t, (1, 2, 0)) for t in cotans]
    vectors = [
        token_affine_factor,
        token_affine_addend,
        token_blend_factor,
        feedforward_affine_factor,
        feedforward_affine_addend,
        feedforward_factor,
        narrowing_addend,
    ]
    w1, w2 = widening_matrix, narrowing_matrix

    first, second = pieces
    mixes = [with_layout_constraint(m, Layout((0, 1, 2))) for m in mixes]
    x_bufs = [pack(piece, k, patches, me, live, tensors, False) for piece in pieces]
    c_bufs = [pack(piece, k, patches, me, live, cotans, True) for piece in pieces]
    far = [k // 2]
    near = [s for s in range(1, k) if s != k // 2]

    x_first = after(spread(x_bufs[0]), (mixes, x_bufs[1], c_bufs))
    x_second = spread(after(x_bufs[1], x_first))
    out_first, kept_first = forward(first, k, patches, me, x_first, w1, w2, mixes, biases, vectors, widening_addend)
    x_second = after(x_second, out_first)
    c_first = spread(after(c_bufs[0], x_second))
    out_second, kept_second = forward(second, k, patches, me, x_second, w1, w2, mixes, biases, vectors, widening_addend)
    c_first = after(c_first, out_second)
    c_second = spread(after(c_bufs[1], c_first))
    came = {0: out_first[0]}
    came.update(zip(near, spread(after(out_first, c_first), near)))
    grad_first, sums = backward(first, k, patches, rows, me, c_first, kept_first, w1, w2, mixes, vectors, None, False)
    accs = [v[0] for v in sums]
    c_second, came = after((c_second, came), grad_first)
    came.update(zip(far, spread(after(out_first, c_second), far)))
    out_first = [came[s] for s in range(k)]
    out_second = spread(after(out_second, c_second))
    grad_second, halves = backward(second, k, patches, rows, me, c_second, kept_second, w1, w2, mixes, vectors, accs, True)
    out_first, out_second = after((out_first, out_second), grad_second)

    halves, grad_first = after((halves, grad_first), (out_first, out_second))
    came = {0: grad_first[0]}
    came.update(zip(near + far, spread(grad_first, near + far)))
    grad_first = [came[s] for s in range(k)]
    order = list(reversed(range(L)))
    chains = [Chain(me, rows, n_dp, k) for _ in order]
    for chain, l in zip(chains, order):
        chain.begin(*halves[l])
    token = ()

    def turn(step, *events):
        nonlocal token
        for i, chain in enumerate(chains):
            then = events[i] if i < len(events) else ()
            chain.ready(token, then() if callable(then) else then)
            token = step(chain)

    outs = [None] * 6
    alone = [g for g in range(3) if g not in second.groups]

    def arrange(base, used, groups, bufs, masked):
        chosen = [pieces[i] for i in used]
        got = unpack(chosen, groups, k, patches, images, me, live, [bufs[i] for i in used], masked)
        for i, g in enumerate(groups):
            outs[base + g] = got[i]
        return got

    count = len(orders(n_dp))
    for t in range(count):
        turn(lambda chain: chain.split(t), [came[s] for s in near] if t == 1 else ())
    turn(lambda chain: chain.split_swap(), grad_first)
    turn(lambda chain: chain.add_swap(), (), lambda: arrange(0, (0,), alone, (after(out_first, token),), True))
    turn(
        lambda chain: chain.join_swap(),
        (),
        lambda: (
            arrange(0, (0, 1), second.groups, (after(out_first, token), out_second), True),
            arrange(3, (0,), alone, (after(grad_first, token),), False),
            chains[0].came,
        ),
    )
    came = {0: grad_second[0]}
    came.update(zip(near + far, spread(after(grad_second, token), near + far)))
    grad_second = [came[s] for s in range(k)]
    for t in reversed(range(count)):
        late = [came[s] for s in (near if t == count - 1 else far if t == 0 else [])]
        turn(lambda chain: chain.join(t), (), late)
    token = arrange(3, (0, 1), second.groups, (grad_first, after(grad_second, token)), False)
    sums = []
    for chain, l in zip(chains, order):
        chain.ready(token, sums)
        sums = finish(me, rows, F, l, L, patches, chain.keep, chain.came, sums)
    outs = [jnp.transpose(v, (2, 0, 1)) for v in outs]
    grad_in, grad_out, *small = sums
    vec, bias_in, patch_bias, mix_of = small[:7], small[7], small[8:11], small[11:]
    mix_of = [jnp.transpose(v, (1, 0, 2)) for v in mix_of]

    return (
        *outs,
        vec[0],
        vec[1],
        *mix_of,
        *patch_bias,
        vec[2],
        vec[3],
        vec[4],
        grad_in,
        bias_in,
        grad_out,
        vec[6],
        vec[5],
    )


def solution(mesh):
    tokens = P(None, "dp", "swap")
    in_specs = (tokens,) * 6 + (P("dp", None),) + (P(),) * 16
    out_specs = (tokens,) * 6 + (P(),) * 16
    return jax.shard_map(
        functools.partial(on_device, mesh.shape["dp"], mesh.shape["swap"]),
        mesh=mesh,
        in_specs=in_specs,
        out_specs=out_specs,
        check_vma=False,
    )
```

```python
import functools

import jax
import jax.numpy as jnp
from jax import lax
from jax.experimental import pallas as pl
from jax.experimental.layout import Layout, with_layout_constraint
from jax.experimental.pallas import tpu as pltpu
from jax.sharding import PartitionSpec as P

BF = jnp.bfloat16
F32 = jnp.float32
FFC = 256
ROWS = 384
VMEM_LIMIT = 64 << 20


def round_up(value, unit):
    return -(-value // unit) * unit


def nt(a, b):
    return lax.dot_general(a, b, (((1,), (1,)), ((), ())), preferred_element_type=F32)


def tn(a, b):
    return lax.dot_general(a, b, (((0,), (0,)), ((), ())), preferred_element_type=F32)


def nn(a, b):
    return jnp.dot(a, b, preferred_element_type=F32)


class Piece:
    def __init__(self, members, patches):
        self.members = []
        offset = 0
        for group, index in members:
            self.members.append((group, index, offset))
            offset += patches[group]
        self.total = offset
        self.width = round_up(offset, 128)
        self.work = round_up(offset, 128)
        self.groups = sorted({group for group, _ in members})


def pack_kernel(piece, k, patches, masked, me_ref, live_ref, *refs):
    ng = len(piece.groups)
    xs = dict(zip(piece.groups, refs[:ng]))
    outs = refs[ng:]
    me = me_ref[0]
    for s in range(k):
        owner = lax.rem(me + s, k)
        out = outs[s]
        for group, index, offset in piece.members:
            p = patches[group]
            image = owner + k * index
            v = xs[group][image]
            if masked:
                v = (v.astype(F32) * (image < live_ref[group]).astype(F32)).astype(BF)
            out[:, offset : offset + p] = v
        if piece.width > piece.total:
            out[:, piece.total :] = jnp.zeros((out.shape[0], piece.width - piece.total), BF)


def pack(piece, k, patches, me, live, tensors, masked):
    c = tensors[0].shape[1]
    vmem = pl.BlockSpec(memory_space=pltpu.VMEM)
    smem = pl.BlockSpec(memory_space=pltpu.SMEM)
    return pl.pallas_call(
        functools.partial(pack_kernel, piece, k, patches, masked),
        out_shape=[jax.ShapeDtypeStruct((c, piece.width), BF)] * k,
        in_specs=[smem, smem] + [vmem] * len(piece.groups),
        out_specs=[vmem] * k,
        compiler_params=pltpu.CompilerParams(vmem_limit_bytes=32 << 20),
        name="pack",
    )(me, live, *[tensors[g] for g in piece.groups])


def unpack_kernel(pieces, groups, k, patches, masked, me_ref, live_ref, *refs):
    buffers = [refs[i * k : (i + 1) * k] for i in range(len(pieces))]
    outs = refs[len(pieces) * k :]
    me = me_ref[0]
    for piece, bufs in zip(pieces, buffers):
        for s in range(k):
            owner = lax.rem(me - s + k, k)
            for group, index, offset in piece.members:
                if group not in groups:
                    continue
                p = patches[group]
                image = owner + k * index
                v = bufs[s][:, offset : offset + p].astype(F32)
                if masked:
                    v = v * (image < live_ref[group]).astype(F32)
                outs[groups.index(group)][image] = v


def unpack(pieces, groups, k, patches, images, me, live, buffers, masked):
    c = buffers[0][0].shape[0]
    vmem = pl.BlockSpec(memory_space=pltpu.VMEM)
    smem = pl.BlockSpec(memory_space=pltpu.SMEM)
    return pl.pallas_call(
        functools.partial(unpack_kernel, pieces, groups, k, patches, masked),
        out_shape=[jax.ShapeDtypeStruct((images[g], c, patches[g]), F32) for g in groups],
        in_specs=[smem, smem] + [vmem] * (k * len(pieces)),
        out_specs=[vmem] * len(groups),
        compiler_params=pltpu.CompilerParams(vmem_limit_bytes=32 << 20),
        name="unpack",
    )(me, live, *[b for bufs in buffers for b in bufs])


class Rows:
    def __init__(self, ff, width, patches, blocks):
        small, medium, large = patches
        self.out = ff
        self.misc = 2 * ff
        self.lanes = width // 128
        side = round_up(medium, 128)
        top = self.misc + round_up(large, 8)
        self.side = side
        self.vec = top + round_up(small, 8)
        rest = self.vec + 16 * self.lanes
        pieces = -(-medium // (width - side))
        span = -(-medium // pieces)
        for cut in range(8, round_up(medium, 8) + 1, 8):
            left = max(medium - cut, 0)
            if rest - top + pieces * round_up(left, 8) <= cut:
                break
        self.mix = [[(0, small, 0, small, top, side)], [(0, min(cut, medium), 0, medium, top, 0)], [(0, large, 0, large, self.misc, 0)]]
        for i in range(pieces if left else 0):
            lanes = min(span, medium - i * span)
            self.mix[1].append((cut, left, i * span, lanes, rest + i * round_up(left, 8), side))
        self.used = top + cut
        self.blocks = blocks
        self.block = round_up(-(-self.used // blocks), 8)
        self.total = blocks * self.block

    def vector(self, index, length):
        return [(128 * q, min(128, length - 128 * q), self.vec + 16 * q + index) for q in range(-(-length // 128))]


BIAS_IN, PATCH = 8, 12


def over_rows(count, body):
    def step(i, carry):
        body(pl.ds(pl.multiple_of(i * ROWS, ROWS), ROWS))
        return carry

    lax.fori_loop(0, count // ROWS, step, 0)


def channel(cols, layer, j):
    return lambda r: cols[layer, r, j : j + 1]


class Copies:
    def __init__(self, sem):
        self.sem, self.count = sem, 0
        self.started = {}

    def start(self, key, src, dst):
        cp = pltpu.make_async_copy(src, dst, self.sem.at[self.count])
        self.count += 1
        cp.start()
        self.started[key] = cp

    def wait(self, *keys):
        for key in keys:
            self.started.pop(key).wait()

    def wait_all(self):
        self.wait(*list(self.started))


KEPT = ("state", "mixs", "nrm", "sc", "brs", "act", "dact")


def kept_shapes(layer, D, F, W):
    return {
        "state": ((D, W), BF if layer == 0 else F32),
        "mixs": ((D, W), F32),
        "nrm": ((D, W), BF),
        "sc": ((D, W), BF),
        "brs": ((D, W), BF),
        "act": ((F, W), BF),
        "dact": ((F, W), BF),
    }


def load_columns(refs, line, cols, layers):
    line[...] = jnp.zeros(line.shape, F32)
    for l in range(layers):
        for j, ref in enumerate(refs):
            line[j : j + 1, :] = ref[l : l + 1, :]
        cols[l] = jnp.transpose(line[...])


def forward_kernel(piece, k, patches, layers, *refs):
    refs = list(refs)

    def take(n):
        out, refs[:] = refs[:n], refs[n:]
        return out

    (me_ref,) = take(1)
    ins = take(k)
    w1_h, w2_h = take(2)
    mix = dict(zip(piece.groups, take(len(piece.groups))))
    bias = dict(zip(piece.groups, take(len(piece.groups))))
    vectors = take(7)
    (b1_ref,) = take(1)
    outs = take(k)
    kept_h = [dict(zip(KEPT, take(len(KEPT)))) for _ in range(layers)]
    kept = [dict(zip(KEPT, take(len(KEPT)))) for _ in range(layers)]
    last, w1, w2, line, cols, sem = refs
    D, W = last.shape
    F = w2.shape[1]
    c = D // k
    me = me_ref[0]
    copies = Copies(sem)
    for l in range(layers):
        copies.start((l, "w1"), w1_h.at[l], w1.at[l, pl.ds(0, D)])
        copies.start((l, "w2"), w2_h.at[l], w2.at[l])

    def keep(l, name):
        copies.start((l, name), kept[l][name].at[pl.ds(0, D)], kept_h[l][name])

    x0 = kept[0]["state"]
    for s in range(k):
        at = pl.ds(pl.multiple_of(lax.rem(me - s + k, k) * c, 16), c)
        x0[at, : piece.width] = ins[s][...]
    if W > piece.width:
        x0[:, piece.width :] = jnp.zeros((D, W - piece.width), BF)
    keep(0, "state")
    load_columns(vectors, line, cols, layers)

    for l in range(layers):
        a, b, g, f, h, ff, b2 = [channel(cols, l, j) for j in range(7)]
        state, mixs, nrm, sc, brs, act, dact = [kept[l][name] for name in KEPT]
        nxt = kept[l + 1]["state"] if l + 1 < layers else last
        if W > piece.total:
            mixs[:, piece.total :] = jnp.zeros((D, W - piece.total), F32)

        def normalise(r):
            nrm[r, :] = (state[r, :].astype(F32) * a(r) + b(r)).astype(BF)

        over_rows(D, normalise)
        keep(l, "nrm")
        for group, _, o in piece.members:
            p = patches[group]
            mixs[:, o : o + p] = nt(nrm[:, o : o + p], mix[group][l]) + bias[group][l : l + 1, :]

        def blend(r):
            middle = state[r, :].astype(F32) + g(r) * mixs[r, :]
            nxt[r, :] = middle
            sc[r, :] = (middle * f(r) + h(r)).astype(BF)

        over_rows(D, blend)
        keep(l, "mixs")
        keep(l, "sc")
        sc[D:, :] = jnp.ones((sc.shape[0] - D, W), BF)
        rest = b1_ref[l : l + 1, :]
        parts = []
        for _ in range(3):
            parts.append(rest.astype(BF).astype(F32))
            rest = rest - parts[-1]
        parts.append(jnp.zeros((w1.shape[1] - D - 3, F), F32))
        w1[l, D:, :] = jnp.concatenate(parts, 0).astype(BF)
        copies.wait((l, "w1"), (l, "w2"))
        s = sc[...]
        for i in range(F // FFC):
            fr = pl.ds(i * FFC, FFC)
            v = tn(w1[l, :, fr], s)
            v2 = v * v
            t = jnp.tanh(v * (0.7978845608 + (0.7978845608 * 0.044715) * v2))
            hp = 0.5 * t + 0.5
            ac = v * hp
            q = 2 * 0.7978845608 + (6 * 0.7978845608 * 0.044715) * v2
            act[fr, :] = ac.astype(BF)
            dact[fr, :] = (hp + (ac - ac * hp) * q).astype(BF)
            for name in ("act", "dact"):
                copies.start((l, name, i), kept[l][name].at[fr], kept_h[l][name].at[fr])
        br = (tn(w2[l], act[...]) + cols[l, :, 6:7]).astype(BF)
        brs[...] = br
        nxt[...] = nxt[...] + cols[l, :, 5:6] * br.astype(F32)
        keep(l, "brs")
        if l + 1 < layers:
            keep(l + 1, "state")

    for s in range(k):
        at = pl.ds(pl.multiple_of(lax.rem(me + s, k) * c, 16), c)
        outs[s][...] = last[at, : piece.width].astype(BF)
    copies.wait_all()


def with_ones(shapes, D, W):
    return {**shapes, "sc": ((D + 16, W), BF)}


def forward(piece, k, patches, me, bufs, w1, w2, mixes, biases, vectors, b1):
    L, D, F = w1.shape
    W = piece.work
    vmem = pl.BlockSpec(memory_space=pltpu.VMEM)
    smem = pl.BlockSpec(memory_space=pltpu.SMEM)
    hbm = pl.BlockSpec(memory_space=pl.ANY)
    args = [me, *bufs, w1, w2, *[mixes[g] for g in piece.groups], *[biases[g] for g in piece.groups], *vectors, b1]
    specs = [smem] + [vmem] * k + [hbm] * 2 + [vmem] * (2 * len(piece.groups) + len(vectors) + 1)
    c = bufs[0].shape[0]
    kept = [shape for l in range(L) for shape in kept_shapes(l, D, F, W).values()]
    scratch = [pltpu.VMEM(*v) for l in range(L) for v in with_ones(kept_shapes(l, D, F, W), D, W).values()]
    scratch += [
        pltpu.VMEM((D, W), F32),
        pltpu.VMEM((L, D + 16, F), BF),
        pltpu.VMEM((L, F, D), BF),
        pltpu.VMEM((128, D), F32),
        pltpu.VMEM((L, D, 128), F32),
        pltpu.SemaphoreType.DMA((L * (7 + 2 * (F // FFC)),)),
    ]
    out = pl.pallas_call(
        functools.partial(forward_kernel, piece, k, patches, L),
        out_shape=[jax.ShapeDtypeStruct((c, piece.width), BF)] * k + [jax.ShapeDtypeStruct(*v) for v in kept],
        in_specs=specs,
        out_specs=[vmem] * k + [hbm] * len(kept),
        scratch_shapes=scratch,
        compiler_params=pltpu.CompilerParams(vmem_limit_bytes=VMEM_LIMIT),
        name="forward",
    )(*args)
    n = len(KEPT)
    return out[:k], out[k:]


def backward_kernel(piece, k, patches, rows, layers, first, final, *refs):
    refs = list(refs)

    def take(n):
        out, refs[:] = refs[:n], refs[n:]
        return out

    (me_ref,) = take(1)
    ins = take(k)
    kept_h = [dict(zip(KEPT, take(len(KEPT)))) for _ in range(layers)]
    w1_h, w2_h = take(2)
    mix = dict(zip(piece.groups, take(len(piece.groups))))
    vectors = take(7)
    accs_h = [] if first else take(layers)
    outs = take(k)
    sums_h = [take(2 if final else 1) for _ in range(layers)]
    kept = [dict(zip(KEPT, take(len(KEPT)))) for _ in range(layers)]
    gn, gb, gs, dy, w1s, w2s, accs, stages, gb1, gcol, gpb, line, cols, sem = refs
    D, W = gn.shape
    F = w2s.shape[1]
    c = D // k
    me = me_ref[0]
    core = lax.rem(me_ref[1], 2)
    copies = Copies(sem)
    half_f = F // 2
    for l in reversed(range(layers)):
        copies.start((l, "w2"), w2_h.at[l], w2s.at[l])
        for i in range(2):
            at = pl.ds(i * half_f, half_f)
            copies.start((l, "dact", i), kept_h[l]["dact"].at[at], kept[l]["dact"].at[at])
        copies.start((l, "w1"), w1_h.at[l], w1s.at[l])
        copies.start((l, "sc"), kept_h[l]["sc"], kept[l]["sc"].at[pl.ds(0, D)])
        if not first:
            copies.start((l, "acc"), accs_h[l], accs.at[l])
        for name in ("act", "brs", "mixs", "state", "nrm"):
            copies.start((l, name), kept_h[l][name], kept[l][name])

    load_columns(vectors, line, cols, layers)
    for s in range(k):
        at = pl.ds(pl.multiple_of(lax.rem(me - s + k, k) * c, 16), c)
        dy[at, : piece.width] = ins[s][...].astype(F32)
    if W > piece.width:
        dy[:, piece.width :] = jnp.zeros((D, W - piece.width), F32)
    if W > piece.total:
        gn[:, piece.total :] = jnp.zeros((D, W - piece.total), F32)
    gcol[...] = jnp.zeros(gcol.shape, F32)

    def put(r, j, v):
        gcol[r, j : j + 1] = jnp.sum(v, 1, keepdims=True)

    for l in reversed(range(layers)):
        a, b, g, f, h, ff, b2 = [channel(cols, l, j) for j in range(7)]
        state, mixs, nrm, sc, brs, act, dact = [kept[l][name] for name in KEPT]
        acc = accs.at[l]
        w1, w2 = w1s.at[l], w2s.at[l]
        sc[D:, :] = jnp.ones((sc.shape[0] - D, W), BF)
        if first:
            acc[rows.misc :, :] = jnp.zeros((rows.total - rows.misc, D), F32)
        gpb[...] = jnp.zeros(gpb.shape, F32)

        def gain(r):
            gbv = (dy[r, :] * ff(r)).astype(BF)
            gb[r, :] = gbv
            put(r, 6, gbv.astype(F32))

        over_rows(D, gain)
        copies.wait((l, "w2"))
        up = gb[...]
        for i in range(F // FFC):
            if i * FFC % half_f == 0:
                copies.wait((l, "dact", i * FFC // half_f))
            fr = pl.ds(i * FFC, FFC)
            dact[fr, :] = (nn(w2[fr, :], up) * dact[fr, :].astype(F32)).astype(BF)
        copies.wait((l, "w1"))
        gs[...] = nn(w1[...], dact[...]).astype(BF)
        copies.wait((l, "sc"))
        if not first:
            copies.wait((l, "acc"))

        def weight_in(n, carry):
            r = nt(sc[...], dact[pl.ds(pl.multiple_of(n * 2 * D, 2 * D), 2 * D), :])
            for i in range(2):
                at = pl.ds(pl.multiple_of((2 * n + i) * D, D), D)
                part = r[:D, i * D : (i + 1) * D]
                acc[at, :] = part if first else acc[at, :] + part
            gb1[:, pl.ds(pl.multiple_of(n * 2 * D, 2 * D), 2 * D)] = r[D : D + 8]
            return carry

        lax.fori_loop(0, F // (2 * D), weight_in, 0)
        copies.wait((l, "act"))

        def weight_out(n, carry):
            r = nt(act[pl.ds(pl.multiple_of(n * 512, 512), 512), :], gb[...])
            at = pl.ds(pl.multiple_of(rows.out + n * 512, 512), 512)
            acc[at, :] = r if first else acc[at, :] + r
            return carry

        lax.fori_loop(0, F // 512, weight_out, 0)
        copies.wait((l, "brs"), (l, "mixs"), (l, "state"))

        def back(r):
            gsf = gs[r, :].astype(F32)
            mixture = mixs[r, :]
            middle = state[r, :].astype(F32) + g(r) * mixture
            d = dy[r, :]
            put(r, 5, d * brs[r, :].astype(F32))
            gm = d + f(r) * gsf
            dy[r, :] = gm
            put(r, 3, gsf * middle)
            put(r, 4, gsf)
            put(r, 2, gm * mixture)
            gmb = (g(r) * gm).astype(BF)
            gb[r, :] = gmb
            gpb[...] = gpb[...] + gmb.astype(F32).reshape(ROWS // 8, 8, W).sum(0)

        over_rows(D, back)
        pbias = jnp.sum(gpb[...], 0, keepdims=True)
        copies.wait((l, "nrm"))
        side = rows.side
        for group, _, o in piece.members:
            p = patches[group]
            gi = gb[:, o : o + p]
            product = tn(gi, nrm[:, o : o + p])
            for r0, nr, c0, nc, at, lane in rows.mix[group]:
                part = product[r0 : r0 + nr, c0 : c0 + nc]
                acc[at : at + nr, lane : lane + nc] = acc[at : at + nr, lane : lane + nc] + part
            gn[:, o : o + p] = nn(gi, mix[group][l])
            for c0, nc, at in rows.vector(PATCH + group, p):
                part = pbias[:, o + c0 : o + c0 + nc]
                acc[at : at + 1, side : side + nc] = acc[at : at + 1, side : side + nc] + part

        def pass_down(r):
            n = gn[r, :]
            put(r, 0, n * state[r, :].astype(F32))
            put(r, 1, n)
            dy[r, :] = dy[r, :] + a(r) * n

        over_rows(D, pass_down)
        sums = jnp.transpose(gcol[...])[:8]
        for c0, nc, at in rows.vector(0, D):
            acc[at : at + 8, side : side + nc] = acc[at : at + 8, side : side + nc] + sums[:, c0 : c0 + nc]
        for t in range(F // D):
            for c0, nc, at in rows.vector(BIAS_IN + t, D):
                part = gb1[0:1, t * D + c0 : t * D + c0 + nc]
                acc[at : at + 1, side : side + nc] = acc[at : at + 1, side : side + nc] + part
        if final:
            half = rows.total // 2
            stages[l] = acc[pl.ds(pl.multiple_of((1 - core) * half, 16), half), :].astype(BF)
            copies.start((l, "send"), stages.at[l], sums_h[l][0])
            copies.start((l, "keep"), acc.at[pl.ds(pl.multiple_of(core * half, 16), half)], sums_h[l][1])
        else:
            copies.start((l, "sums"), acc, sums_h[l][0])

    for s in range(k):
        at = pl.ds(pl.multiple_of(lax.rem(me + s, k) * c, 16), c)
        outs[s][...] = dy[at, : piece.width].astype(BF)
    copies.wait_all()


def backward(piece, k, patches, rows, me, incoming, kept, w1, w2, mixes, vectors, accs, final):
    L, D, F = w1.shape
    W = piece.work
    first = accs is None
    vmem = pl.BlockSpec(memory_space=pltpu.VMEM)
    smem = pl.BlockSpec(memory_space=pltpu.SMEM)
    hbm = pl.BlockSpec(memory_space=pl.ANY)
    args = [me, *incoming, *kept, w1, w2, *[mixes[g] for g in piece.groups], *vectors]
    specs = [smem] + [vmem] * k + [hbm] * (len(kept) + 2) + [vmem] * (len(piece.groups) + len(vectors))
    if not first:
        args += accs
        specs += [hbm] * L
    out_shape = [jax.ShapeDtypeStruct((D // k, piece.width), BF)] * k
    half = rows.total // 2
    if final:
        out_shape += [jax.ShapeDtypeStruct((half, D), BF), jax.ShapeDtypeStruct((half, D), F32)] * L
    else:
        out_shape += [jax.ShapeDtypeStruct((rows.total, D), F32)] * L
    scratch = [pltpu.VMEM(*v) for l in range(L) for v in with_ones(kept_shapes(l, D, F, W), D, W).values()]
    scratch += [
        pltpu.VMEM((D, W), F32),
        pltpu.VMEM((D, W), BF),
        pltpu.VMEM((D, W), BF),
        pltpu.VMEM((D, W), F32),
        pltpu.VMEM((L, D, F), BF),
        pltpu.VMEM((L, F, D), BF),
        pltpu.VMEM((L, rows.total, D), F32),
        pltpu.VMEM((L, half, D) if final else (8, 128), BF),
        pltpu.VMEM((8, F), F32),
        pltpu.VMEM((D, 128), F32),
        pltpu.VMEM((8, W), F32),
        pltpu.VMEM((128, D), F32),
        pltpu.VMEM((L, D, 128), F32),
        pltpu.SemaphoreType.DMA((13 * L,)),
    ]
    out = pl.pallas_call(
        functools.partial(backward_kernel, piece, k, patches, rows, L, first, final),
        out_shape=out_shape,
        in_specs=specs,
        out_specs=[vmem] * k + [hbm] * (len(out_shape) - k),
        scratch_shapes=scratch,
        compiler_params=pltpu.CompilerParams(vmem_limit_bytes=VMEM_LIMIT),
        name="backward",
    )(*args)
    sums = out[k:]
    n = 2 if final else 1
    return out[:k], [sums[l * n : (l + 1) * n] for l in range(L)]


def after(value, *events):
    return lax.optimization_barrier((value, events))[0]


def flip(v, bit, n):
    return lax.ppermute(v, "dp", [(i, i ^ bit) for i in range(n)])


def cycle(v, s, k):
    return lax.ppermute(v, "swap", [(i, (i + s) % k) for i in range(k)])


def spread(bufs, distances=None):
    return [cycle(bufs[s], s, len(bufs)) if s else bufs[0] for s in distances or range(len(bufs))]


def local(body, pos, ins, shapes, name):
    vmem = pl.BlockSpec(memory_space=pltpu.VMEM)
    return pl.pallas_call(
        body,
        out_shape=[jax.ShapeDtypeStruct(*shape) for shape in shapes],
        in_specs=[pl.BlockSpec(memory_space=pltpu.SMEM)] + [vmem] * len(ins),
        out_specs=[vmem] * len(shapes),
        compiler_params=pltpu.CompilerParams(vmem_limit_bytes=40 << 20),
        name=name,
    )(pos, *ins)


def side(pos_ref, bit):
    return lax.rem(lax.div(pos_ref[1], bit), 2)


def split_first(pos, keep, came, bits):
    n, r, d = keep.shape
    q = n // 4

    def body(pos_ref, keep_ref, came_ref, *outs):
        for h in range(2):
            mine = side(pos_ref, bits[h])
            at = pl.ds(2 * q * h + mine * q, q)
            outs[2 * h][...] = keep_ref[at] + came_ref[at].astype(F32)
            at = pl.ds(2 * q * h + (1 - mine) * q, q)
            outs[2 * h + 1][...] = (keep_ref[at] + came_ref[at].astype(F32)).astype(BF)

    out = local(body, pos, [keep, came], [((q, r, d), F32), ((q, r, d), BF)] * 2, "split")
    return [(out[0], out[1]), (out[2], out[3])]


def split_next(pos, keeps, cames, bits):
    n, r, d = keeps[0].shape
    q = n // 2

    def body(pos_ref, k0, k1, c0, c1, *outs):
        for h, (keep_ref, came_ref) in enumerate(((k0, c0), (k1, c1))):
            mine = side(pos_ref, bits[h])
            at = pl.ds(mine * q, q)
            outs[2 * h][...] = keep_ref[at] + came_ref[at].astype(F32)
            at = pl.ds((1 - mine) * q, q)
            outs[2 * h + 1][...] = (keep_ref[at] + came_ref[at].astype(F32)).astype(BF)

    out = local(body, pos, [*keeps, *cames], [((q, r, d), F32), ((q, r, d), BF)] * 2, "split")
    return [(out[0], out[1]), (out[2], out[3])]


def split_swap(pos, keeps, cames, k):
    n, r, d = keeps[0].shape

    def body(pos_ref, k0, k1, c0, c1, *refs):
        outs, both = refs[:k], refs[k]
        both[:n] = k0[...] + c0[...].astype(F32)
        both[n:] = k1[...] + c1[...].astype(F32)
        me = pos_ref[0]
        outs[0][...] = both[me]
        for s in range(1, k):
            outs[s][...] = both[lax.rem(me + s, k)].astype(BF)

    vmem = pl.BlockSpec(memory_space=pltpu.VMEM)
    return pl.pallas_call(
        body,
        out_shape=[jax.ShapeDtypeStruct((r, d), F32)] + [jax.ShapeDtypeStruct((r, d), BF)] * (k - 1),
        in_specs=[pl.BlockSpec(memory_space=pltpu.SMEM)] + [vmem] * 4,
        out_specs=[vmem] * k,
        scratch_shapes=[pltpu.VMEM((2 * n, r, d), F32)],
        name="split_swap",
    )(pos, *keeps, *cames)


def add_swap(pos, keep, cames):
    def body(pos_ref, keep_ref, *refs):
        total = keep_ref[...]
        for came in refs[:-1]:
            total = total + came[...].astype(F32)
        refs[-1][...] = total.astype(BF)

    return local(body, pos, [keep, *cames], [(keep.shape, BF)], "add_swap")[0]


def join_swap(pos, parts, k):
    r, d = parts[0].shape
    n = k // 2

    def body(pos_ref, *refs):
        ins, (o0, o1), both = refs[:k], refs[k : k + 2], refs[k + 2]
        for s in range(k):
            both[lax.rem(pos_ref[0] - s + k, k)] = ins[s][...]
        o0[...] = both[:n]
        o1[...] = both[n:]

    vmem = pl.BlockSpec(memory_space=pltpu.VMEM)
    return pl.pallas_call(
        body,
        out_shape=[jax.ShapeDtypeStruct((n, r, d), BF)] * 2,
        in_specs=[pl.BlockSpec(memory_space=pltpu.SMEM)] + [vmem] * k,
        out_specs=[vmem] * 2,
        scratch_shapes=[pltpu.VMEM((k, r, d), BF)],
        name="join_swap",
    )(pos, *parts)


def join(pos, owns, cames, bits, whole):
    q, r, d = owns[0].shape

    def body(pos_ref, v0, v1, c0, c1, *outs):
        for h, (own, came) in enumerate(((v0, c0), (v1, c1))):
            mine = side(pos_ref, bits[h])
            out, base = (outs[0], 2 * q * h) if whole else (outs[h], 0)
            out[pl.ds(base + mine * q, q)] = own[...]
            out[pl.ds(base + (1 - mine) * q, q)] = came[...]

    shapes = [((4 * q, r, d), BF)] if whole else [((2 * q, r, d), BF)] * 2
    return local(body, pos, [*owns, *cames], shapes, "join")


def finish(pos, rows, ff, layer, layers, patches, mine, other, before):
    r, d = rows.total, mine.shape[-1]
    half = r // 2
    nm = rows.used - rows.misc
    last = layer == 0
    big = [(layers, d, ff), (layers, ff, d)]
    small = [(layers, d)] * 7 + [(layers, ff)] + [(layers, p) for p in patches] + [(p, layers, p) for p in patches]
    kept = before[:2]
    miscs = before[2:]

    def body(pos_ref, a_ref, b_ref, *refs):
        refs = refs[len(kept) :]
        misc_refs, refs = refs[: len(miscs)], refs[len(miscs) :]
        outs, rest, (full, win, sem) = refs[:2], refs[2:-3], refs[-3:]
        core = lax.rem(pos_ref[1], 2)
        full[pl.ds(pl.multiple_of(core * half, 16), half), :] = a_ref[...].astype(F32)
        full[pl.ds(pl.multiple_of((1 - core) * half, 16), half), :] = b_ref[...].astype(F32)
        copies = [pltpu.make_async_copy(full.at[pl.ds(rows.out, ff)], outs[1].at[layer], sem.at[1])]
        copies[0].start()
        for t in range(ff // d):
            win[:, t * d : (t + 1) * d] = full[t * d : (t + 1) * d, :]
        copies.append(pltpu.make_async_copy(win, outs[0].at[layer], sem.at[0]))
        copies[1].start()
        if last:
            sources = [(layers - 1 - i, ref, 0) for i, ref in enumerate(misc_refs)] + [(0, full, rows.misc)]
            for l, ref, base in sources:
                base -= rows.misc
                side = rows.side
                vectors = [(rest[j], 0, j, d) for j in range(7)]
                vectors += [(rest[7], t * d, BIAS_IN + t, d) for t in range(ff // d)]
                vectors += [(rest[8 + g], 0, PATCH + g, p) for g, p in enumerate(patches)]
                for out, start, index, length in vectors:
                    for c0, nc, at in rows.vector(index, length):
                        out[l : l + 1, start + c0 : start + c0 + nc] = ref[base + at : base + at + 1, side : side + nc]
                for g in range(len(patches)):
                    parts = [
                        (r0, ref[base + at : base + at + nr, lane : lane + nc])
                        for r0, nr, _, nc, at, lane in rows.mix[g]
                    ]
                    whole = parts[0][1]
                    if len(parts) > 1:
                        low = jnp.concatenate([part for _, part in parts[1:]], 1)
                        whole = jnp.concatenate([whole, low], 0)
                    rest[11 + g][:, l, :] = whole
        else:
            rest[0][...] = full[rows.misc : rows.used, :]
        for cp in copies:
            cp.wait()

    vmem = pl.BlockSpec(memory_space=pltpu.VMEM)
    hbm = pl.BlockSpec(memory_space=pl.ANY)
    shapes = big + (small if last else [(nm, d)])
    out = pl.pallas_call(
        body,
        out_shape=[jax.ShapeDtypeStruct(shape, F32) for shape in shapes],
        in_specs=[pl.BlockSpec(memory_space=pltpu.SMEM), vmem, vmem] + [hbm] * len(kept) + [vmem] * len(miscs),
        out_specs=[hbm] * 2 + [vmem] * (len(shapes) - 2),
        scratch_shapes=[pltpu.VMEM((r, d), F32), pltpu.VMEM((d, ff), F32), pltpu.SemaphoreType.DMA((2,))],
        input_output_aliases={3 + i: i for i in range(len(kept))},
        compiler_params=pltpu.CompilerParams(vmem_limit_bytes=40 << 20),
        name="finish",
    )(pos, mine, other, *kept, *miscs)
    return out if last else [*out[:2], *miscs, out[2]]


def orders(n):
    bits = [1 << i for i in range(1, n.bit_length() - 1)]
    return list(zip(bits, bits[::-1]))


class Chain:
    def __init__(self, pos, rows, n, k):
        self.pos, self.rows, self.n, self.k = pos, rows, n, k
        self.steps = orders(n)

    def begin(self, send, keep):
        view = (self.rows.blocks // 2, self.rows.block, send.shape[-1])
        self.keep, self.came = keep.reshape(view), flip(send, 1, self.n).reshape(view)

    def ready(self, *events):
        self.came = after(self.came, events)

    def split(self, t):
        if t == 0:
            halves = split_first(self.pos, self.keep, self.came, self.steps[0])
        else:
            halves = split_next(self.pos, self.keep, self.came, self.steps[t])
        self.keep = [h[0] for h in halves]
        self.came = [flip(h[1], bit, self.n) for h, bit in zip(halves, self.steps[t])]
        return halves

    def split_swap(self):
        parts = split_swap(self.pos, self.keep, self.came, self.k)
        self.keep, self.came = parts[0], [cycle(parts[s], s, self.k) for s in range(1, self.k)]
        return parts

    def add_swap(self):
        self.keep = add_swap(self.pos, self.keep, self.came)
        self.came = [cycle(self.keep, s, self.k) for s in range(1, self.k)]
        return self.keep

    def join_swap(self):
        self.keep = join_swap(self.pos, [self.keep, *self.came], self.k)
        self.came = [flip(v, bit, self.n) for v, bit in zip(self.keep, self.steps[-1])]
        return self.keep

    def join(self, t):
        self.keep = join(self.pos, self.keep, self.came, self.steps[t], t == 0)
        if t > 0:
            self.came = [flip(v, bit, self.n) for v, bit in zip(self.keep, self.steps[t - 1])]
        else:
            self.keep = self.keep[0].reshape(-1, self.keep[0].shape[-1])
            self.came = flip(self.keep, 1, self.n)
        return self.keep


def on_device(
    n_dp,
    k,
    source_tiles_smallest,
    source_tiles_moderate,
    source_tiles_largest,
    target_cotangent_smallest,
    target_cotangent_moderate,
    target_cotangent_largest,
    surviving_tallies,
    token_affine_factor,
    token_affine_addend,
    crosstile_matrix_smallest,
    crosstile_matrix_moderate,
    crosstile_matrix_largest,
    crosstile_addend_smallest,
    crosstile_addend_moderate,
    crosstile_addend_largest,
    token_blend_factor,
    feedforward_affine_factor,
    feedforward_affine_addend,
    widening_matrix,
    widening_addend,
    narrowing_matrix,
    narrowing_addend,
    feedforward_factor,
):
    L, D, F = widening_matrix.shape
    tensors = [source_tiles_smallest, source_tiles_moderate, source_tiles_largest]
    cotans = [target_cotangent_smallest, target_cotangent_moderate, target_cotangent_largest]
    mixes = [crosstile_matrix_smallest, crosstile_matrix_moderate, crosstile_matrix_largest]
    biases = [crosstile_addend_smallest, crosstile_addend_moderate, crosstile_addend_largest]
    patches = [t.shape[0] for t in tensors]
    images = [t.shape[1] for t in tensors]
    own = [count // k for count in images]
    idx = lax.axis_index("dp")
    pos = lax.axis_index("swap")
    me = jnp.stack([pos, idx]).astype(jnp.int32)
    live = surviving_tallies[0]

    pieces = [
        Piece([(2, i) for i in range(own[2])] + [(0, i) for i in range(1, own[0])], patches),
        Piece([(1, i) for i in range(own[1])] + [(0, 0)], patches),
    ]
    rows = Rows(F, D, patches, n_dp * k)

    tensors = [jnp.transpose(t, (1, 2, 0)) for t in tensors]
    cotans = [jnp.transpose(t, (1, 2, 0)) for t in cotans]
    vectors = [
        token_affine_factor,
        token_affine_addend,
        token_blend_factor,
        feedforward_affine_factor,
        feedforward_affine_addend,
        feedforward_factor,
        narrowing_addend,
    ]
    w1, w2 = widening_matrix, narrowing_matrix

    first, second = pieces
    mixes = [with_layout_constraint(m, Layout((0, 1, 2))) for m in mixes]
    x_bufs = [pack(piece, k, patches, me, live, tensors, False) for piece in pieces]
    c_bufs = [pack(piece, k, patches, me, live, cotans, True) for piece in pieces]
    far = [k // 2]
    near = [s for s in range(1, k) if s != k // 2]

    x_first = after(spread(x_bufs[0]), (mixes, x_bufs[1], c_bufs))
    x_second = spread(after(x_bufs[1], x_first))
    out_first, kept_first = forward(first, k, patches, me, x_first, w1, w2, mixes, biases, vectors, widening_addend)
    x_second = after(x_second, out_first)
    c_first = spread(after(c_bufs[0], x_second))
    out_second, kept_second = forward(second, k, patches, me, x_second, w1, w2, mixes, biases, vectors, widening_addend)
    c_first = after(c_first, out_second)
    c_second = spread(after(c_bufs[1], c_first))
    came = {0: out_first[0]}
    came.update(zip(near, spread(after(out_first, c_first), near)))
    grad_first, sums = backward(first, k, patches, rows, me, c_first, kept_first, w1, w2, mixes, vectors, None, False)
    accs = [v[0] for v in sums]
    c_second, came = after((c_second, came), grad_first)
    came.update(zip(far, spread(after(out_first, c_second), far)))
    out_first = [came[s] for s in range(k)]
    out_second = spread(after(out_second, c_second))
    grad_second, halves = backward(second, k, patches, rows, me, c_second, kept_second, w1, w2, mixes, vectors, accs, True)
    out_first, out_second = after((out_first, out_second), grad_second)

    halves, grad_first = after((halves, grad_first), (out_first, out_second))
    came = {0: grad_first[0]}
    came.update(zip(near + far, spread(grad_first, near + far)))
    grad_first = [came[s] for s in range(k)]
    order = list(reversed(range(L)))
    chains = [Chain(me, rows, n_dp, k) for _ in order]
    for chain, l in zip(chains, order):
        chain.begin(*halves[l])
    token = ()

    def turn(step, *events):
        nonlocal token
        for i, chain in enumerate(chains):
            then = events[i] if i < len(events) else ()
            chain.ready(token, then() if callable(then) else then)
            token = step(chain)

    outs = [None] * 6
    alone = [g for g in range(3) if g not in second.groups]

    def arrange(base, used, groups, bufs, masked):
        chosen = [pieces[i] for i in used]
        got = unpack(chosen, groups, k, patches, images, me, live, [bufs[i] for i in used], masked)
        for i, g in enumerate(groups):
            outs[base + g] = got[i]
        return got

    count = len(orders(n_dp))
    for t in range(count):
        turn(lambda chain: chain.split(t), [came[s] for s in near] if t == 1 else ())
    turn(lambda chain: chain.split_swap(), grad_first)
    turn(lambda chain: chain.add_swap(), (), lambda: arrange(0, (0,), alone, (after(out_first, token),), True))
    turn(
        lambda chain: chain.join_swap(),
        (),
        lambda: (
            arrange(0, (0, 1), second.groups, (after(out_first, token), out_second), True),
            arrange(3, (0,), alone, (after(grad_first, token),), False),
            chains[0].came,
        ),
    )
    came = {0: grad_second[0]}
    came.update(zip(near + far, spread(after(grad_second, token), near + far)))
    grad_second = [came[s] for s in range(k)]
    for t in reversed(range(count)):
        late = [came[s] for s in (near if t == count - 1 else far if t == 0 else [])]
        turn(lambda chain: chain.join(t), (), late)
    token = arrange(3, (0, 1), second.groups, (grad_first, after(grad_second, token)), False)
    sums = []
    for chain, l in zip(chains, order):
        chain.ready(token, sums)
        sums = finish(me, rows, F, l, L, patches, chain.keep, chain.came, sums)
    outs = [jnp.transpose(v, (2, 0, 1)) for v in outs]
    grad_in, grad_out, *small = sums
    vec, bias_in, patch_bias, mix_of = small[:7], small[7], small[8:11], small[11:]
    mix_of = [jnp.transpose(v, (1, 0, 2)) for v in mix_of]

    return (
        *outs,
        vec[0],
        vec[1],
        *mix_of,
        *patch_bias,
        vec[2],
        vec[3],
        vec[4],
        grad_in,
        bias_in,
        grad_out,
        vec[6],
        vec[5],
    )


def solution(mesh):
    tokens = P(None, "dp", "swap")
    in_specs = (tokens,) * 6 + (P("dp", None),) + (P(),) * 16
    out_specs = (tokens,) * 6 + (P(),) * 16
    return jax.shard_map(
        functools.partial(on_device, mesh.shape["dp"], mesh.shape["swap"]),
        mesh=mesh,
        in_specs=in_specs,
        out_specs=out_specs,
        check_vma=False,
    )
```

```python
import functools

import jax
import jax.numpy as jnp
from jax import lax
from jax.experimental import pallas as pl
from jax.experimental.layout import Layout, with_layout_constraint
from jax.experimental.pallas import tpu as pltpu
from jax.sharding import PartitionSpec as P

BF = jnp.bfloat16
F32 = jnp.float32
FFC = 256
ROWS = 384
VMEM_LIMIT = 64 << 20


def round_up(value, unit):
    return -(-value // unit) * unit


def nt(a, b):
    return lax.dot_general(a, b, (((1,), (1,)), ((), ())), preferred_element_type=F32)


def tn(a, b):
    return lax.dot_general(a, b, (((0,), (0,)), ((), ())), preferred_element_type=F32)


def nn(a, b):
    return jnp.dot(a, b, preferred_element_type=F32)


class Piece:
    def __init__(self, members, patches):
        self.members = []
        offset = 0
        for group, index in members:
            self.members.append((group, index, offset))
            offset += patches[group]
        self.total = offset
        self.width = round_up(offset, 128)
        self.work = round_up(offset, 128)
        self.groups = sorted({group for group, _ in members})


def pack_kernel(piece, k, patches, masked, me_ref, live_ref, *refs):
    ng = len(piece.groups)
    xs = dict(zip(piece.groups, refs[:ng]))
    outs = refs[ng:]
    me = me_ref[0]
    for s in range(k):
        owner = lax.rem(me + s, k)
        out = outs[s]
        for group, index, offset in piece.members:
            p = patches[group]
            image = owner + k * index
            v = xs[group][image]
            if masked:
                v = (v.astype(F32) * (image < live_ref[group]).astype(F32)).astype(BF)
            out[:, offset : offset + p] = v
        if piece.width > piece.total:
            out[:, piece.total :] = jnp.zeros((out.shape[0], piece.width - piece.total), BF)


def pack(piece, k, patches, me, live, tensors, masked):
    c = tensors[0].shape[1]
    vmem = pl.BlockSpec(memory_space=pltpu.VMEM)
    smem = pl.BlockSpec(memory_space=pltpu.SMEM)
    return pl.pallas_call(
        functools.partial(pack_kernel, piece, k, patches, masked),
        out_shape=[jax.ShapeDtypeStruct((c, piece.width), BF)] * k,
        in_specs=[smem, smem] + [vmem] * len(piece.groups),
        out_specs=[vmem] * k,
        compiler_params=pltpu.CompilerParams(vmem_limit_bytes=32 << 20),
        name="pack",
    )(me, live, *[tensors[g] for g in piece.groups])


def unpack_kernel(pieces, groups, k, patches, masked, me_ref, live_ref, *refs):
    buffers = [refs[i * k : (i + 1) * k] for i in range(len(pieces))]
    outs = refs[len(pieces) * k :]
    me = me_ref[0]
    for piece, bufs in zip(pieces, buffers):
        for s in range(k):
            owner = lax.rem(me - s + k, k)
            for group, index, offset in piece.members:
                if group not in groups:
                    continue
                p = patches[group]
                image = owner + k * index
                v = bufs[s][:, offset : offset + p].astype(F32)
                if masked:
                    v = v * (image < live_ref[group]).astype(F32)
                outs[groups.index(group)][image] = v


def unpack(pieces, groups, k, patches, images, me, live, buffers, masked):
    c = buffers[0][0].shape[0]
    vmem = pl.BlockSpec(memory_space=pltpu.VMEM)
    smem = pl.BlockSpec(memory_space=pltpu.SMEM)
    return pl.pallas_call(
        functools.partial(unpack_kernel, pieces, groups, k, patches, masked),
        out_shape=[jax.ShapeDtypeStruct((images[g], c, patches[g]), F32) for g in groups],
        in_specs=[smem, smem] + [vmem] * (k * len(pieces)),
        out_specs=[vmem] * len(groups),
        compiler_params=pltpu.CompilerParams(vmem_limit_bytes=32 << 20),
        name="unpack",
    )(me, live, *[b for bufs in buffers for b in bufs])


class Rows:
    def __init__(self, ff, width, patches, blocks):
        small, medium, large = patches
        self.out = ff
        self.misc = 2 * ff
        self.lanes = width // 128
        side = round_up(medium, 128)
        top = self.misc + round_up(large, 8)
        self.side = side
        self.vec = top + round_up(small, 8)
        rest = self.vec + 16 * self.lanes
        pieces = -(-medium // (width - side))
        span = -(-medium // pieces)
        for cut in range(8, round_up(medium, 8) + 1, 8):
            left = max(medium - cut, 0)
            if rest - top + pieces * round_up(left, 8) <= cut:
                break
        self.mix = [[(0, small, 0, small, top, side)], [(0, min(cut, medium), 0, medium, top, 0)], [(0, large, 0, large, self.misc, 0)]]
        for i in range(pieces if left else 0):
            lanes = min(span, medium - i * span)
            self.mix[1].append((cut, left, i * span, lanes, rest + i * round_up(left, 8), side))
        self.used = top + cut
        self.blocks = blocks
        self.block = round_up(-(-self.used // blocks), 8)
        self.total = blocks * self.block

    def vector(self, index, length):
        return [(128 * q, min(128, length - 128 * q), self.vec + 16 * q + index) for q in range(-(-length // 128))]


BIAS_IN, PATCH = 8, 12


def over_rows(count, body):
    def step(i, carry):
        body(pl.ds(pl.multiple_of(i * ROWS, ROWS), ROWS))
        return carry

    lax.fori_loop(0, count // ROWS, step, 0)


def channel(cols, layer, j):
    return lambda r: cols[layer, r, j : j + 1]


class Copies:
    def __init__(self, sem):
        self.sem, self.count = sem, 0
        self.started = {}

    def start(self, key, src, dst):
        cp = pltpu.make_async_copy(src, dst, self.sem.at[self.count])
        self.count += 1
        cp.start()
        self.started[key] = cp

    def wait(self, *keys):
        for key in keys:
            self.started.pop(key).wait()

    def wait_all(self):
        self.wait(*list(self.started))


KEPT = ("state", "mixs", "nrm", "sc", "brs", "act", "dact")


def kept_shapes(layer, D, F, W):
    return {
        "state": ((D, W), BF if layer == 0 else F32),
        "mixs": ((D, W), F32),
        "nrm": ((D, W), BF),
        "sc": ((D, W), BF),
        "brs": ((D, W), BF),
        "act": ((F, W), BF),
        "dact": ((F, W), BF),
    }


def load_columns(refs, line, cols, layers):
    line[...] = jnp.zeros(line.shape, F32)
    for l in range(layers):
        for j, ref in enumerate(refs):
            line[j : j + 1, :] = ref[l : l + 1, :]
        cols[l] = jnp.transpose(line[...])


def forward_kernel(piece, k, patches, layers, *refs):
    refs = list(refs)

    def take(n):
        out, refs[:] = refs[:n], refs[n:]
        return out

    (me_ref,) = take(1)
    ins = take(k)
    w1_h, w2_h = take(2)
    mix = dict(zip(piece.groups, take(len(piece.groups))))
    bias = dict(zip(piece.groups, take(len(piece.groups))))
    vectors = take(7)
    (b1_ref,) = take(1)
    outs = take(k)
    kept_h = [dict(zip(KEPT, take(len(KEPT)))) for _ in range(layers)]
    kept = [dict(zip(KEPT, take(len(KEPT)))) for _ in range(layers)]
    last, w1, w2, line, cols, sem = refs
    D, W = last.shape
    F = w2.shape[1]
    c = D // k
    me = me_ref[0]
    copies = Copies(sem)
    for l in range(layers):
        copies.start((l, "w1"), w1_h.at[l], w1.at[l, pl.ds(0, D)])
        copies.start((l, "w2"), w2_h.at[l], w2.at[l])

    def keep(l, name):
        copies.start((l, name), kept[l][name].at[pl.ds(0, D)], kept_h[l][name])

    x0 = kept[0]["state"]
    for s in range(k):
        at = pl.ds(pl.multiple_of(lax.rem(me - s + k, k) * c, 16), c)
        x0[at, : piece.width] = ins[s][...]
    if W > piece.width:
        x0[:, piece.width :] = jnp.zeros((D, W - piece.width), BF)
    keep(0, "state")
    load_columns(vectors, line, cols, layers)

    for l in range(layers):
        a, b, g, f, h, ff, b2 = [channel(cols, l, j) for j in range(7)]
        state, mixs, nrm, sc, brs, act, dact = [kept[l][name] for name in KEPT]
        nxt = kept[l + 1]["state"] if l + 1 < layers else last
        if W > piece.total:
            mixs[:, piece.total :] = jnp.zeros((D, W - piece.total), F32)

        def normalise(r):
            nrm[r, :] = (state[r, :].astype(F32) * a(r) + b(r)).astype(BF)

        over_rows(D, normalise)
        keep(l, "nrm")
        for group, _, o in piece.members:
            p = patches[group]
            mixs[:, o : o + p] = nt(nrm[:, o : o + p], mix[group][l]) + bias[group][l : l + 1, :]

        def blend(r):
            middle = state[r, :].astype(F32) + g(r) * mixs[r, :]
            nxt[r, :] = middle
            sc[r, :] = (middle * f(r) + h(r)).astype(BF)

        over_rows(D, blend)
        keep(l, "mixs")
        keep(l, "sc")
        sc[D:, :] = jnp.ones((sc.shape[0] - D, W), BF)
        rest = b1_ref[l : l + 1, :]
        parts = []
        for _ in range(3):
            parts.append(rest.astype(BF).astype(F32))
            rest = rest - parts[-1]
        parts.append(jnp.zeros((w1.shape[1] - D - 3, F), F32))
        w1[l, D:, :] = jnp.concatenate(parts, 0).astype(BF)
        copies.wait((l, "w1"), (l, "w2"))
        s = sc[...]
        for i in range(F // FFC):
            fr = pl.ds(i * FFC, FFC)
            v = tn(w1[l, :, fr], s)
            v2 = v * v
            t = jnp.tanh(v * (0.7978845608 + (0.7978845608 * 0.044715) * v2))
            hp = 0.5 * t + 0.5
            ac = v * hp
            q = 2 * 0.7978845608 + (6 * 0.7978845608 * 0.044715) * v2
            act[fr, :] = ac.astype(BF)
            dact[fr, :] = (hp + (ac - ac * hp) * q).astype(BF)
            for name in ("act", "dact"):
                copies.start((l, name, i), kept[l][name].at[fr], kept_h[l][name].at[fr])
        br = (tn(w2[l], act[...]) + cols[l, :, 6:7]).astype(BF)
        brs[...] = br
        nxt[...] = nxt[...] + cols[l, :, 5:6] * br.astype(F32)
        keep(l, "brs")
        if l + 1 < layers:
            keep(l + 1, "state")

    for s in range(k):
        at = pl.ds(pl.multiple_of(lax.rem(me + s, k) * c, 16), c)
        outs[s][...] = last[at, : piece.width].astype(BF)
    copies.wait_all()


def with_ones(shapes, D, W):
    return {**shapes, "sc": ((D + 16, W), BF)}


def forward(piece, k, patches, me, bufs, w1, w2, mixes, biases, vectors, b1):
    L, D, F = w1.shape
    W = piece.work
    vmem = pl.BlockSpec(memory_space=pltpu.VMEM)
    smem = pl.BlockSpec(memory_space=pltpu.SMEM)
    hbm = pl.BlockSpec(memory_space=pl.ANY)
    args = [me, *bufs, w1, w2, *[mixes[g] for g in piece.groups], *[biases[g] for g in piece.groups], *vectors, b1]
    specs = [smem] + [vmem] * k + [hbm] * 2 + [vmem] * (2 * len(piece.groups) + len(vectors) + 1)
    c = bufs[0].shape[0]
    kept = [shape for l in range(L) for shape in kept_shapes(l, D, F, W).values()]
    scratch = [pltpu.VMEM(*v) for l in range(L) for v in with_ones(kept_shapes(l, D, F, W), D, W).values()]
    scratch += [
        pltpu.VMEM((D, W), F32),
        pltpu.VMEM((L, D + 16, F), BF),
        pltpu.VMEM((L, F, D), BF),
        pltpu.VMEM((128, D), F32),
        pltpu.VMEM((L, D, 128), F32),
        pltpu.SemaphoreType.DMA((L * (7 + 2 * (F // FFC)),)),
    ]
    out = pl.pallas_call(
        functools.partial(forward_kernel, piece, k, patches, L),
        out_shape=[jax.ShapeDtypeStruct((c, piece.width), BF)] * k + [jax.ShapeDtypeStruct(*v) for v in kept],
        in_specs=specs,
        out_specs=[vmem] * k + [hbm] * len(kept),
        scratch_shapes=scratch,
        compiler_params=pltpu.CompilerParams(vmem_limit_bytes=VMEM_LIMIT),
        name="forward",
    )(*args)
    n = len(KEPT)
    return out[:k], out[k:]


def backward_kernel(piece, k, patches, rows, layers, first, final, *refs):
    refs = list(refs)

    def take(n):
        out, refs[:] = refs[:n], refs[n:]
        return out

    (me_ref,) = take(1)
    ins = take(k)
    kept_h = [dict(zip(KEPT, take(len(KEPT)))) for _ in range(layers)]
    w1_h, w2_h = take(2)
    mix = dict(zip(piece.groups, take(len(piece.groups))))
    vectors = take(7)
    accs_h = [] if first else take(layers)
    outs = take(k)
    sums_h = [take(2 if final else 1) for _ in range(layers)]
    kept = [dict(zip(KEPT, take(len(KEPT)))) for _ in range(layers)]
    gn, gb, gs, dy, w1s, w2s, accs, stages, gb1, gcol, gpb, line, cols, sem = refs
    D, W = gn.shape
    F = w2s.shape[1]
    c = D // k
    me = me_ref[0]
    core = lax.rem(me_ref[1], 2)
    copies = Copies(sem)
    half_f = F // 2
    for l in reversed(range(layers)):
        copies.start((l, "w2"), w2_h.at[l], w2s.at[l])
        for i in range(2):
            at = pl.ds(i * half_f, half_f)
            copies.start((l, "dact", i), kept_h[l]["dact"].at[at], kept[l]["dact"].at[at])
        copies.start((l, "w1"), w1_h.at[l], w1s.at[l])
        copies.start((l, "sc"), kept_h[l]["sc"], kept[l]["sc"].at[pl.ds(0, D)])
        if not first:
            copies.start((l, "acc"), accs_h[l], accs.at[l])
        for name in ("act", "brs", "mixs", "state", "nrm"):
            copies.start((l, name), kept_h[l][name], kept[l][name])

    load_columns(vectors, line, cols, layers)
    for s in range(k):
        at = pl.ds(pl.multiple_of(lax.rem(me - s + k, k) * c, 16), c)
        dy[at, : piece.width] = ins[s][...].astype(F32)
    if W > piece.width:
        dy[:, piece.width :] = jnp.zeros((D, W - piece.width), F32)
    if W > piece.total:
        gn[:, piece.total :] = jnp.zeros((D, W - piece.total), F32)
    gcol[...] = jnp.zeros(gcol.shape, F32)

    def put(r, j, v):
        gcol[r, j : j + 1] = jnp.sum(v, 1, keepdims=True)

    for l in reversed(range(layers)):
        a, b, g, f, h, ff, b2 = [channel(cols, l, j) for j in range(7)]
        state, mixs, nrm, sc, brs, act, dact = [kept[l][name] for name in KEPT]
        acc = accs.at[l]
        w1, w2 = w1s.at[l], w2s.at[l]
        sc[D:, :] = jnp.ones((sc.shape[0] - D, W), BF)
        if first:
            acc[rows.misc :, :] = jnp.zeros((rows.total - rows.misc, D), F32)
        gpb[...] = jnp.zeros(gpb.shape, F32)

        def gain(r):
            gbv = (dy[r, :] * ff(r)).astype(BF)
            gb[r, :] = gbv
            put(r, 6, gbv.astype(F32))

        over_rows(D, gain)
        copies.wait((l, "w2"))
        up = gb[...]
        for i in range(F // FFC):
            if i * FFC % half_f == 0:
                copies.wait((l, "dact", i * FFC // half_f))
            fr = pl.ds(i * FFC, FFC)
            dact[fr, :] = (nn(w2[fr, :], up) * dact[fr, :].astype(F32)).astype(BF)
        copies.wait((l, "w1"))
        gs[...] = nn(w1[...], dact[...]).astype(BF)
        copies.wait((l, "sc"))
        if not first:
            copies.wait((l, "acc"))

        def weight_in(n, carry):
            r = nt(sc[...], dact[pl.ds(pl.multiple_of(n * 2 * D, 2 * D), 2 * D), :])
            for i in range(2):
                at = pl.ds(pl.multiple_of((2 * n + i) * D, D), D)
                part = r[:D, i * D : (i + 1) * D]
                acc[at, :] = part if first else acc[at, :] + part
            gb1[:, pl.ds(pl.multiple_of(n * 2 * D, 2 * D), 2 * D)] = r[D : D + 8]
            return carry

        lax.fori_loop(0, F // (2 * D), weight_in, 0)
        copies.wait((l, "act"))

        def weight_out(n, carry):
            r = nt(act[pl.ds(pl.multiple_of(n * 512, 512), 512), :], gb[...])
            at = pl.ds(pl.multiple_of(rows.out + n * 512, 512), 512)
            acc[at, :] = r if first else acc[at, :] + r
            return carry

        lax.fori_loop(0, F // 512, weight_out, 0)
        copies.wait((l, "brs"), (l, "mixs"), (l, "state"))

        def back(r):
            gsf = gs[r, :].astype(F32)
            mixture = mixs[r, :]
            middle = state[r, :].astype(F32) + g(r) * mixture
            d = dy[r, :]
            put(r, 5, d * brs[r, :].astype(F32))
            gm = d + f(r) * gsf
            dy[r, :] = gm
            put(r, 3, gsf * middle)
            put(r, 4, gsf)
            put(r, 2, gm * mixture)
            gmb = (g(r) * gm).astype(BF)
            gb[r, :] = gmb
            gpb[...] = gpb[...] + gmb.astype(F32).reshape(ROWS // 8, 8, W).sum(0)

        over_rows(D, back)
        pbias = jnp.sum(gpb[...], 0, keepdims=True)
        copies.wait((l, "nrm"))
        side = rows.side
        for group, _, o in piece.members:
            p = patches[group]
            gi = gb[:, o : o + p]
            product = tn(gi, nrm[:, o : o + p])
            for r0, nr, c0, nc, at, lane in rows.mix[group]:
                part = product[r0 : r0 + nr, c0 : c0 + nc]
                acc[at : at + nr, lane : lane + nc] = acc[at : at + nr, lane : lane + nc] + part
            gn[:, o : o + p] = nn(gi, mix[group][l])
            for c0, nc, at in rows.vector(PATCH + group, p):
                part = pbias[:, o + c0 : o + c0 + nc]
                acc[at : at + 1, side : side + nc] = acc[at : at + 1, side : side + nc] + part

        def pass_down(r):
            n = gn[r, :]
            put(r, 0, n * state[r, :].astype(F32))
            put(r, 1, n)
            dy[r, :] = dy[r, :] + a(r) * n

        over_rows(D, pass_down)
        sums = jnp.transpose(gcol[...])[:8]
        for c0, nc, at in rows.vector(0, D):
            acc[at : at + 8, side : side + nc] = acc[at : at + 8, side : side + nc] + sums[:, c0 : c0 + nc]
        for t in range(F // D):
            for c0, nc, at in rows.vector(BIAS_IN + t, D):
                part = gb1[0:1, t * D + c0 : t * D + c0 + nc]
                acc[at : at + 1, side : side + nc] = acc[at : at + 1, side : side + nc] + part
        if final:
            half = rows.total // 2
            stages[l] = acc[pl.ds(pl.multiple_of((1 - core) * half, 16), half), :].astype(BF)
            copies.start((l, "send"), stages.at[l], sums_h[l][0])
            copies.start((l, "keep"), acc.at[pl.ds(pl.multiple_of(core * half, 16), half)], sums_h[l][1])
        else:
            copies.start((l, "sums"), acc, sums_h[l][0])

    for s in range(k):
        at = pl.ds(pl.multiple_of(lax.rem(me + s, k) * c, 16), c)
        outs[s][...] = dy[at, : piece.width].astype(BF)
    copies.wait_all()


def backward(piece, k, patches, rows, me, incoming, kept, w1, w2, mixes, vectors, accs, final):
    L, D, F = w1.shape
    W = piece.work
    first = accs is None
    vmem = pl.BlockSpec(memory_space=pltpu.VMEM)
    smem = pl.BlockSpec(memory_space=pltpu.SMEM)
    hbm = pl.BlockSpec(memory_space=pl.ANY)
    args = [me, *incoming, *kept, w1, w2, *[mixes[g] for g in piece.groups], *vectors]
    specs = [smem] + [vmem] * k + [hbm] * (len(kept) + 2) + [vmem] * (len(piece.groups) + len(vectors))
    if not first:
        args += accs
        specs += [hbm] * L
    out_shape = [jax.ShapeDtypeStruct((D // k, piece.width), BF)] * k
    half = rows.total // 2
    if final:
        out_shape += [jax.ShapeDtypeStruct((half, D), BF), jax.ShapeDtypeStruct((half, D), F32)] * L
    else:
        out_shape += [jax.ShapeDtypeStruct((rows.total, D), F32)] * L
    scratch = [pltpu.VMEM(*v) for l in range(L) for v in with_ones(kept_shapes(l, D, F, W), D, W).values()]
    scratch += [
        pltpu.VMEM((D, W), F32),
        pltpu.VMEM((D, W), BF),
        pltpu.VMEM((D, W), BF),
        pltpu.VMEM((D, W), F32),
        pltpu.VMEM((L, D, F), BF),
        pltpu.VMEM((L, F, D), BF),
        pltpu.VMEM((L, rows.total, D), F32),
        pltpu.VMEM((L, half, D) if final else (8, 128), BF),
        pltpu.VMEM((8, F), F32),
        pltpu.VMEM((D, 128), F32),
        pltpu.VMEM((8, W), F32),
        pltpu.VMEM((128, D), F32),
        pltpu.VMEM((L, D, 128), F32),
        pltpu.SemaphoreType.DMA((13 * L,)),
    ]
    out = pl.pallas_call(
        functools.partial(backward_kernel, piece, k, patches, rows, L, first, final),
        out_shape=out_shape,
        in_specs=specs,
        out_specs=[vmem] * k + [hbm] * (len(out_shape) - k),
        scratch_shapes=scratch,
        compiler_params=pltpu.CompilerParams(vmem_limit_bytes=VMEM_LIMIT),
        name="backward",
    )(*args)
    sums = out[k:]
    n = 2 if final else 1
    return out[:k], [sums[l * n : (l + 1) * n] for l in range(L)]


def after(value, *events):
    return lax.optimization_barrier((value, events))[0]


def flip(v, bit, n):
    return lax.ppermute(v, "dp", [(i, i ^ bit) for i in range(n)])


def cycle(v, s, k):
    return lax.ppermute(v, "swap", [(i, (i + s) % k) for i in range(k)])


def spread(bufs, distances=None):
    return [cycle(bufs[s], s, len(bufs)) if s else bufs[0] for s in distances or range(len(bufs))]


def local(body, pos, ins, shapes, name):
    vmem = pl.BlockSpec(memory_space=pltpu.VMEM)
    return pl.pallas_call(
        body,
        out_shape=[jax.ShapeDtypeStruct(*shape) for shape in shapes],
        in_specs=[pl.BlockSpec(memory_space=pltpu.SMEM)] + [vmem] * len(ins),
        out_specs=[vmem] * len(shapes),
        compiler_params=pltpu.CompilerParams(vmem_limit_bytes=40 << 20),
        name=name,
    )(pos, *ins)


def side(pos_ref, bit):
    return lax.rem(lax.div(pos_ref[1], bit), 2)


def split_first(pos, keep, came, bits):
    n, r, d = keep.shape
    q = n // 4

    def body(pos_ref, keep_ref, came_ref, *outs):
        for h in range(2):
            mine = side(pos_ref, bits[h])
            at = pl.ds(2 * q * h + mine * q, q)
            outs[2 * h][...] = keep_ref[at] + came_ref[at].astype(F32)
            at = pl.ds(2 * q * h + (1 - mine) * q, q)
            outs[2 * h + 1][...] = (keep_ref[at] + came_ref[at].astype(F32)).astype(BF)

    out = local(body, pos, [keep, came], [((q, r, d), F32), ((q, r, d), BF)] * 2, "split")
    return [(out[0], out[1]), (out[2], out[3])]


def split_next(pos, keeps, cames, bits):
    n, r, d = keeps[0].shape
    q = n // 2

    def body(pos_ref, k0, k1, c0, c1, *outs):
        for h, (keep_ref, came_ref) in enumerate(((k0, c0), (k1, c1))):
            mine = side(pos_ref, bits[h])
            at = pl.ds(mine * q, q)
            outs[2 * h][...] = keep_ref[at] + came_ref[at].astype(F32)
            at = pl.ds((1 - mine) * q, q)
            outs[2 * h + 1][...] = (keep_ref[at] + came_ref[at].astype(F32)).astype(BF)

    out = local(body, pos, [*keeps, *cames], [((q, r, d), F32), ((q, r, d), BF)] * 2, "split")
    return [(out[0], out[1]), (out[2], out[3])]


def split_swap(pos, keeps, cames, k):
    n, r, d = keeps[0].shape

    def body(pos_ref, k0, k1, c0, c1, *refs):
        outs, both = refs[:k], refs[k]
        both[:n] = k0[...] + c0[...].astype(F32)
        both[n:] = k1[...] + c1[...].astype(F32)
        me = pos_ref[0]
        outs[0][...] = both[me]
        for s in range(1, k):
            outs[s][...] = both[lax.rem(me + s, k)].astype(BF)

    vmem = pl.BlockSpec(memory_space=pltpu.VMEM)
    return pl.pallas_call(
        body,
        out_shape=[jax.ShapeDtypeStruct((r, d), F32)] + [jax.ShapeDtypeStruct((r, d), BF)] * (k - 1),
        in_specs=[pl.BlockSpec(memory_space=pltpu.SMEM)] + [vmem] * 4,
        out_specs=[vmem] * k,
        scratch_shapes=[pltpu.VMEM((2 * n, r, d), F32)],
        name="split_swap",
    )(pos, *keeps, *cames)


def add_swap(pos, keep, cames):
    def body(pos_ref, keep_ref, *refs):
        total = keep_ref[...]
        for came in refs[:-1]:
            total = total + came[...].astype(F32)
        refs[-1][...] = total.astype(BF)

    return local(body, pos, [keep, *cames], [(keep.shape, BF)], "add_swap")[0]


def join_swap(pos, parts, k):
    r, d = parts[0].shape
    n = k // 2

    def body(pos_ref, *refs):
        ins, (o0, o1), both = refs[:k], refs[k : k + 2], refs[k + 2]
        for s in range(k):
            both[lax.rem(pos_ref[0] - s + k, k)] = ins[s][...]
        o0[...] = both[:n]
        o1[...] = both[n:]

    vmem = pl.BlockSpec(memory_space=pltpu.VMEM)
    return pl.pallas_call(
        body,
        out_shape=[jax.ShapeDtypeStruct((n, r, d), BF)] * 2,
        in_specs=[pl.BlockSpec(memory_space=pltpu.SMEM)] + [vmem] * k,
        out_specs=[vmem] * 2,
        scratch_shapes=[pltpu.VMEM((k, r, d), BF)],
        name="join_swap",
    )(pos, *parts)


def join(pos, owns, cames, bits, whole):
    q, r, d = owns[0].shape

    def body(pos_ref, v0, v1, c0, c1, *outs):
        for h, (own, came) in enumerate(((v0, c0), (v1, c1))):
            mine = side(pos_ref, bits[h])
            out, base = (outs[0], 2 * q * h) if whole else (outs[h], 0)
            out[pl.ds(base + mine * q, q)] = own[...]
            out[pl.ds(base + (1 - mine) * q, q)] = came[...]

    shapes = [((4 * q, r, d), BF)] if whole else [((2 * q, r, d), BF)] * 2
    return local(body, pos, [*owns, *cames], shapes, "join")


def finish(pos, rows, ff, layer, layers, patches, mine, other, before):
    r, d = rows.total, mine.shape[-1]
    half = r // 2
    nm = rows.used - rows.misc
    last = layer == 0
    big = [(layers, d, ff), (layers, ff, d)]
    small = [(layers, d)] * 7 + [(layers, ff)] + [(layers, p) for p in patches] + [(p, layers, p) for p in patches]
    kept = before[:2]
    miscs = before[2:]

    def body(pos_ref, a_ref, b_ref, *refs):
        refs = refs[len(kept) :]
        misc_refs, refs = refs[: len(miscs)], refs[len(miscs) :]
        outs, rest, (full, sem) = refs[:2], refs[2:-2], refs[-2:]
        core = lax.rem(pos_ref[1], 2)
        full[pl.ds(pl.multiple_of(core * half, 16), half), :] = a_ref[...].astype(F32)
        full[pl.ds(pl.multiple_of((1 - core) * half, 16), half), :] = b_ref[...].astype(F32)
        copies = [pltpu.make_async_copy(full.at[pl.ds(rows.out, ff)], outs[1].at[layer], sem.at[0])]
        for t in range(ff // d):
            block = outs[0].at[layer, :, pl.ds(t * d, d)]
            copies.append(pltpu.make_async_copy(full.at[pl.ds(t * d, d)], block, sem.at[1 + t]))
        for cp in copies:
            cp.start()
        if last:
            sources = [(layers - 1 - i, ref, 0) for i, ref in enumerate(misc_refs)] + [(0, full, rows.misc)]
            for l, ref, base in sources:
                base -= rows.misc
                side = rows.side
                vectors = [(rest[j], 0, j, d) for j in range(7)]
                vectors += [(rest[7], t * d, BIAS_IN + t, d) for t in range(ff // d)]
                vectors += [(rest[8 + g], 0, PATCH + g, p) for g, p in enumerate(patches)]
                for out, start, index, length in vectors:
                    for c0, nc, at in rows.vector(index, length):
                        out[l : l + 1, start + c0 : start + c0 + nc] = ref[base + at : base + at + 1, side : side + nc]
                for g in range(len(patches)):
                    parts = [
                        (r0, ref[base + at : base + at + nr, lane : lane + nc])
                        for r0, nr, _, nc, at, lane in rows.mix[g]
                    ]
                    whole = parts[0][1]
                    if len(parts) > 1:
                        low = jnp.concatenate([part for _, part in parts[1:]], 1)
                        whole = jnp.concatenate([whole, low], 0)
                    rest[11 + g][:, l, :] = whole
        else:
            rest[0][...] = full[rows.misc : rows.used, :]
        for cp in copies:
            cp.wait()

    vmem = pl.BlockSpec(memory_space=pltpu.VMEM)
    hbm = pl.BlockSpec(memory_space=pl.ANY)
    shapes = big + (small if last else [(nm, d)])
    out = pl.pallas_call(
        body,
        out_shape=[jax.ShapeDtypeStruct(shape, F32) for shape in shapes],
        in_specs=[pl.BlockSpec(memory_space=pltpu.SMEM), vmem, vmem] + [hbm] * len(kept) + [vmem] * len(miscs),
        out_specs=[hbm] * 2 + [vmem] * (len(shapes) - 2),
        scratch_shapes=[pltpu.VMEM((r, d), F32), pltpu.SemaphoreType.DMA((1 + ff // d,))],
        input_output_aliases={3 + i: i for i in range(len(kept))},
        compiler_params=pltpu.CompilerParams(vmem_limit_bytes=40 << 20),
        name="finish",
    )(pos, mine, other, *kept, *miscs)
    return out if last else [*out[:2], *miscs, out[2]]


def orders(n):
    bits = [1 << i for i in range(1, n.bit_length() - 1)]
    return list(zip(bits, bits[::-1]))


class Chain:
    def __init__(self, pos, rows, n, k):
        self.pos, self.rows, self.n, self.k = pos, rows, n, k
        self.steps = orders(n)

    def begin(self, send, keep):
        view = (self.rows.blocks // 2, self.rows.block, send.shape[-1])
        self.keep, self.came = keep.reshape(view), flip(send, 1, self.n).reshape(view)

    def ready(self, *events):
        self.came = after(self.came, events)

    def split(self, t):
        if t == 0:
            halves = split_first(self.pos, self.keep, self.came, self.steps[0])
        else:
            halves = split_next(self.pos, self.keep, self.came, self.steps[t])
        self.keep = [h[0] for h in halves]
        self.came = [flip(h[1], bit, self.n) for h, bit in zip(halves, self.steps[t])]
        return halves

    def split_swap(self):
        parts = split_swap(self.pos, self.keep, self.came, self.k)
        self.keep, self.came = parts[0], [cycle(parts[s], s, self.k) for s in range(1, self.k)]
        return parts

    def add_swap(self):
        self.keep = add_swap(self.pos, self.keep, self.came)
        self.came = [cycle(self.keep, s, self.k) for s in range(1, self.k)]
        return self.keep

    def join_swap(self):
        self.keep = join_swap(self.pos, [self.keep, *self.came], self.k)
        self.came = [flip(v, bit, self.n) for v, bit in zip(self.keep, self.steps[-1])]
        return self.keep

    def join(self, t):
        self.keep = join(self.pos, self.keep, self.came, self.steps[t], t == 0)
        if t > 0:
            self.came = [flip(v, bit, self.n) for v, bit in zip(self.keep, self.steps[t - 1])]
        else:
            self.keep = self.keep[0].reshape(-1, self.keep[0].shape[-1])
            self.came = flip(self.keep, 1, self.n)
        return self.keep


def on_device(
    n_dp,
    k,
    source_tiles_smallest,
    source_tiles_moderate,
    source_tiles_largest,
    target_cotangent_smallest,
    target_cotangent_moderate,
    target_cotangent_largest,
    surviving_tallies,
    token_affine_factor,
    token_affine_addend,
    crosstile_matrix_smallest,
    crosstile_matrix_moderate,
    crosstile_matrix_largest,
    crosstile_addend_smallest,
    crosstile_addend_moderate,
    crosstile_addend_largest,
    token_blend_factor,
    feedforward_affine_factor,
    feedforward_affine_addend,
    widening_matrix,
    widening_addend,
    narrowing_matrix,
    narrowing_addend,
    feedforward_factor,
):
    L, D, F = widening_matrix.shape
    tensors = [source_tiles_smallest, source_tiles_moderate, source_tiles_largest]
    cotans = [target_cotangent_smallest, target_cotangent_moderate, target_cotangent_largest]
    mixes = [crosstile_matrix_smallest, crosstile_matrix_moderate, crosstile_matrix_largest]
    biases = [crosstile_addend_smallest, crosstile_addend_moderate, crosstile_addend_largest]
    patches = [t.shape[0] for t in tensors]
    images = [t.shape[1] for t in tensors]
    own = [count // k for count in images]
    idx = lax.axis_index("dp")
    pos = lax.axis_index("swap")
    me = jnp.stack([pos, idx]).astype(jnp.int32)
    live = surviving_tallies[0]

    pieces = [
        Piece([(2, i) for i in range(own[2])] + [(0, i) for i in range(1, own[0])], patches),
        Piece([(1, i) for i in range(own[1])] + [(0, 0)], patches),
    ]
    rows = Rows(F, D, patches, n_dp * k)

    tensors = [jnp.transpose(t, (1, 2, 0)) for t in tensors]
    cotans = [jnp.transpose(t, (1, 2, 0)) for t in cotans]
    vectors = [
        token_affine_factor,
        token_affine_addend,
        token_blend_factor,
        feedforward_affine_factor,
        feedforward_affine_addend,
        feedforward_factor,
        narrowing_addend,
    ]
    w1, w2 = widening_matrix, narrowing_matrix

    first, second = pieces
    mixes = [with_layout_constraint(m, Layout((0, 1, 2))) for m in mixes]
    x_bufs = [pack(piece, k, patches, me, live, tensors, False) for piece in pieces]
    c_bufs = [pack(piece, k, patches, me, live, cotans, True) for piece in pieces]
    far = [k // 2]
    near = [s for s in range(1, k) if s != k // 2]

    x_first = after(spread(x_bufs[0]), (mixes, x_bufs[1], c_bufs))
    x_second = spread(after(x_bufs[1], x_first))
    out_first, kept_first = forward(first, k, patches, me, x_first, w1, w2, mixes, biases, vectors, widening_addend)
    x_second = after(x_second, out_first)
    c_first = spread(after(c_bufs[0], x_second))
    out_second, kept_second = forward(second, k, patches, me, x_second, w1, w2, mixes, biases, vectors, widening_addend)
    c_first = after(c_first, out_second)
    c_second = spread(after(c_bufs[1], c_first))
    came = {0: out_first[0]}
    came.update(zip(near, spread(after(out_first, c_first), near)))
    grad_first, sums = backward(first, k, patches, rows, me, c_first, kept_first, w1, w2, mixes, vectors, None, False)
    accs = [v[0] for v in sums]
    c_second, came = after((c_second, came), grad_first)
    came.update(zip(far, spread(after(out_first, c_second), far)))
    out_first = [came[s] for s in range(k)]
    out_second = spread(after(out_second, c_second))
    grad_second, halves = backward(second, k, patches, rows, me, c_second, kept_second, w1, w2, mixes, vectors, accs, True)
    out_first, out_second = after((out_first, out_second), grad_second)

    halves, grad_first = after((halves, grad_first), (out_first, out_second))
    came = {0: grad_first[0]}
    came.update(zip(near + far, spread(grad_first, near + far)))
    grad_first = [came[s] for s in range(k)]
    order = list(reversed(range(L)))
    chains = [Chain(me, rows, n_dp, k) for _ in order]
    for chain, l in zip(chains, order):
        chain.begin(*halves[l])
    token = ()

    def turn(step, *events):
        nonlocal token
        for i, chain in enumerate(chains):
            then = events[i] if i < len(events) else ()
            chain.ready(token, then() if callable(then) else then)
            token = step(chain)

    outs = [None] * 6
    alone = [g for g in range(3) if g not in second.groups]

    def arrange(base, used, groups, bufs, masked):
        chosen = [pieces[i] for i in used]
        got = unpack(chosen, groups, k, patches, images, me, live, [bufs[i] for i in used], masked)
        for i, g in enumerate(groups):
            outs[base + g] = got[i]
        return got

    count = len(orders(n_dp))
    for t in range(count):
        turn(lambda chain: chain.split(t), [came[s] for s in near] if t == 1 else ())
    turn(lambda chain: chain.split_swap(), grad_first)
    turn(lambda chain: chain.add_swap(), (), lambda: arrange(0, (0,), alone, (after(out_first, token),), True))
    turn(
        lambda chain: chain.join_swap(),
        (),
        lambda: (
            arrange(0, (0, 1), second.groups, (after(out_first, token), out_second), True),
            arrange(3, (0,), alone, (after(grad_first, token),), False),
            chains[0].came,
        ),
    )
    came = {0: grad_second[0]}
    came.update(zip(near + far, spread(after(grad_second, token), near + far)))
    grad_second = [came[s] for s in range(k)]
    for t in reversed(range(count)):
        late = [came[s] for s in (near if t == count - 1 else far if t == 0 else [])]
        turn(lambda chain: chain.join(t), (), late)
    token = arrange(3, (0, 1), second.groups, (grad_first, after(grad_second, token)), False)
    sums = []
    for chain, l in zip(chains, order):
        chain.ready(token, sums)
        sums = finish(me, rows, F, l, L, patches, chain.keep, chain.came, sums)
    outs = [jnp.transpose(v, (2, 0, 1)) for v in outs]
    grad_in, grad_out, *small = sums
    vec, bias_in, patch_bias, mix_of = small[:7], small[7], small[8:11], small[11:]
    mix_of = [jnp.transpose(v, (1, 0, 2)) for v in mix_of]

    return (
        *outs,
        vec[0],
        vec[1],
        *mix_of,
        *patch_bias,
        vec[2],
        vec[3],
        vec[4],
        grad_in,
        bias_in,
        grad_out,
        vec[6],
        vec[5],
    )


def solution(mesh):
    tokens = P(None, "dp", "swap")
    in_specs = (tokens,) * 6 + (P("dp", None),) + (P(),) * 16
    out_specs = (tokens,) * 6 + (P(),) * 16
    return jax.shard_map(
        functools.partial(on_device, mesh.shape["dp"], mesh.shape["swap"]),
        mesh=mesh,
        in_specs=in_specs,
        out_specs=out_specs,
        check_vma=False,
    )
```
